32 devices in a mesh: dp: 8 (over y, x, core), expert: 4 (over z).
Axes of the slice: x: 2, y: 2, z: 4, core: 2. Of those that a mesh axis runs over, the one named last changes fastest.
Arguments:
- tokens: bfloat16 [4096, 2048], P(('dp', 'expert')), may hold values from -6 to 6
- expert_ids: int32 [4096, 2], P(('dp', 'expert')), may hold values from 0 to 3, all different within a row; in each aligned block of 128 rows (0 to 127, 128 to 255, ...) at most 64 rows name the same one
- gate_probs: float32 [4096, 2], P(('dp', 'expert')), may hold values from 0.25 to 1
- w_gate: bfloat16 [4, 2048, 768], P('expert'), may hold values from -0.125 to 0.125
- w_up: bfloat16 [4, 2048, 768], P('expert'), may hold values from -0.125 to 0.125
- w_down: bfloat16 [4, 768, 2048], P('expert'), may hold values from -0.21875 to 0.21875
- out_grad: bfloat16 [4096, 2048], P(('dp', 'expert')), may hold values from -6 to 6
Outputs:
- layer_out: bfloat16 [4096, 2048], P(('dp', 'expert'))
- prob_grad: float32 [4096, 2], P(('dp', 'expert'))
- token_grad: bfloat16 [4096, 2048], P(('dp', 'expert'))
- grad_gate: bfloat16 [4, 2048, 768], P('expert', 'dp')
- grad_up: bfloat16 [4, 2048, 768], P('expert', 'dp')
- grad_down: bfloat16 [4, 768, 2048], P('expert', 'dp')
The draws below stay inside these ranges and needn't reach their ends.
Inputs may be any that keep to these rules, and one draw needn't show every extreme that they name: `expert_ids`: the 2 experts of one token differ. Among the 128 tokens of one device (aligned blocks of rows), no expert is chosen by more than 64 tokens, and in every draw some expert is chosen by exactly 64 of some device's tokens.
All inputs are finite; a program needn't handle non-finite values.
Results may differ from the reference program's by a relative error of at most 0.015.
Values may be sent and summed in bfloat16 or wider, within the bound.
No kernel may reach another device: no remote copies, remote signals or barrier semaphores. Data moves between devices by JAX's collectives and lax.ppermute only.
A program may use at most 128 MiB of HBM per device.

```python
import math
import jax
import jax.numpy as jnp
import numpy as np
from jax import lax

D = 2048
FF = 768
TOP = 2
TOK_DEV = 128
CAP = 64
EXPERTS = 4
TOKENS = 4096


def with_spikes(entries, key, source, target, shards_of, factor):
    def block_of(axis_at):
        return (jnp.arange(entries.shape[axis_at]) // (entries.shape[axis_at] // shards_of)).reshape((-1,) + (1,) * (entries.ndim - 1 - axis_at))

    one_side = jax.random.permutation(key, shards_of)[block_of(target)]
    far = (block_of(target) + shards_of // 2) % shards_of
    return jnp.where((block_of(source) == one_side) | (block_of(source) == far), factor * entries, entries)


def steps_of(own_key, extent, split, low, largest):
    gain, own = 1.0, jax.random.fold_in(own_key, 6)
    for position, parts in split:
        heights = jnp.exp(jax.random.uniform(jax.random.fold_in(own, position), (parts,), jnp.float32, low / len(split), largest / len(split)))
        gain = gain * jnp.repeat(heights, extent[position] // parts).reshape([-1 if axis == position else 1 for axis in range(len(extent))])
    return gain


def shared_out(stream_key, own, number, rows, number_of, top, bound, skew):
    order = jax.random.permutation(stream_key, number_of)
    heavy_load, common = shares(number_of, rows * top, bound, skew, True), shares(number_of, rows * top, bound, skew, False)
    places = jnp.arange(number_of)

    def named(sizes, turn):
        used = int((sizes > 0).sum())
        fixed = max(1, used // 4)
        moved = fixed + (places - fixed + turn * (used - fixed)) % max(1, number_of - fixed)
        return jnp.zeros((number_of,), jnp.int32).at[order[jnp.where(places < fixed, places, moved)]].set(jnp.asarray(sizes, jnp.int32))

    sizes = jnp.where(number % 4 == 0, named(heavy_load, number // 4), named(common, number - number // 4 - 1))
    mixed = jax.random.permutation(jax.random.fold_in(own, 3), number_of)
    source_of, taker = mixed[0:number_of // 2 * 2:2], mixed[1:number_of // 2 * 2:2]
    margin = jnp.minimum(sizes[source_of] - 1, bound - sizes[taker]) // 2
    margin = jnp.where((source_of == order[0]) | (taker == order[0]) | (sizes[taker] == 0), 0, jnp.maximum(margin, 0))
    moved = jax.random.randint(jax.random.fold_in(own, 4), (number_of // 2,), 0, 1 << 20) % (margin + 1)
    sizes = sizes.at[source_of].add(-moved).at[taker].add(moved)
    items = jnp.searchsorted(jnp.cumsum(sizes), jnp.arange(rows * top), side="right").astype(jnp.int32)
    listing = items.reshape(top, rows).T
    listing = listing[jax.random.permutation(jax.random.fold_in(own, 1), rows)]
    turn = jax.random.randint(jax.random.fold_in(own, 2), (rows, 1), 0, top)
    return jnp.take_along_axis(listing, (jnp.arange(top)[None, :] + turn) % top, axis=1)


def shares(amount, total, bound, slope, full):
    weights = [(1 << 20) // math.isqrt(rank ** slope) + 1 for rank in range(1, amount + 1)]
    largest = bound if full else min(bound, max(-(-total // amount), total * weights[0] // sum(weights)))
    least = 1 if total - largest >= amount - 1 else 0
    counts, surplus = [largest] + [least] * (amount - 1), total - largest - least * (amount - 1)
    while surplus > 0:
        movable = [i for i in range(1, amount) if counts[i] < largest] or [i for i in range(1, amount) if counts[i] < bound]
        whole, budget = sum([weights[i] for i in movable]), surplus
        for i in movable:
            extra = min(bound - counts[i], max(1, budget * weights[i] // whole), surplus)
            counts[i] = counts[i] + extra
            surplus = surplus - extra
    return np.array(counts)


def bell_draw(own_key, dims, deviation, limit, shards=(), kind=jnp.bfloat16):
    result = deviation * jax.random.normal(own_key, dims, jnp.float32)
    if shards:
        result = result * steps_of(own_key, dims, shards, -0.22, 0.18)
    return jnp.clip(result, -limit, limit).astype(kind)


def gaussian_with(stream_key, dims, spread, bound, shards, heavy, kind=jnp.bfloat16):
    entries = spread * jax.random.normal(stream_key, dims, jnp.float32)
    if shards:
        entries = entries * steps_of(stream_key, dims, shards, -0.22, 0.18)
    return jnp.clip(with_spikes(entries, jax.random.fold_in(stream_key, 3), *heavy), -bound, bound).astype(kind)


def setup_inputs(seed: int = 0) -> dict:
    keys = jax.random.split(jax.random.key(seed), 8)
    tokens = gaussian_with(keys[0], (TOKENS, D), 1.0, 6.0, ((0, 32),), (0, 1, 32, 2.75))
    expert_ids_keys = jax.random.split(jax.random.fold_in(keys[1], 1), TOKENS // TOK_DEV)
    expert_ids_turns = jax.random.permutation(jax.random.fold_in(keys[1], 3), TOKENS // TOK_DEV)
    expert_ids = jax.vmap(lambda own, number: shared_out(jax.random.fold_in(keys[1], 2), own, number, TOK_DEV, EXPERTS, TOP, CAP, 2))(expert_ids_keys, expert_ids_turns).reshape((TOKENS, TOP))
    gate_probs = jnp.clip(0.25 + 0.75 * jax.random.uniform(keys[2], (TOKENS, TOP), jnp.float32) ** steps_of(keys[2], (TOKENS, TOP), ((0, 32),), -0.2, 0.2), 0.25, 1.0)
    w_gate = bell_draw(keys[3], (EXPERTS, D, FF), D ** -0.5, 0.125, ((0, 4),))
    w_up = bell_draw(keys[4], (EXPERTS, D, FF), D ** -0.5, 0.125, ((0, 4),))
    w_down = bell_draw(keys[5], (EXPERTS, FF, D), FF ** -0.5, 0.21875, ((0, 4),))
    out_grad = bell_draw(keys[6], (TOKENS, D), 1.0, 6.0, ((0, 32),))
    return {"tokens": tokens, "expert_ids": expert_ids, "gate_probs": gate_probs, "w_gate": w_gate, "w_up": w_up, "w_down": w_down, "out_grad": out_grad}


def silu_parts(gate_val):
    sig_val = jax.nn.sigmoid(gate_val)
    return gate_val * sig_val, sig_val * (1.0 + gate_val * (1.0 - sig_val))


def reference(tokens, expert_ids, gate_probs, w_gate, w_up, w_down, out_grad):
    tok_count, model_width = tokens.shape
    top_count = expert_ids.shape[1]
    expert_count = w_gate.shape[0]
    ff_width = w_gate.shape[2]
    slot_count = tok_count * top_count
    block_len = 512
    flat_ids = expert_ids.reshape(slot_count).astype(jnp.int32)
    expert_ix = jnp.arange(expert_count, dtype=jnp.int32)
    onehot = (flat_ids[:, None] == expert_ix[None, :]).astype(jnp.int32)
    expert_load = jnp.sum(onehot, axis=0).astype(jnp.int32)
    seg_sizes = ((expert_load + block_len - 1) // block_len * block_len).astype(jnp.int32)
    seg_ends = jnp.cumsum(seg_sizes).astype(jnp.int32)
    seg_starts = (seg_ends - seg_sizes).astype(jnp.int32)
    slot_rank = jnp.sum((jnp.cumsum(onehot, axis=0).astype(jnp.int32) - 1) * onehot, axis=1).astype(jnp.int32)
    dest_rows = (jnp.sum(seg_starts[None, :] * onehot, axis=1) + slot_rank).astype(jnp.int32)
    block_total = (slot_count + block_len - 1) // block_len + expert_count
    padded_len = block_total * block_len
    token_of_slot = jnp.arange(slot_count, dtype=jnp.int32) // top_count
    x_rows = jnp.zeros((padded_len, model_width), tokens.dtype).at[dest_rows].set(tokens[token_of_slot])
    scaled_grad = (gate_probs.reshape(slot_count, 1) * out_grad[token_of_slot].astype(jnp.float32)).astype(jnp.bfloat16)
    d_rows = jnp.zeros((padded_len, model_width), jnp.bfloat16).at[dest_rows].set(scaled_grad)
    row_firsts = jnp.arange(block_total, dtype=jnp.int32) * block_len
    block_owner = jnp.minimum(jnp.sum((seg_ends[None, :] <= row_firsts[:, None]).astype(jnp.int32), axis=1), expert_count - 1).astype(jnp.int32)

    def block_step(totals, block_ix):
        sum_gate, sum_up, sum_down = totals
        owner_ix = block_owner[block_ix]
        row_start = block_ix * block_len
        x_block = lax.dynamic_slice_in_dim(x_rows, row_start, block_len, 0)
        d_block = lax.dynamic_slice_in_dim(d_rows, row_start, block_len, 0)
        gate_w = lax.dynamic_index_in_dim(w_gate, owner_ix, 0, keepdims=False)
        up_w = lax.dynamic_index_in_dim(w_up, owner_ix, 0, keepdims=False)
        down_w = lax.dynamic_index_in_dim(w_down, owner_ix, 0, keepdims=False)
        gate_val = jnp.dot(x_block, gate_w, preferred_element_type=jnp.float32)
        up_val = jnp.dot(x_block, up_w, preferred_element_type=jnp.float32)
        act_val, act_slope = silu_parts(gate_val)
        hidden = (act_val * up_val).astype(jnp.bfloat16)
        out_block = jnp.dot(hidden, down_w, preferred_element_type=jnp.float32).astype(jnp.bfloat16)
        hid_grad = jnp.dot(d_block, down_w.T, preferred_element_type=jnp.float32)
        gate_grad = (hid_grad * up_val * act_slope).astype(jnp.bfloat16)
        up_grad = (hid_grad * act_val).astype(jnp.bfloat16)
        in_grad = (jnp.dot(gate_grad, gate_w.T, preferred_element_type=jnp.float32)
                   + jnp.dot(up_grad, up_w.T, preferred_element_type=jnp.float32)).astype(jnp.bfloat16)
        part_gate = jnp.dot(x_block.T, gate_grad, preferred_element_type=jnp.float32)
        part_up = jnp.dot(x_block.T, up_grad, preferred_element_type=jnp.float32)
        part_down = jnp.dot(hidden.T, d_block, preferred_element_type=jnp.float32)
        sum_gate = lax.dynamic_update_index_in_dim(sum_gate, lax.dynamic_index_in_dim(sum_gate, owner_ix, 0, keepdims=False) + part_gate, owner_ix, 0)
        sum_up = lax.dynamic_update_index_in_dim(sum_up, lax.dynamic_index_in_dim(sum_up, owner_ix, 0, keepdims=False) + part_up, owner_ix, 0)
        sum_down = lax.dynamic_update_index_in_dim(sum_down, lax.dynamic_index_in_dim(sum_down, owner_ix, 0, keepdims=False) + part_down, owner_ix, 0)
        return (sum_gate, sum_up, sum_down), (out_block, in_grad)

    start_sums = (jnp.zeros((expert_count, model_width, ff_width), jnp.float32),
                  jnp.zeros((expert_count, model_width, ff_width), jnp.float32),
                  jnp.zeros((expert_count, ff_width, model_width), jnp.float32))
    final_sums, (out_blocks, in_blocks) = lax.scan(block_step, start_sums, jnp.arange(block_total, dtype=jnp.int32))
    out_slots = out_blocks.reshape(padded_len, model_width)[dest_rows].reshape(tok_count, top_count, model_width).astype(jnp.float32)
    in_slots = in_blocks.reshape(padded_len, model_width)[dest_rows].reshape(tok_count, top_count, model_width).astype(jnp.float32)
    layer_out = jnp.sum(gate_probs[:, :, None] * out_slots, axis=1).astype(jnp.bfloat16)
    prob_grad = jnp.sum(out_grad.astype(jnp.float32)[:, None, :] * out_slots, axis=2)
    token_grad = jnp.sum(in_slots, axis=1).astype(jnp.bfloat16)
    return (layer_out, prob_grad, token_grad, final_sums[0].astype(jnp.bfloat16),
            final_sums[1].astype(jnp.bfloat16), final_sums[2].astype(jnp.bfloat16))
```

```python
import functools
import jax
import jax.numpy as jnp
from jax import lax
from jax.experimental import pallas as pl
from jax.experimental.pallas import tpu as pltpu
from jax.sharding import PartitionSpec as P

CAP = 64
BF = jnp.bfloat16
F32 = jnp.float32
MIB = 1 << 20


def mm(left, right):
    return jnp.dot(left, right, preferred_element_type=F32)


def mm_rows(left, right):
    return lax.dot_general(left, right, (((0,), (0,)), ((), ())), preferred_element_type=F32)


def mm_cols(left, right):
    return lax.dot_general(left, right, (((1,), (1,)), ((), ())), preferred_element_type=F32)


def shape_of(shape, dtype=BF):
    return jax.ShapeDtypeStruct(tuple(shape), dtype)


def whole(shape):
    return pl.BlockSpec(tuple(shape), lambda *_: (0,) * len(shape))


def in_smem():
    return pl.BlockSpec(memory_space=pltpu.SMEM)


def params(limit=48):
    return pltpu.CompilerParams(vmem_limit_bytes=limit * MIB)


def cost(flops, moved):
    return pl.CostEstimate(flops=int(flops), bytes_accessed=int(moved), transcendentals=0)


def chosen(ids, expert):
    first = ids[0:1, :] == expert
    second = ids[1:2, :] == expert
    return first, second


def ranks(ids, experts):
    tok_count = ids.shape[1]
    masks = [jnp.where(jnp.logical_or(*chosen(ids, e)), 1.0, 0.0) for e in experts]
    mask = jnp.concatenate(masks + [jnp.zeros((-len(masks) % 16, tok_count), F32)], axis=0)
    before = lax.broadcasted_iota(jnp.int32, (tok_count, tok_count), 0)
    after = lax.broadcasted_iota(jnp.int32, (tok_count, tok_count), 1)
    upper = jnp.where(before < after, 1.0, 0.0).astype(BF)
    return mm(mask.astype(BF), upper).astype(jnp.int32)


def places(rank_row):
    tok_count = rank_row.shape[1]
    return lax.broadcasted_iota(jnp.int32, (CAP, tok_count), 0) == rank_row


def pick_kernel(n, z_ref, ids_ref, prob_ref, tok_ref, grad_ref, *outs):
    ids = ids_ref[...]
    prob = prob_ref[...]
    experts = [lax.rem(z_ref[0] + k, n) for k in range(n)]
    rank = ranks(ids, experts)
    for k in range(n):
        first, second = chosen(ids, experts[k])
        at = places(rank[k : k + 1, :])
        here = jnp.logical_and(at, jnp.logical_or(first, second))
        pick = jnp.where(here, 1.0, 0.0)
        outs[k][...] = mm(pick.astype(BF), tok_ref[...]).astype(BF)
        weight = jnp.where(first, prob[0:1, :], prob[1:2, :])
        scale = jnp.sum(jnp.where(here, weight, 0.0), axis=1, keepdims=True)
        outs[n + k][...] = (scale * mm(pick.astype(BF), grad_ref[...])).astype(BF)


def pick_rows(n, z, ids_t, prob_t, tokens, out_grad):
    tok_count, width = tokens.shape
    return pl.pallas_call(
        functools.partial(pick_kernel, n),
        out_shape=[shape_of((CAP, width))] * (2 * n),
        in_specs=[in_smem(), whole(ids_t.shape), whole(prob_t.shape)] + [whole(tokens.shape)] * 2,
        out_specs=[whole((CAP, width))] * (2 * n),
        grid=(1,),
        compiler_params=params(),
        cost_estimate=cost(4 * n * CAP * tok_count * width, 4 * tok_count * width * 3),
        name="pick_rows",
    )(z, ids_t, prob_t, tokens, out_grad)


def forward_kernel(n, steps, *refs):
    x_refs = refs[:n]
    wg_ref, wu_ref, wd_ref = refs[n : n + 3]
    slope_ref, act_ref, hid_ref = refs[n + 3 : n + 6]
    out_refs = refs[n + 6 : 2 * n + 6]
    rows, total = refs[2 * n + 6 :]
    step = pl.program_id(0)

    @pl.when(step == 0)
    def _():
        for k in range(n):
            rows[k * CAP : (k + 1) * CAP, :] = x_refs[k][...]

    x = rows[...]
    gate = mm(x, wg_ref[0])
    up = mm(x, wu_ref[0])
    sig = jax.nn.sigmoid(gate)
    act = gate * sig
    act_ref[...] = act
    slope_ref[...] = up * (sig * (1.0 + gate * (1.0 - sig)))
    hidden = (act * up).astype(BF)
    hid_ref[...] = hidden
    part = mm(hidden, wd_ref[0])

    @pl.when(step == 0)
    def _():
        total[...] = part

    @pl.when(step > 0)
    def _():
        total[...] += part

    @pl.when(step == steps - 1)
    def _():
        for k in range(n):
            out_refs[k][...] = total[k * CAP : (k + 1) * CAP, :].astype(BF)


def forward(xs, w_gate, w_up, w_down):
    n = len(xs)
    width, ff = w_gate.shape[1:]
    tile = 256
    steps = ff // tile
    rows = n * CAP
    by_col = pl.BlockSpec((1, width, tile), lambda j: (0, 0, j))
    by_row = pl.BlockSpec((1, tile, width), lambda j: (0, j, 0))
    part = pl.BlockSpec((rows, tile), lambda j: (0, j))
    return pl.pallas_call(
        functools.partial(forward_kernel, n, steps),
        grid=(steps,),
        out_shape=[shape_of((rows, ff), F32)] * 2 + [shape_of((rows, ff))] + [shape_of((CAP, width))] * n,
        in_specs=[whole((CAP, width))] * n + [by_col, by_col, by_row],
        out_specs=[part, part, part] + [whole((CAP, width))] * n,
        scratch_shapes=[pltpu.VMEM((rows, width), BF), pltpu.VMEM((rows, width), F32)],
        compiler_params=params(),
        cost_estimate=cost(6 * rows * width * ff, 6 * width * ff + 4 * rows * width + 10 * rows * ff),
        name="forward",
    )(*xs, w_gate, w_up, w_down)


def down_kernel(n, parts, me_ref, *refs):
    g_refs = refs[:n]
    hid_ref, keep_ref, send_ref, rows, total = refs[n:]
    for k in range(n):
        rows[k * CAP : (k + 1) * CAP, :] = g_refs[k][...]
    total[...] = mm_rows(hid_ref[...], rows[...])
    size = keep_ref.shape[1]
    half = parts // 2
    for rel in range(parts):
        owner = me_ref[rel]
        block = total[pl.ds(pl.multiple_of(owner * size, 16), size), :].astype(BF)
        if rel < half:
            keep_ref[rel] = block
        else:
            send_ref[rel - half] = block


def down_part(parts, owners, gs, hidden):
    n = len(gs)
    rows, width = n * CAP, gs[0].shape[1]
    ff = hidden.shape[1]
    size = ff // parts
    tile = 512
    part = pl.BlockSpec((parts // 2, size, tile), lambda j: (0, 0, j))
    return pl.pallas_call(
        functools.partial(down_kernel, n, parts),
        grid=(width // tile,),
        out_shape=[shape_of((parts // 2, size, width))] * 2,
        in_specs=[in_smem()] + [pl.BlockSpec((CAP, tile), lambda j: (0, j))] * n + [whole((rows, ff))],
        out_specs=[part, part],
        scratch_shapes=[pltpu.VMEM((rows, tile), BF), pltpu.VMEM((ff, tile), F32)],
        compiler_params=params(),
        cost_estimate=cost(2 * rows * width * ff, 2 * width * ff + 2 * rows * (width + ff)),
        name="down_part",
    )(owners, *gs, hidden)


def hidden_grad_kernel(n, *refs):
    g_refs = refs[:n]
    wd_ref, slope_ref, act_ref, dgate_ref, dup_ref, rows = refs[n:]

    @pl.when(pl.program_id(0) == 0)
    def _():
        for k in range(n):
            rows[k * CAP : (k + 1) * CAP, :] = g_refs[k][...]

    grad = mm_cols(rows[...], wd_ref[0])
    dgate_ref[...] = (grad * slope_ref[...]).astype(BF)
    dup_ref[...] = (grad * act_ref[...]).astype(BF)


def hidden_grad(gs, w_down, slope, act):
    n = len(gs)
    ff, width = w_down.shape[1:]
    rows = n * CAP
    tile = 256
    part = pl.BlockSpec((rows, tile), lambda j: (0, j))
    return pl.pallas_call(
        functools.partial(hidden_grad_kernel, n),
        grid=(ff // tile,),
        out_shape=[shape_of((rows, ff))] * 2,
        in_specs=[whole((CAP, width))] * n + [pl.BlockSpec((1, tile, width), lambda j: (0, j, 0)), part, part],
        out_specs=[part, part],
        scratch_shapes=[pltpu.VMEM((rows, width), BF)],
        compiler_params=params(),
        cost_estimate=cost(2 * rows * width * ff, 2 * width * ff + 2 * rows * width + 12 * rows * ff),
        name="hidden_grad",
    )(*gs, w_down, slope, act)


def weight_kernel(n, parts, me_ref, *refs):
    x_refs = refs[:n]
    d_ref, keep_ref, send_ref, rows = refs[n:]
    half = parts // 2
    size = keep_ref.shape[1]

    @pl.when(pl.program_id(0) == 0)
    def _():
        for k in range(n):
            rows[k * CAP : (k + 1) * CAP, :] = x_refs[k][...]

    d = d_ref[...]
    for rel in range(parts):
        at = pl.multiple_of(me_ref[rel] * size, size)
        block = mm_rows(rows[:, pl.ds(at, size)], d).astype(BF)
        if rel < half:
            keep_ref[rel] = block
        else:
            send_ref[rel - half] = block


def weight_part(parts, owners, xs, d):
    n = len(xs)
    rows, width = n * CAP, xs[0].shape[1]
    ff = d.shape[1]
    size = width // parts
    tile = 256
    part = pl.BlockSpec((parts // 2, size, tile), lambda j: (0, 0, j))
    return pl.pallas_call(
        functools.partial(weight_kernel, n, parts),
        grid=(ff // tile,),
        out_shape=[shape_of((parts // 2, size, ff))] * 2,
        in_specs=[in_smem()] + [whole((CAP, width))] * n + [pl.BlockSpec((rows, tile), lambda j: (0, j))],
        out_specs=[part, part],
        scratch_shapes=[pltpu.VMEM((rows, width), BF)],
        compiler_params=params(),
        cost_estimate=cost(2 * rows * width * ff, 2 * width * ff + 2 * rows * (width + ff)),
        name="weight_part",
    )(owners, *xs, d)


def input_grad_kernel(n, dgate_ref, dup_ref, wg_ref, wu_ref, *out_refs):
    total = mm_cols(dgate_ref[...], wg_ref[0]) + mm_cols(dup_ref[...], wu_ref[0])
    for k in range(n):
        out_refs[k][...] = total[k * CAP : (k + 1) * CAP, :].astype(BF)


def input_grad(n, dgate, dup, w_gate, w_up):
    rows, ff = dgate.shape
    width = w_gate.shape[1]
    tile = 512
    by_row = pl.BlockSpec((1, tile, ff), lambda j: (0, j, 0))
    return pl.pallas_call(
        functools.partial(input_grad_kernel, n),
        grid=(width // tile,),
        out_shape=[shape_of((CAP, width))] * n,
        in_specs=[whole((rows, ff))] * 2 + [by_row, by_row],
        out_specs=[pl.BlockSpec((CAP, tile), lambda j: (0, j))] * n,
        compiler_params=params(),
        cost_estimate=cost(4 * rows * width * ff, 4 * width * ff + 2 * rows * (width + 2 * ff)),
        name="input_grad",
    )(dgate, dup, w_gate, w_up)


def fold_kernel(keep_ref, recv_ref, a_send, a_keep, b_send, b_keep):
    half = a_send.shape[1]
    total = [keep_ref[i].astype(F32) + recv_ref[i].astype(F32) for i in range(4)]
    for i in range(2):
        a_keep[i] = total[2 * i][:half].astype(BF)
        a_send[i] = total[2 * i + 1][:half].astype(BF)
        b_keep[i] = total[i][half:].astype(BF)
        b_send[i] = total[2 + i][half:].astype(BF)


def fold(keep, recv):
    _, size, width = keep.shape
    tile = 256 if width < 1024 else 512
    full = pl.BlockSpec((4, size, tile), lambda j: (0, 0, j))
    half = pl.BlockSpec((2, size // 2, tile), lambda j: (0, 0, j))
    return pl.pallas_call(
        fold_kernel,
        grid=(width // tile,),
        out_shape=[shape_of((2, size // 2, width))] * 4,
        in_specs=[full, full],
        out_specs=[half] * 4,
        compiler_params=params(),
        cost_estimate=cost(4 * size * width, 24 * size * width),
        name="fold",
    )(keep, recv)


def fold_two_kernel(a_keep, a_recv, b_keep, b_recv, a_next, a_mine, b_next, b_mine):
    for keep, recv, away, mine in ((a_keep, a_recv, a_next, a_mine), (b_keep, b_recv, b_next, b_mine)):
        mine[...] = (keep[0].astype(F32) + recv[0].astype(F32)).astype(BF)
        away[...] = (keep[1].astype(F32) + recv[1].astype(F32)).astype(BF)


def fold_two(a_keep, a_recv, b_keep, b_recv):
    _, half, width = a_keep.shape
    return pl.pallas_call(
        fold_two_kernel,
        grid=(1,),
        out_shape=[shape_of((half, width))] * 4,
        in_specs=[whole((2, half, width))] * 4,
        out_specs=[whole((half, width))] * 4,
        compiler_params=params(),
        cost_estimate=cost(4 * half * width, 24 * half * width),
        name="fold_two",
    )(a_keep, a_recv, b_keep, b_recv)


def fold_last_kernel(a_mine, a_recv, b_mine, b_recv, out_ref):
    half = a_mine.shape[0]
    out_ref[0, :half] = (a_mine[...].astype(F32) + a_recv[...].astype(F32)).astype(BF)
    out_ref[0, half:] = (b_mine[...].astype(F32) + b_recv[...].astype(F32)).astype(BF)


def fold_last(a_mine, a_recv, b_mine, b_recv):
    half, width = a_mine.shape
    return pl.pallas_call(
        fold_last_kernel,
        grid=(1,),
        out_shape=shape_of((1, 2 * half, width)),
        in_specs=[whole((half, width))] * 4,
        out_specs=whole((1, 2 * half, width)),
        compiler_params=params(),
        cost_estimate=cost(2 * half * width, 12 * half * width),
        name="fold_last",
    )(a_mine, a_recv, b_mine, b_recv)


def swap(value, bit, count=8):
    return lax.ppermute(value, "dp", [(i, i ^ bit) for i in range(count)])


def sum_over_dp(keep, send):
    a_send, a_keep, b_send, b_keep = fold(keep, swap(send, 1))
    a_recv, b_recv = swap(a_send, 2), swap(b_send, 4)
    a_next, a_mine, b_next, b_mine = fold_two(a_keep, a_recv, b_keep, b_recv)
    return fold_last(a_mine, swap(a_next, 4), b_mine, swap(b_next, 2))


def combine_out_kernel(n, z_ref, ids_ref, prob_ref, grad_ref, *refs):
    back_refs = refs[:n]
    out_ref, prob_grad_ref, rows, sums = refs[n:]
    ids = ids_ref[...]
    experts = [lax.rem(z_ref[0] + k, n) for k in range(n)]
    rank = ranks(ids, experts)
    firsts, seconds = [], []
    for k in range(n):
        rows[k * CAP : (k + 1) * CAP, :] = back_refs[k][...]
        first, second = chosen(ids, experts[k])
        at = places(rank[k : k + 1, :])
        firsts.append(jnp.where(jnp.logical_and(at, first), 1.0, 0.0))
        seconds.append(jnp.where(jnp.logical_and(at, second), 1.0, 0.0))
    tok_count = ids.shape[1]
    prob = jnp.concatenate([prob_ref[...], jnp.zeros((6, tok_count), F32)], axis=0).T
    grad = grad_ref[...].astype(F32)
    total = 0.0
    part = []
    for choice, at in enumerate((firsts, seconds)):
        out = mm_rows(jnp.concatenate(at, axis=0).astype(BF), rows[...])
        total = total + prob[:, choice : choice + 1] * out
        part.append(jnp.sum(grad * out, axis=1, keepdims=True))
    out_ref[...] = total.astype(BF)
    step = pl.program_id(0)
    both = jnp.concatenate(part + [jnp.zeros((tok_count, 6), F32)], axis=1)

    @pl.when(step == 0)
    def _():
        sums[...] = both

    @pl.when(step > 0)
    def _():
        sums[...] += both

    @pl.when(step == pl.num_programs(0) - 1)
    def _():
        prob_grad_ref[...] = sums[...].T[0:2, :]


def combine_out(z, ids_t, prob_t, out_grad, backs):
    n = len(backs)
    tok_count, width = out_grad.shape
    tile = 512
    by_tile = pl.BlockSpec((tok_count, tile), lambda j: (0, j))
    return pl.pallas_call(
        functools.partial(combine_out_kernel, n),
        grid=(width // tile,),
        out_shape=[shape_of((tok_count, width)), shape_of((2, tok_count), F32)],
        in_specs=[in_smem(), whole(ids_t.shape), whole(prob_t.shape), by_tile]
        + [pl.BlockSpec((CAP, tile), lambda j: (0, j))] * n,
        out_specs=[by_tile, whole((2, tok_count))],
        scratch_shapes=[pltpu.VMEM((n * CAP, tile), BF), pltpu.VMEM((tok_count, 8), F32)],
        compiler_params=params(),
        cost_estimate=cost(4 * n * CAP * tok_count * width, 2 * width * (n * CAP + 2 * tok_count)),
        name="combine_out",
    )(z, ids_t, prob_t, out_grad, *backs)


def combine_in_kernel(n, z_ref, ids_ref, *refs):
    back_refs = refs[:n]
    out_ref, rows = refs[n:]
    ids = ids_ref[...]
    experts = [lax.rem(z_ref[0] + k, n) for k in range(n)]
    rank = ranks(ids, experts)
    picks = []
    for k in range(n):
        rows[k * CAP : (k + 1) * CAP, :] = back_refs[k][...]
        here = jnp.logical_and(places(rank[k : k + 1, :]), jnp.logical_or(*chosen(ids, experts[k])))
        picks.append(jnp.where(here, 1.0, 0.0))
    out_ref[...] = mm_rows(jnp.concatenate(picks, axis=0).astype(BF), rows[...]).astype(BF)


def combine_in(z, ids_t, backs):
    n = len(backs)
    width = backs[0].shape[1]
    tok_count = ids_t.shape[1]
    tile = 1024
    return pl.pallas_call(
        functools.partial(combine_in_kernel, n),
        grid=(width // tile,),
        out_shape=shape_of((tok_count, width)),
        in_specs=[in_smem(), whole(ids_t.shape)] + [pl.BlockSpec((CAP, tile), lambda j: (0, j))] * n,
        out_specs=pl.BlockSpec((tok_count, tile), lambda j: (0, j)),
        scratch_shapes=[pltpu.VMEM((n * CAP, tile), BF)],
        compiler_params=params(),
        cost_estimate=cost(2 * n * CAP * tok_count * width, 2 * width * (n * CAP + tok_count)),
        name="combine_in",
    )(z, ids_t, *backs)


def shift(values, sign):
    n = len(values)
    order = sorted(range(1, n), key=lambda k: -min(k, n - k))
    moved = list(values)
    for k in order:
        moved[k] = lax.ppermute(values[k], "expert", [(i, (i + sign * k) % n) for i in range(n)])
    return moved


def local(tokens, expert_ids, gate_probs, w_gate, w_up, w_down, out_grad):
    n = lax.axis_size("expert")
    parts = lax.axis_size("dp")
    z = lax.axis_index("expert").astype(jnp.int32).reshape(1)
    ids_t, prob_t = expert_ids.T, gate_probs.T
    sent = pick_rows(n, z, ids_t, prob_t, tokens, out_grad)
    xs = shift(sent[:n], 1)
    gs = shift(sent[n:], 1)
    made = forward(xs, w_gate, w_up, w_down)
    slope, act, hidden = made[:3]
    back_out = shift(made[3:], -1)
    dgate, dup = hidden_grad(gs, w_down, slope, act)
    if parts == 8:
        me = lax.axis_index("dp").astype(jnp.int32)
        flips = [(r >> 2 & 1) | (r & 1) << 1 | (r >> 1 & 1) << 2 for r in range(8)]
        owners = jnp.stack([me ^ f for f in flips])
        sum_down = sum_over_dp(*down_part(parts, owners, gs, hidden))
        sum_gate = sum_over_dp(*weight_part(parts, owners, xs, dgate))
        sum_up = sum_over_dp(*weight_part(parts, owners, xs, dup))
    else:
        x_rows, d_rows = jnp.concatenate(xs, 0), jnp.concatenate(gs, 0)
        sum_gate, sum_up, sum_down = (
            lax.psum_scatter(mm_rows(a, b).astype(BF), "dp", scatter_dimension=0, tiled=True)[None]
            for a, b in ((x_rows, dgate), (x_rows, dup), (hidden, d_rows))
        )
    back_in = shift(input_grad(n, dgate, dup, w_gate, w_up), -1)
    layer_out, prob_grad_t = combine_out(z, ids_t, prob_t, out_grad, back_out)
    token_grad = combine_in(z, ids_t, back_in)
    return layer_out, prob_grad_t.T, token_grad, sum_gate, sum_up, sum_down


def solution(mesh):
    rows = P(("dp", "expert"), None)
    weights = P("expert", None, None)
    summed = P("expert", "dp", None)
    return jax.shard_map(
        local,
        mesh=mesh,
        in_specs=(rows, rows, rows, weights, weights, weights, rows),
        out_specs=(rows, rows, rows, summed, summed, summed),
        check_vma=False,
    )
```

```python
import functools
import jax
import jax.numpy as jnp
from jax import lax
from jax.experimental import pallas as pl
from jax.experimental.pallas import tpu as pltpu
from jax.sharding import PartitionSpec as P

CAP = 64
BF = jnp.bfloat16
F32 = jnp.float32
MIB = 1 << 20


def mm(left, right):
    return jnp.dot(left, right, preferred_element_type=F32)


def mm_rows(left, right):
    return lax.dot_general(left, right, (((0,), (0,)), ((), ())), preferred_element_type=F32)


def mm_cols(left, right):
    return lax.dot_general(left, right, (((1,), (1,)), ((), ())), preferred_element_type=F32)


def shape_of(shape, dtype=BF):
    return jax.ShapeDtypeStruct(tuple(shape), dtype)


def whole(shape):
    return pl.BlockSpec(tuple(shape), lambda *_: (0,) * len(shape))


def in_smem():
    return pl.BlockSpec(memory_space=pltpu.SMEM)


def params(limit=28):
    return pltpu.CompilerParams(vmem_limit_bytes=limit * MIB)


def call(kernel, after, in_specs, args, **kwargs):
    count = len(args)

    def body(*refs):
        kernel(*refs[:count], *refs[count + len(after) :])

    specs = list(in_specs) + [pl.BlockSpec(memory_space=pl.ANY)] * len(after)
    return pl.pallas_call(body, in_specs=specs, **kwargs)(*args, *after)


def cost(flops, moved):
    return pl.CostEstimate(flops=int(flops), bytes_accessed=int(moved), transcendentals=0)


def chosen(ids, expert):
    first = ids[0:1, :] == expert
    second = ids[1:2, :] == expert
    return first, second


def ranks(ids, experts):
    tok_count = ids.shape[1]
    masks = [jnp.where(jnp.logical_or(*chosen(ids, e)), 1.0, 0.0) for e in experts]
    mask = jnp.concatenate(masks + [jnp.zeros((-len(masks) % 16, tok_count), F32)], axis=0)
    before = lax.broadcasted_iota(jnp.int32, (tok_count, tok_count), 0)
    after = lax.broadcasted_iota(jnp.int32, (tok_count, tok_count), 1)
    upper = jnp.where(before < after, 1.0, 0.0).astype(BF)
    return mm(mask.astype(BF), upper).astype(jnp.int32)


def places(rank_row):
    tok_count = rank_row.shape[1]
    return lax.broadcasted_iota(jnp.int32, (CAP, tok_count), 0) == rank_row


def pick_kernel(n, z_ref, ids_ref, prob_ref, tok_ref, grad_ref, *outs):
    ids = ids_ref[...]
    prob = prob_ref[...]
    tok, grad = tok_ref[...], grad_ref[...]
    experts = [jnp.bitwise_xor(z_ref[0], k) for k in range(n)]
    rank = ranks(ids, experts)
    for k in range(n):
        first, second = chosen(ids, experts[k])
        at = places(rank[k : k + 1, :])
        here = jnp.logical_and(at, jnp.logical_or(first, second))
        pick = jnp.where(here, 1.0, 0.0)
        weight = jnp.where(first, prob[0:1, :], prob[1:2, :])
        scale = jnp.sum(jnp.where(here, weight, 0.0), axis=1, keepdims=True)
        outs[k][...] = mm(pick.astype(BF), tok).astype(BF)
        outs[n + k][...] = (scale * mm(pick.astype(BF), grad)).astype(BF)


def pick_rows(n, z, ids_t, prob_t, tokens, out_grad):
    tok_count, width = tokens.shape
    return pl.pallas_call(
        functools.partial(pick_kernel, n),
        out_shape=[shape_of((CAP, width))] * (2 * n),
        in_specs=[in_smem(), whole(ids_t.shape), whole(prob_t.shape)] + [whole(tokens.shape)] * 2,
        out_specs=[whole((CAP, width))] * (2 * n),
        grid=(1,),
        compiler_params=params(60),
        cost_estimate=cost(4 * n * CAP * tok_count * width, 4 * tok_count * width * 3),
        name="pick_rows",
    )(z, ids_t, prob_t, tokens, out_grad)


def silu_parts(gate):
    sig = jax.nn.sigmoid(gate)
    return gate * sig, sig * (1.0 + gate * (1.0 - sig))


def forward_kernel(n, steps, tile, *refs):
    x_refs = refs[:n]
    weights = refs[n : n + 3]
    slope_ref, act_ref, hid_ref = refs[n + 3 : n + 6]
    out_refs = refs[n + 6 : 2 * n + 6]
    rows, total, wg_buf, wu_buf, wd_buf, sems = refs[2 * n + 6 :]
    step = pl.program_id(0)

    def loads(j):
        at = pl.ds(pl.multiple_of(j * tile, tile), tile)
        wg_ref, wu_ref, wd_ref = weights
        return (
            pltpu.make_async_copy(wg_ref.at[0, :, at], wg_buf.at[j], sems.at[0, j]),
            pltpu.make_async_copy(wu_ref.at[0, :, at], wu_buf.at[j], sems.at[1, j]),
            pltpu.make_async_copy(wd_ref.at[0, at, :], wd_buf.at[j], sems.at[2, j]),
        )

    @pl.when(step == 0)
    def _():
        for j in range(steps):
            for load in loads(j):
                load.start()
        for k in range(n):
            rows[k * CAP : (k + 1) * CAP, :] = x_refs[k][...]

    for load in loads(step):
        load.wait()
    gate = mm(rows[...], wg_buf[step])
    up = mm(rows[...], wu_buf[step])
    act, slope = silu_parts(gate)
    act_ref[...] = act
    slope_ref[...] = up * slope
    hidden = (act * up).astype(BF)
    hid_ref[...] = hidden
    part = mm(hidden, wd_buf[step])

    @pl.when(step == 0)
    def _():
        total[...] = part

    @pl.when(step > 0)
    def _():
        total[...] += part

    @pl.when(step == steps - 1)
    def _():
        for k in range(n):
            out_refs[k][...] = total[k * CAP : (k + 1) * CAP, :].astype(BF)


def weight_specs(width, tile):
    by_col = pl.BlockSpec((1, width, tile), lambda j: (0, 0, j))
    by_row = pl.BlockSpec((1, tile, width), lambda j: (0, j, 0))
    return [by_col, by_col, by_row]


def forward(xs, w_gate, w_up, w_down):
    n = len(xs)
    width, ff = w_gate.shape[1:]
    tile = 256
    steps = ff // tile
    rows = n * CAP
    part = pl.BlockSpec((rows, tile), lambda j: (0, j))
    return pl.pallas_call(
        functools.partial(forward_kernel, n, steps, tile),
        grid=(steps,),
        out_shape=[shape_of((rows, ff), F32)] * 2 + [shape_of((rows, ff))] + [shape_of((CAP, width))] * n,
        in_specs=[whole((CAP, width))] * n + [pl.BlockSpec(memory_space=pltpu.HBM)] * 3,
        out_specs=[part, part, part] + [whole((CAP, width))] * n,
        scratch_shapes=[
            pltpu.VMEM((rows, width), BF),
            pltpu.VMEM((rows, width), F32),
            pltpu.VMEM((steps, width, tile), BF),
            pltpu.VMEM((steps, width, tile), BF),
            pltpu.VMEM((steps, tile, width), BF),
            pltpu.SemaphoreType.DMA((3, steps)),
        ],
        compiler_params=params(),
        cost_estimate=cost(6 * rows * width * ff, 6 * width * ff + 4 * rows * width + 10 * rows * ff),
        name="forward",
    )(*xs, w_gate, w_up, w_down)


def turn_kernel(n, parts, me_ref, *refs):
    x_refs = refs[:n]
    hid_ref, keep_ref, send_ref, rows, turned = refs[n:]
    for k in range(n):
        rows[k * CAP : (k + 1) * CAP, :] = x_refs[k][...]
    turned[...] = hid_ref[...].T
    half = parts // 2
    x_size, h_size = rows.shape[1] // parts, turned.shape[0] // parts
    strip = h_size // 6
    for rel in range(parts):
        out_ref, i = (keep_ref, rel) if rel < half else (send_ref, rel - half)
        at = pl.multiple_of(me_ref[rel] * x_size, x_size)
        out_ref[i * x_size : (i + 1) * x_size, :] = rows[:, pl.ds(at, x_size)].T
        for j in range(6):
            at = pl.multiple_of(me_ref[rel] * h_size + j * strip, strip)
            base = half * x_size + ((j % 3) * 2 * half + 2 * i + j // 3) * strip
            out_ref[base : base + strip, :] = turned[pl.ds(at, strip), :]


def turn(parts, owners, xs, hidden):
    n = len(xs)
    width = xs[0].shape[1]
    rows, ff = hidden.shape
    high = (width + ff) // 2
    return pl.pallas_call(
        functools.partial(turn_kernel, n, parts),
        grid=(1,),
        out_shape=[shape_of((high, rows))] * 2,
        in_specs=[in_smem()] + [whole((CAP, width))] * n + [whole(hidden.shape)],
        out_specs=[whole((high, rows))] * 2,
        scratch_shapes=[pltpu.VMEM((rows, width), BF), pltpu.VMEM((ff, rows), BF)],
        compiler_params=params(),
        cost_estimate=cost(2 * rows * width, 6 * rows * (width + ff)),
        name="turn",
    )(owners, *xs, hidden)


def outer_kernel(keep_ref, recv_ref, own_ref, other_ref, own_g_ref, other_g_ref, x_send, x_keep, y_send, y_keep):
    step = pl.program_id(0)
    half, high = 4, own_ref.shape[0] // 2
    size = 256
    strip = 16
    for block in range(half):
        at = slice(block * size, (block + 1) * size)
        across, along = block & 1, block >> 1
        gate = mm(keep_ref[at, :], own_ref[:high, :]) + mm(recv_ref[at, :], other_ref[:high, :])
        (x_send if across else x_keep)[along, :size, :] = gate.astype(BF)
        up = mm(keep_ref[at, :], own_ref[high:, :]) + mm(recv_ref[at, :], other_ref[high:, :])
        (y_send if along else y_keep)[across, :size, :] = up.astype(BF)
    at = pl.ds(pl.multiple_of(half * size + step * 2 * half * strip, strip), 2 * half * strip)
    down = mm(keep_ref[at, :], own_g_ref[...]) + mm(recv_ref[at, :], other_g_ref[...])
    down = down.astype(BF)
    tile = x_send.shape[2]
    for block in range(half):
        across, along = block & 1, block >> 1
        for part, (out_ref, i) in enumerate(
            ((x_send if across else x_keep, along), (y_send if along else y_keep, across))
        ):
            base = (2 * block + part) * strip
            for c in range(down.shape[1] // tile):
                out_ref[i, size + c * strip : size + (c + 1) * strip, :] = down[
                    base : base + strip, c * tile : (c + 1) * tile
                ]


def outer(keep, recv, own, other, own_g, other_g):
    rows, width = own_g.shape
    ff = own.shape[1]
    tile = 256
    col = pl.BlockSpec((2 * rows, tile), lambda j: (0, j))
    high = 256 + 16 * (width // tile)
    part = pl.BlockSpec((2, high, tile), lambda j: (0, 0, j))
    return pl.pallas_call(
        outer_kernel,
        grid=(ff // tile,),
        out_shape=[shape_of((2, high, ff))] * 4,
        in_specs=[whole(keep.shape)] * 2 + [col] * 2 + [whole(own_g.shape)] * 2,
        out_specs=[part] * 4,
        compiler_params=params(),
        cost_estimate=cost(6 * rows * width * ff, 4 * keep.size + 16 * high * ff),
        name="outer",
    )(keep, recv, own, other, own_g, other_g)


def hidden_grad_kernel(n, *refs):
    g_refs = refs[:n]
    wd_ref, slope_ref, act_ref, grad_ref, rows = refs[n:]

    @pl.when(pl.program_id(0) == 0)
    def _():
        for k in range(n):
            rows[k * CAP : (k + 1) * CAP, :] = g_refs[k][...]

    grad = mm_cols(rows[...], wd_ref[0])
    grad_ref[: n * CAP, :] = (grad * slope_ref[...]).astype(BF)
    grad_ref[n * CAP :, :] = (grad * act_ref[...]).astype(BF)


def hidden_grad(gs, w_down, slope, act, after):
    n = len(gs)
    ff, width = w_down.shape[1:]
    rows = n * CAP
    tile = 256
    part = pl.BlockSpec((rows, tile), lambda j: (0, j))
    return call(
        functools.partial(hidden_grad_kernel, n),
        after,
        grid=(ff // tile,),
        out_shape=[shape_of((2 * rows, ff)), shape_of((rows, width))],
        in_specs=[whole((CAP, width))] * n + [weight_specs(width, tile)[2], part, part],
        args=(*gs, w_down, slope, act),
        out_specs=[pl.BlockSpec((2 * rows, tile), lambda j: (0, j)), whole((rows, width))],
        compiler_params=params(),
        cost_estimate=cost(2 * rows * width * ff, 2 * width * ff + 4 * rows * width + 12 * rows * ff),
        name="hidden_grad",
    )


def input_grad_kernel(n, grad_ref, wg_ref, wu_ref, *out_refs):
    rows = n * CAP
    total = mm_cols(grad_ref[:rows, :], wg_ref[0]) + mm_cols(grad_ref[rows:, :], wu_ref[0])
    for k in range(n):
        out_refs[k][...] = total[k * CAP : (k + 1) * CAP, :].astype(BF)


def input_grad(n, grad, w_gate, w_up, after):
    rows, ff = n * CAP, grad.shape[1]
    width = w_gate.shape[1]
    tile = 512
    by_row = pl.BlockSpec((1, tile, ff), lambda j: (0, j, 0))
    return call(
        functools.partial(input_grad_kernel, n),
        after,
        grid=(width // tile,),
        out_shape=[shape_of((CAP, width))] * n,
        in_specs=[whole((2 * rows, ff)), by_row, by_row],
        args=(grad, w_gate, w_up),
        out_specs=[pl.BlockSpec((CAP, tile), lambda j: (0, j))] * n,
        compiler_params=params(),
        cost_estimate=cost(4 * rows * width * ff, 4 * width * ff + 2 * rows * (width + 2 * ff)),
        name="input_grad",
    )


def fold_two_kernel(x_keep, x_recv, y_keep, y_recv, x_next, x_mine, y_next, y_mine):
    for keep, recv, away, mine in ((x_keep, x_recv, x_next, x_mine), (y_keep, y_recv, y_next, y_mine)):
        away[...] = (keep[1].astype(F32) + recv[1].astype(F32)).astype(BF)
        mine[...] = (keep[0].astype(F32) + recv[0].astype(F32)).astype(BF)


def fold_two(x_keep, x_recv, y_keep, y_recv, after):
    _, high, width = x_keep.shape
    return call(
        fold_two_kernel,
        after,
        grid=(1,),
        out_shape=[shape_of((high, width))] * 4,
        in_specs=[whole((2, high, width))] * 4,
        args=(x_keep, x_recv, y_keep, y_recv),
        out_specs=[whole((high, width))] * 4,
        compiler_params=params(),
        cost_estimate=cost(4 * high * width, 24 * high * width),
        name="fold_two",
    )


def fold_last_kernel(x_mine, x_recv, y_mine, y_recv, gate_ref, up_ref, down_ref):
    size, strip = gate_ref.shape[1], 16
    tile = 256
    for i, (mine, recv, out_ref) in enumerate(((x_mine, x_recv, gate_ref), (y_mine, y_recv, up_ref))):
        total = (mine[...].astype(F32) + recv[...].astype(F32)).astype(BF)
        out_ref[0] = total[:size]
        for c in range(down_ref.shape[2] // tile):
            for j in range(3):
                down_ref[0, (3 * i + j) * strip : (3 * i + j + 1) * strip, c * tile : (c + 1) * tile] = total[
                    size + c * strip : size + (c + 1) * strip, j * tile : (j + 1) * tile
                ]


def fold_last(x_mine, x_recv, y_mine, y_recv, shapes):
    high, width = x_mine.shape
    return pl.pallas_call(
        fold_last_kernel,
        grid=(1,),
        out_shape=[shape_of(s) for s in shapes],
        in_specs=[whole((high, width))] * 4,
        out_specs=[whole(s) for s in shapes],
        compiler_params=params(),
        cost_estimate=cost(2 * high * width, 12 * high * width),
        name="fold_last",
    )(x_mine, x_recv, y_mine, y_recv)


CORE, ALONG_X, ALONG_Y = 1, 2, 4


def swap(value, bit, count=8):
    return lax.ppermute(value, "dp", [(i, i ^ bit) for i in range(count)])


def combine_kernel(n, z_ref, ids_ref, prob_ref, grad_ref, *refs):
    out_back_refs, in_back_refs = refs[:n], refs[n : 2 * n]
    out_ref, in_ref, prob_grad_ref, out_rows, in_rows, sums, firsts, seconds = refs[2 * n :]
    tok_count = ids_ref.shape[1]
    step = pl.program_id(0)

    @pl.when(step == 0)
    def _():
        ids = ids_ref[...]
        experts = [jnp.bitwise_xor(z_ref[0], k) for k in range(n)]
        rank = ranks(ids, experts)
        for k in range(n):
            first, second = chosen(ids, experts[k])
            at = places(rank[k : k + 1, :])
            rows = slice(k * CAP, (k + 1) * CAP)
            firsts[rows, :] = jnp.where(jnp.logical_and(at, first), 1.0, 0.0)
            seconds[rows, :] = jnp.where(jnp.logical_and(at, second), 1.0, 0.0)
        sums[...] = jnp.zeros_like(sums)

    for k in range(n):
        out_rows[k * CAP : (k + 1) * CAP, :] = out_back_refs[k][...]
        in_rows[k * CAP : (k + 1) * CAP, :] = in_back_refs[k][...]
    prob = jnp.concatenate([prob_ref[...], jnp.zeros((6, tok_count), F32)], axis=0).T
    grad = grad_ref[...].astype(F32)
    one, two = firsts[...].astype(BF), seconds[...].astype(BF)
    total = 0.0
    part = []
    for choice, at in enumerate((one, two)):
        out = mm_rows(at, out_rows[...])
        total = total + prob[:, choice : choice + 1] * out
        part.append(jnp.sum(grad * out, axis=1, keepdims=True))
    out_ref[...] = total.astype(BF)
    in_ref[...] = mm_rows(one + two, in_rows[...]).astype(BF)
    sums[...] += jnp.concatenate(part + [jnp.zeros((tok_count, 6), F32)], axis=1)

    @pl.when(step == pl.num_programs(0) - 1)
    def _():
        prob_grad_ref[...] = sums[...].T[0:2, :]


def combine(z, ids_t, prob_t, out_grad, back_out, back_in):
    n = len(back_in)
    tok_count, width = out_grad.shape
    tile = 512
    by_tile = pl.BlockSpec((tok_count, tile), lambda j: (0, j))
    rows = n * CAP
    return pl.pallas_call(
        functools.partial(combine_kernel, n),
        grid=(width // tile,),
        out_shape=[shape_of((tok_count, width))] * 2 + [shape_of((2, tok_count), F32)],
        in_specs=[in_smem(), whole(ids_t.shape), whole(prob_t.shape), by_tile]
        + [pl.BlockSpec((CAP, tile), lambda j: (0, j))] * (2 * n),
        out_specs=[by_tile, by_tile, whole((2, tok_count))],
        scratch_shapes=[pltpu.VMEM((rows, tile), BF)] * 2
        + [pltpu.VMEM((tok_count, 8), F32)]
        + [pltpu.VMEM((rows, tok_count), F32)] * 2,
        compiler_params=params(),
        cost_estimate=cost(6 * rows * tok_count * width, 4 * width * (rows + 2 * tok_count)),
        name="combine",
    )(z, ids_t, prob_t, out_grad, *back_out, *back_in)


def exchange(values):
    n = len(values)
    moved = list(values)
    for k in range(n - 1, 0, -1):
        moved[k] = lax.ppermute(values[k], "expert", [(i, i ^ k) for i in range(n)])
    return moved


def local(tokens, expert_ids, gate_probs, w_gate, w_up, w_down, out_grad):
    n = lax.axis_size("expert")
    parts = lax.axis_size("dp")
    z = lax.axis_index("expert").astype(jnp.int32).reshape(1)
    ids_t, prob_t = expert_ids.T, gate_probs.T
    sent = pick_rows(n, z, ids_t, prob_t, tokens, out_grad)
    xs, gs = exchange(sent[:n]), exchange(sent[n:])
    made = forward(xs, w_gate, w_up, w_down)
    slope, act, hidden = made[:3]
    back_out = exchange(made[3:])
    if parts == 8:
        me = lax.axis_index("dp").astype(jnp.int32)
        flips = [(r >> 2 & 1) * CORE | (r & 1) * ALONG_X | (r >> 1 & 1) * ALONG_Y for r in range(8)]
        owners = jnp.stack([me ^ f for f in flips])
        keep_t, send_t = turn(parts, owners, xs, hidden)
        grad, g_rows = hidden_grad(gs, w_down, slope, act, [keep_t])
        x_send, x_keep, y_send, y_keep = outer(
            keep_t, swap(send_t, CORE), grad, swap(grad, CORE), g_rows, swap(g_rows, CORE)
        )
        back_in = exchange(input_grad(n, grad, w_gate, w_up, [x_send]))
        x_next, x_mine, y_next, y_mine = fold_two(
            x_keep, swap(x_send, ALONG_X), y_keep, swap(y_send, ALONG_Y), [back_in[0], *back_out[1:]]
        )
        shapes = [(1, d // parts, w) for d, w in (w_gate.shape[1:], w_up.shape[1:], w_down.shape[1:])]
        sum_gate, sum_up, sum_down = fold_last(x_mine, swap(x_next, ALONG_Y), y_mine, swap(y_next, ALONG_X), shapes)
    else:
        grad, d_rows = hidden_grad(gs, w_down, slope, act, [])
        back_in = exchange(input_grad(n, grad, w_gate, w_up, []))
        x_rows, count = jnp.concatenate(xs, 0), n * CAP
        sum_gate, sum_up, sum_down = (
            lax.psum_scatter(mm_rows(a, b).astype(BF), "dp", scatter_dimension=0, tiled=True)[None]
            for a, b in ((x_rows, grad[:count]), (x_rows, grad[count:]), (hidden, d_rows))
        )
    layer_out, token_grad, prob_grad_t = combine(z, ids_t, prob_t, out_grad, back_out, back_in)
    return layer_out, prob_grad_t.T, token_grad, sum_gate, sum_up, sum_down


def solution(mesh):
    rows = P(("dp", "expert"), None)
    weights = P("expert", None, None)
    summed = P("expert", "dp", None)
    return jax.shard_map(
        local,
        mesh=mesh,
        in_specs=(rows, rows, rows, weights, weights, weights, rows),
        out_specs=(rows, rows, rows, summed, summed, summed),
        check_vma=False,
    )
```

```python
import functools
import jax
import jax.numpy as jnp
from jax import lax
from jax.experimental import pallas as pl
from jax.experimental.pallas import tpu as pltpu
from jax.sharding import PartitionSpec as P

CAP = 64
BF = jnp.bfloat16
F32 = jnp.float32
MIB = 1 << 20


def mm(left, right):
    return jnp.dot(left, right, preferred_element_type=F32)


def mm_rows(left, right):
    return lax.dot_general(left, right, (((0,), (0,)), ((), ())), preferred_element_type=F32)


def mm_cols(left, right):
    return lax.dot_general(left, right, (((1,), (1,)), ((), ())), preferred_element_type=F32)


def shape_of(shape, dtype=BF):
    return jax.ShapeDtypeStruct(tuple(shape), dtype)


def whole(shape):
    return pl.BlockSpec(tuple(shape), lambda *_: (0,) * len(shape))


def in_smem():
    return pl.BlockSpec(memory_space=pltpu.SMEM)


def params(limit=16):
    return pltpu.CompilerParams(vmem_limit_bytes=limit * MIB)


def call(kernel, after, in_specs, args, **kwargs):
    count = len(args)

    def body(*refs):
        kernel(*refs[:count], *refs[count + len(after) :])

    specs = list(in_specs) + [pl.BlockSpec(memory_space=pl.ANY)] * len(after)
    return pl.pallas_call(body, in_specs=specs, **kwargs)(*args, *after)


def cost(flops, moved):
    return pl.CostEstimate(flops=int(flops), bytes_accessed=int(moved), transcendentals=0)


def chosen(ids, expert):
    first = ids[0:1, :] == expert
    second = ids[1:2, :] == expert
    return first, second


def ranks(ids, experts):
    tok_count = ids.shape[1]
    masks = [jnp.where(jnp.logical_or(*chosen(ids, e)), 1.0, 0.0) for e in experts]
    mask = jnp.concatenate(masks + [jnp.zeros((-len(masks) % 16, tok_count), F32)], axis=0)
    before = lax.broadcasted_iota(jnp.int32, (tok_count, tok_count), 0)
    after = lax.broadcasted_iota(jnp.int32, (tok_count, tok_count), 1)
    upper = jnp.where(before < after, 1.0, 0.0).astype(BF)
    return mm(mask.astype(BF), upper).astype(jnp.int32)


def places(rank_row):
    tok_count = rank_row.shape[1]
    return lax.broadcasted_iota(jnp.int32, (CAP, tok_count), 0) == rank_row


def pick_kernel(n, z_ref, ids_ref, prob_ref, tok_ref, grad_ref, *outs):
    ids = ids_ref[...]
    prob = prob_ref[...]
    tok, grad = tok_ref[...], grad_ref[...]
    experts = [jnp.bitwise_xor(z_ref[0], k) for k in range(n)]
    rank = ranks(ids, experts)
    for k in range(n):
        first, second = chosen(ids, experts[k])
        at = places(rank[k : k + 1, :])
        here = jnp.logical_and(at, jnp.logical_or(first, second))
        pick = jnp.where(here, 1.0, 0.0)
        weight = jnp.where(first, prob[0:1, :], prob[1:2, :])
        scale = jnp.sum(jnp.where(here, weight, 0.0), axis=1, keepdims=True)
        outs[k][...] = mm(pick.astype(BF), tok).astype(BF)
        outs[n + k][...] = (scale * mm(pick.astype(BF), grad)).astype(BF)


def pick_rows(n, z, ids_t, prob_t, tokens, out_grad):
    tok_count, width = tokens.shape
    return pl.pallas_call(
        functools.partial(pick_kernel, n),
        out_shape=[shape_of((CAP, width))] * (2 * n),
        in_specs=[in_smem(), whole(ids_t.shape), whole(prob_t.shape)] + [whole(tokens.shape)] * 2,
        out_specs=[whole((CAP, width))] * (2 * n),
        grid=(1,),
        compiler_params=params(60),
        cost_estimate=cost(4 * n * CAP * tok_count * width, 4 * tok_count * width * 3),
        name="pick_rows",
    )(z, ids_t, prob_t, tokens, out_grad)


def silu_parts(gate):
    sig = jax.nn.sigmoid(gate)
    return gate * sig, sig * (1.0 + gate * (1.0 - sig))


def forward_kernel(n, steps, tile, *refs):
    x_refs = refs[:n]
    weights = refs[n : n + 3]
    slope_ref, act_ref, hid_ref = refs[n + 3 : n + 6]
    out_refs = refs[n + 6 : 2 * n + 6]
    rows, total, wg_buf, wu_buf, wd_buf, sems = refs[2 * n + 6 :]
    step = pl.program_id(0)

    def loads(j):
        at = pl.ds(pl.multiple_of(j * tile, tile), tile)
        wg_ref, wu_ref, wd_ref = weights
        return (
            pltpu.make_async_copy(wg_ref.at[0, :, at], wg_buf.at[j], sems.at[0, j]),
            pltpu.make_async_copy(wu_ref.at[0, :, at], wu_buf.at[j], sems.at[1, j]),
            pltpu.make_async_copy(wd_ref.at[0, at, :], wd_buf.at[j], sems.at[2, j]),
        )

    @pl.when(step == 0)
    def _():
        for j in range(steps):
            for load in loads(j):
                load.start()
        for k in range(n):
            rows[k * CAP : (k + 1) * CAP, :] = x_refs[k][...]

    for load in loads(step):
        load.wait()
    gate = mm(rows[...], wg_buf[step])
    up = mm(rows[...], wu_buf[step])
    act, slope = silu_parts(gate)
    act_ref[...] = act
    slope_ref[...] = up * slope
    hidden = (act * up).astype(BF)
    hid_ref[...] = hidden
    part = mm(hidden, wd_buf[step])

    @pl.when(step == 0)
    def _():
        total[...] = part

    @pl.when(step > 0)
    def _():
        total[...] += part

    @pl.when(step == steps - 1)
    def _():
        for k in range(n):
            out_refs[k][...] = total[k * CAP : (k + 1) * CAP, :].astype(BF)


def weight_specs(width, tile):
    by_col = pl.BlockSpec((1, width, tile), lambda j: (0, 0, j))
    by_row = pl.BlockSpec((1, tile, width), lambda j: (0, j, 0))
    return [by_col, by_col, by_row]


def forward(xs, w_gate, w_up, w_down):
    n = len(xs)
    width, ff = w_gate.shape[1:]
    tile = 256
    steps = ff // tile
    rows = n * CAP
    part = pl.BlockSpec((rows, tile), lambda j: (0, j))
    return pl.pallas_call(
        functools.partial(forward_kernel, n, steps, tile),
        grid=(steps,),
        out_shape=[shape_of((rows, ff), F32)] * 2 + [shape_of((rows, ff))] + [shape_of((CAP, width))] * n,
        in_specs=[whole((CAP, width))] * n + [pl.BlockSpec(memory_space=pltpu.HBM)] * 3,
        out_specs=[part, part, part] + [whole((CAP, width))] * n,
        scratch_shapes=[
            pltpu.VMEM((rows, width), BF),
            pltpu.VMEM((rows, width), F32),
            pltpu.VMEM((steps, width, tile), BF),
            pltpu.VMEM((steps, width, tile), BF),
            pltpu.VMEM((steps, tile, width), BF),
            pltpu.SemaphoreType.DMA((3, steps)),
        ],
        compiler_params=params(50),
        cost_estimate=cost(6 * rows * width * ff, 6 * width * ff + 4 * rows * width + 10 * rows * ff),
        name="forward",
    )(*xs, w_gate, w_up, w_down)


def turn_kernel(n, parts, me_ref, *refs):
    x_refs = refs[:n]
    hid_ref, w_ref, keep_ref, send_ref, copy_ref, rows, turned, sem = refs[n:]
    load = pltpu.make_async_copy(w_ref, copy_ref, sem)
    load.start()
    for k in range(n):
        rows[k * CAP : (k + 1) * CAP, :] = x_refs[k][...]
    turned[...] = hid_ref[...].T
    half = parts // 2
    x_size, h_size = rows.shape[1] // parts, turned.shape[0] // parts
    strip = h_size // 6
    for rel in range(parts):
        out_ref, i = (keep_ref, rel) if rel < half else (send_ref, rel - half)
        at = pl.multiple_of(me_ref[rel] * x_size, x_size)
        out_ref[i * x_size : (i + 1) * x_size, :] = rows[:, pl.ds(at, x_size)].T
        for j in range(6):
            at = pl.multiple_of(me_ref[rel] * h_size + j * strip, strip)
            base = half * x_size + ((j % 3) * 2 * half + 2 * i + j // 3) * strip
            out_ref[base : base + strip, :] = turned[pl.ds(at, strip), :]
    load.wait()


def turn(parts, owners, xs, hidden, w_down):
    n = len(xs)
    width = xs[0].shape[1]
    rows, ff = hidden.shape
    high = (width + ff) // 2
    return pl.pallas_call(
        functools.partial(turn_kernel, n, parts),
        grid=(1,),
        out_shape=[shape_of((high, rows))] * 2 + [shape_of(w_down.shape)],
        in_specs=[in_smem()] + [whole((CAP, width))] * n + [whole(hidden.shape), pl.BlockSpec(memory_space=pltpu.HBM)],
        out_specs=[whole((high, rows))] * 2 + [whole(w_down.shape)],
        scratch_shapes=[pltpu.VMEM((rows, width), BF), pltpu.VMEM((ff, rows), BF), pltpu.SemaphoreType.DMA],
        compiler_params=params(),
        cost_estimate=cost(2 * rows * width, 6 * rows * (width + ff)),
        name="turn",
    )(owners, *xs, hidden, w_down)


def outer_kernel(keep_ref, recv_ref, own_ref, other_ref, own_g_ref, other_g_ref, x_send, x_keep, y_send, y_keep):
    step = pl.program_id(0)
    half, high = 4, own_ref.shape[0] // 2
    size = 256
    strip = 16
    for block in range(half):
        at = slice(block * size, (block + 1) * size)
        across, along = block & 1, block >> 1
        gate = mm(keep_ref[at, :], own_ref[:high, :]) + mm(recv_ref[at, :], other_ref[:high, :])
        (x_send if across else x_keep)[along, :size, :] = gate.astype(BF)
        up = mm(keep_ref[at, :], own_ref[high:, :]) + mm(recv_ref[at, :], other_ref[high:, :])
        (y_send if along else y_keep)[across, :size, :] = up.astype(BF)
    at = pl.ds(pl.multiple_of(half * size + step * 2 * half * strip, strip), 2 * half * strip)
    down = mm(keep_ref[at, :], own_g_ref[...]) + mm(recv_ref[at, :], other_g_ref[...])
    down = down.astype(BF)
    tile = x_send.shape[2]
    for block in range(half):
        across, along = block & 1, block >> 1
        for part, (out_ref, i) in enumerate(
            ((x_send if across else x_keep, along), (y_send if along else y_keep, across))
        ):
            base = (2 * block + part) * strip
            for c in range(down.shape[1] // tile):
                out_ref[i, size + c * strip : size + (c + 1) * strip, :] = down[
                    base : base + strip, c * tile : (c + 1) * tile
                ]


def outer(keep, recv, own, other, own_g, other_g, after):
    rows, width = own_g.shape
    ff = own.shape[1]
    tile = 256
    col = pl.BlockSpec((2 * rows, tile), lambda j: (0, j))
    high = 256 + 16 * (width // tile)
    part = pl.BlockSpec((2, high, tile), lambda j: (0, 0, j))
    return call(
        outer_kernel,
        after,
        grid=(ff // tile,),
        out_shape=[shape_of((2, high, ff))] * 4,
        in_specs=[whole(keep.shape)] * 2 + [col] * 2 + [whole(own_g.shape)] * 2,
        args=(keep, recv, own, other, own_g, other_g),
        out_specs=[part] * 4,
        compiler_params=params(),
        cost_estimate=cost(6 * rows * width * ff, 4 * keep.size + 16 * high * ff),
        name="outer",
    )


def hidden_grad_kernel(n, *refs):
    g_refs = refs[:n]
    wd_ref, slope_ref, act_ref, grad_ref, rows = refs[n:]

    @pl.when(pl.program_id(0) == 0)
    def _():
        for k in range(n):
            rows[k * CAP : (k + 1) * CAP, :] = g_refs[k][...]

    grad = mm_cols(rows[...], wd_ref[0])
    grad_ref[: n * CAP, :] = (grad * slope_ref[...]).astype(BF)
    grad_ref[n * CAP :, :] = (grad * act_ref[...]).astype(BF)


def hidden_grad(gs, w_down, slope, act, after):
    n = len(gs)
    ff, width = w_down.shape[1:]
    rows = n * CAP
    tile = 256
    part = pl.BlockSpec((rows, tile), lambda j: (0, j))
    return call(
        functools.partial(hidden_grad_kernel, n),
        after,
        grid=(ff // tile,),
        out_shape=[shape_of((2 * rows, ff)), shape_of((rows, width))],
        in_specs=[whole((CAP, width))] * n + [weight_specs(width, tile)[2], part, part],
        args=(*gs, w_down, slope, act),
        out_specs=[pl.BlockSpec((2 * rows, tile), lambda j: (0, j)), whole((rows, width))],
        compiler_params=params(),
        cost_estimate=cost(2 * rows * width * ff, 2 * width * ff + 4 * rows * width + 12 * rows * ff),
        name="hidden_grad",
    )


def input_grad_kernel(n, steps, tile, z_ref, grad_ref, wg_ref, wu_ref, *refs):
    out_ref, wg_buf, wu_buf, sems = refs
    step = pl.program_id(0)

    def loads(j):
        at = pl.ds(pl.multiple_of(j * tile, tile), tile)
        return (
            pltpu.make_async_copy(wg_ref.at[0, at, :], wg_buf.at[j], sems.at[0, j]),
            pltpu.make_async_copy(wu_ref.at[0, at, :], wu_buf.at[j], sems.at[1, j]),
        )

    @pl.when(step == 0)
    def _():
        for j in range(steps):
            for load in loads(j):
                load.start()

    for load in loads(step):
        load.wait()
    rows = n * CAP
    total = mm_cols(grad_ref[:rows, :], wg_buf[step]) + mm_cols(grad_ref[rows:, :], wu_buf[step])
    for k in range(n):
        partner = jnp.bitwise_xor(z_ref[0], k)
        out_ref[partner] = total[k * CAP : (k + 1) * CAP, :].astype(BF)


def input_grad(z, n, grad, w_gate, w_up):
    rows, ff = n * CAP, grad.shape[1]
    width = w_gate.shape[1]
    tile = 512
    steps = width // tile
    return pl.pallas_call(
        functools.partial(input_grad_kernel, n, steps, tile),
        grid=(steps,),
        out_shape=shape_of((n, CAP, width)),
        in_specs=[in_smem(), whole((2 * rows, ff))] + [pl.BlockSpec(memory_space=pltpu.HBM)] * 2,
        out_specs=pl.BlockSpec((n, CAP, tile), lambda j: (0, 0, j)),
        scratch_shapes=[pltpu.VMEM((steps, tile, ff), BF)] * 2 + [pltpu.SemaphoreType.DMA((2, steps))],
        compiler_params=params(),
        cost_estimate=cost(4 * rows * width * ff, 4 * width * ff + 2 * rows * (width + 2 * ff)),
        name="input_grad",
    )(z, grad, w_gate, w_up)


def hold_kernel(_, __):
    pass


def hold(value, after):
    return call(
        hold_kernel,
        after,
        [pl.BlockSpec(memory_space=pl.ANY)],
        [value],
        out_shape=shape_of(value.shape),
        out_specs=pl.BlockSpec(memory_space=pl.ANY),
        input_output_aliases={0: 0},
        name="hold",
    )


def fold_two_kernel(x_keep, x_recv, y_keep, y_recv, x_next, x_mine, y_next, y_mine):
    for keep, recv, away, mine in ((x_keep, x_recv, x_next, x_mine), (y_keep, y_recv, y_next, y_mine)):
        away[...] = (keep[1].astype(F32) + recv[1].astype(F32)).astype(BF)
        mine[...] = (keep[0].astype(F32) + recv[0].astype(F32)).astype(BF)


def fold_two(x_keep, x_recv, y_keep, y_recv, after):
    _, high, width = x_keep.shape
    return call(
        fold_two_kernel,
        after,
        grid=(1,),
        out_shape=[shape_of((high, width))] * 4,
        in_specs=[whole((2, high, width))] * 4,
        args=(x_keep, x_recv, y_keep, y_recv),
        out_specs=[whole((high, width))] * 4,
        compiler_params=params(),
        cost_estimate=cost(4 * high * width, 24 * high * width),
        name="fold_two",
    )


def fold_last_kernel(x_mine, x_recv, y_mine, y_recv, gate_ref, up_ref, down_ref):
    size, strip = gate_ref.shape[1], 16
    tile = 256
    for i, (mine, recv, out_ref) in enumerate(((x_mine, x_recv, gate_ref), (y_mine, y_recv, up_ref))):
        total = (mine[...].astype(F32) + recv[...].astype(F32)).astype(BF)
        out_ref[0] = total[:size]
        for c in range(down_ref.shape[2] // tile):
            for j in range(3):
                down_ref[0, (3 * i + j) * strip : (3 * i + j + 1) * strip, c * tile : (c + 1) * tile] = total[
                    size + c * strip : size + (c + 1) * strip, j * tile : (j + 1) * tile
                ]


def fold_last(x_mine, x_recv, y_mine, y_recv, shapes, after):
    high, width = x_mine.shape
    return call(
        fold_last_kernel,
        after,
        grid=(1,),
        out_shape=[shape_of(s) for s in shapes],
        in_specs=[whole((high, width))] * 4,
        args=(x_mine, x_recv, y_mine, y_recv),
        out_specs=[whole(s) for s in shapes],
        compiler_params=params(),
        cost_estimate=cost(2 * high * width, 12 * high * width),
        name="fold_last",
    )


CORE, ALONG_X, ALONG_Y = 1, 2, 4


def swap(value, bit, count=8):
    return lax.ppermute(value, "dp", [(i, i ^ bit) for i in range(count)])


def combine_kernel(n, z_ref, ids_ref, prob_ref, grad_ref, *refs):
    out_back_refs, in_back_ref = refs[:n], refs[n]
    out_ref, in_ref, prob_grad_ref, out_rows, in_rows, sums, firsts, seconds = refs[n + 1 :]
    tok_count = ids_ref.shape[1]
    step = pl.program_id(0)

    @pl.when(step == 0)
    def _():
        ids = ids_ref[...]
        experts = [jnp.bitwise_xor(z_ref[0], k) for k in range(n)]
        rank = ranks(ids, experts)
        for k in range(n):
            first, second = chosen(ids, experts[k])
            at = places(rank[k : k + 1, :])
            rows = slice(k * CAP, (k + 1) * CAP)
            firsts[rows, :] = jnp.where(jnp.logical_and(at, first), 1.0, 0.0)
            seconds[rows, :] = jnp.where(jnp.logical_and(at, second), 1.0, 0.0)
        sums[...] = jnp.zeros_like(sums)

    for k in range(n):
        partner = jnp.bitwise_xor(z_ref[0], k)
        out_rows[k * CAP : (k + 1) * CAP, :] = out_back_refs[k][...]
        in_rows[k * CAP : (k + 1) * CAP, :] = in_back_ref[partner]
    prob = jnp.concatenate([prob_ref[...], jnp.zeros((6, tok_count), F32)], axis=0).T
    grad = grad_ref[...].astype(F32)
    one, two = firsts[...].astype(BF), seconds[...].astype(BF)
    total = 0.0
    part = []
    for choice, at in enumerate((one, two)):
        out = mm_rows(at, out_rows[...])
        total = total + prob[:, choice : choice + 1] * out
        part.append(jnp.sum(grad * out, axis=1, keepdims=True))
    out_ref[...] = total.astype(BF)
    in_ref[...] = mm_rows(one + two, in_rows[...]).astype(BF)
    sums[...] += jnp.concatenate(part + [jnp.zeros((tok_count, 6), F32)], axis=1)

    @pl.when(step == pl.num_programs(0) - 1)
    def _():
        prob_grad_ref[...] = sums[...].T[0:2, :]


def combine(z, ids_t, prob_t, out_grad, back_out, back_in):
    n = len(back_out)
    tok_count, width = out_grad.shape
    tile = 512
    by_tile = pl.BlockSpec((tok_count, tile), lambda j: (0, j))
    rows = n * CAP
    return pl.pallas_call(
        functools.partial(combine_kernel, n),
        grid=(width // tile,),
        out_shape=[shape_of((tok_count, width))] * 2 + [shape_of((2, tok_count), F32)],
        in_specs=[in_smem(), whole(ids_t.shape), whole(prob_t.shape), by_tile]
        + [pl.BlockSpec((CAP, tile), lambda j: (0, j))] * n
        + [pl.BlockSpec((n, CAP, tile), lambda j: (0, 0, j))],
        out_specs=[by_tile, by_tile, whole((2, tok_count))],
        scratch_shapes=[pltpu.VMEM((rows, tile), BF)] * 2
        + [pltpu.VMEM((tok_count, 8), F32)]
        + [pltpu.VMEM((rows, tok_count), F32)] * 2,
        compiler_params=params(),
        cost_estimate=cost(6 * rows * tok_count * width, 4 * width * (rows + 2 * tok_count)),
        name="combine",
    )(z, ids_t, prob_t, out_grad, *back_out, back_in)


def exchange(values):
    n = len(values)
    moved = list(values)
    for k in range(n - 1, 0, -1):
        moved[k] = lax.ppermute(values[k], "expert", [(i, i ^ k) for i in range(n)])
    return moved


def local(tokens, expert_ids, gate_probs, w_gate, w_up, w_down, out_grad):
    n = lax.axis_size("expert")
    parts = lax.axis_size("dp")
    z = lax.axis_index("expert").astype(jnp.int32).reshape(1)
    ids_t, prob_t = expert_ids.T, gate_probs.T
    sent = pick_rows(n, z, ids_t, prob_t, tokens, out_grad)
    xs, gs = exchange(sent[:n]), exchange(sent[n:])
    made = forward(xs, w_gate, w_up, w_down)
    slope, act, hidden = made[:3]
    back_out = exchange(made[3:])
    if parts == 8:
        me = lax.axis_index("dp").astype(jnp.int32)
        flips = [(r >> 2 & 1) * CORE | (r & 1) * ALONG_X | (r >> 1 & 1) * ALONG_Y for r in range(8)]
        owners = jnp.stack([me ^ f for f in flips])
        keep_t, send_t, w_near = turn(parts, owners, xs, hidden, w_down)
        grad, g_rows = hidden_grad(gs, w_near, slope, act, [])
        din = input_grad(z, n, grad, w_gate, w_up)
        x_send, x_keep, y_send, y_keep = outer(
            keep_t, swap(send_t, CORE), grad, swap(grad, CORE), g_rows, swap(g_rows, CORE), []
        )
        din = hold(din, back_out[1:])
        back_in = lax.all_to_all(din, "expert", split_axis=0, concat_axis=0, tiled=True)
        x_next, x_mine, y_next, y_mine = fold_two(
            x_keep, swap(x_send, ALONG_X), y_keep, swap(y_send, ALONG_Y), [din]
        )
        layer_out, token_grad, prob_grad_t = combine(z, ids_t, prob_t, out_grad, back_out, back_in)
        shapes = [(1, d // parts, w) for d, w in (w_gate.shape[1:], w_up.shape[1:], w_down.shape[1:])]
        sum_gate, sum_up, sum_down = fold_last(
            x_mine, swap(x_next, ALONG_Y), y_mine, swap(y_next, ALONG_X), shapes, [token_grad]
        )
    else:
        grad, d_rows = hidden_grad(gs, w_down, slope, act, [])
        din = input_grad(z, n, grad, w_gate, w_up)
        back_in = lax.all_to_all(din, "expert", split_axis=0, concat_axis=0, tiled=True)
        layer_out, token_grad, prob_grad_t = combine(z, ids_t, prob_t, out_grad, back_out, back_in)
        x_rows, count = jnp.concatenate(xs, 0), n * CAP
        sum_gate, sum_up, sum_down = (
            lax.psum_scatter(mm_rows(a, b).astype(BF), "dp", scatter_dimension=0, tiled=True)[None]
            for a, b in ((x_rows, grad[:count]), (x_rows, grad[count:]), (hidden, d_rows))
        )
    return layer_out, prob_grad_t.T, token_grad, sum_gate, sum_up, sum_down


def solution(mesh):
    rows = P(("dp", "expert"), None)
    weights = P("expert", None, None)
    summed = P("expert", "dp", None)
    return jax.shard_map(
        local,
        mesh=mesh,
        in_specs=(rows, rows, rows, weights, weights, weights, rows),
        out_specs=(rows, rows, rows, summed, summed, summed),
        check_vma=False,
    )
```

```python
import functools
import jax
import jax.numpy as jnp
from jax import lax
from jax.experimental import pallas as pl
from jax.experimental.pallas import tpu as pltpu
from jax.sharding import PartitionSpec as P

CAP = 64
BF = jnp.bfloat16
F32 = jnp.float32
MIB = 1 << 20


def mm(left, right):
    return jnp.dot(left, right, preferred_element_type=F32)


def mm_rows(left, right):
    return lax.dot_general(left, right, (((0,), (0,)), ((), ())), preferred_element_type=F32)


def mm_cols(left, right):
    return lax.dot_general(left, right, (((1,), (1,)), ((), ())), preferred_element_type=F32)


def shape_of(shape, dtype=BF):
    return jax.ShapeDtypeStruct(tuple(shape), dtype)


def whole(shape):
    return pl.BlockSpec(tuple(shape), lambda *_: (0,) * len(shape))


def in_smem():
    return pl.BlockSpec(memory_space=pltpu.SMEM)


def params(limit=16):
    return pltpu.CompilerParams(vmem_limit_bytes=limit * MIB)


def call(kernel, after, in_specs, args, **kwargs):
    count = len(args)

    def body(*refs):
        kernel(*refs[:count], *refs[count + len(after) :])

    specs = list(in_specs) + [pl.BlockSpec(memory_space=pl.ANY)] * len(after)
    return pl.pallas_call(body, in_specs=specs, **kwargs)(*args, *after)


def cost(flops, moved):
    return pl.CostEstimate(flops=int(flops), bytes_accessed=int(moved), transcendentals=0)


def chosen(ids, expert):
    first = ids[0:1, :] == expert
    second = ids[1:2, :] == expert
    return first, second


def ranks(ids, experts):
    tok_count = ids.shape[1]
    masks = [jnp.where(jnp.logical_or(*chosen(ids, e)), 1.0, 0.0) for e in experts]
    mask = jnp.concatenate(masks + [jnp.zeros((-len(masks) % 16, tok_count), F32)], axis=0)
    before = lax.broadcasted_iota(jnp.int32, (tok_count, tok_count), 0)
    after = lax.broadcasted_iota(jnp.int32, (tok_count, tok_count), 1)
    upper = jnp.where(before < after, 1.0, 0.0).astype(BF)
    return mm(mask.astype(BF), upper).astype(jnp.int32)


def places(rank_row):
    tok_count = rank_row.shape[1]
    return lax.broadcasted_iota(jnp.int32, (CAP, tok_count), 0) == rank_row


def pick_kernel(n, scaled, z_ref, ids_ref, prob_ref, rows_ref, *outs):
    ids = ids_ref[...]
    prob = prob_ref[...]
    experts = [jnp.bitwise_xor(z_ref[0], k) for k in range(n)]
    rank = ranks(ids, experts)
    for k in range(n - 1, -1, -1):
        first, second = chosen(ids, experts[k])
        at = places(rank[k : k + 1, :])
        here = jnp.logical_and(at, jnp.logical_or(first, second))
        picked = mm(jnp.where(here, 1.0, 0.0).astype(BF), rows_ref[...])
        if scaled:
            weight = jnp.where(first, prob[0:1, :], prob[1:2, :])
            picked = jnp.sum(jnp.where(here, weight, 0.0), axis=1, keepdims=True) * picked
        outs[k][...] = picked.astype(BF)


def pick_rows(n, scaled, z, ids_t, prob_t, rows):
    tok_count, width = rows.shape
    return pl.pallas_call(
        functools.partial(pick_kernel, n, scaled),
        out_shape=[shape_of((CAP, width))] * n,
        in_specs=[in_smem(), whole(ids_t.shape), whole(prob_t.shape), whole(rows.shape)],
        out_specs=[whole((CAP, width))] * n,
        grid=(1,),
        compiler_params=params(60),
        cost_estimate=cost(2 * n * CAP * tok_count * width, 4 * tok_count * width * 2),
        name="pick_rows",
    )(z, ids_t, prob_t, rows)


def silu_parts(gate):
    sig = jax.nn.sigmoid(gate)
    return gate * sig, sig * (1.0 + gate * (1.0 - sig))


def forward_kernel(n, steps, tile, *refs):
    x_refs = refs[:n]
    weights = refs[n : n + 3]
    slope_ref, act_ref, hid_ref = refs[n + 3 : n + 6]
    out_refs = refs[n + 6 : 2 * n + 6]
    rows, total, wg_buf, wu_buf, wd_buf, sems = refs[2 * n + 6 :]
    step = pl.program_id(0)

    def loads(j):
        at = pl.ds(pl.multiple_of(j * tile, tile), tile)
        wg_ref, wu_ref, wd_ref = weights
        return (
            pltpu.make_async_copy(wg_ref.at[0, :, at], wg_buf.at[j], sems.at[0, j]),
            pltpu.make_async_copy(wu_ref.at[0, :, at], wu_buf.at[j], sems.at[1, j]),
            pltpu.make_async_copy(wd_ref.at[0, at, :], wd_buf.at[j], sems.at[2, j]),
        )

    @pl.when(step == 0)
    def _():
        for j in range(steps):
            for load in loads(j):
                load.start()
        for k in range(n):
            rows[k * CAP : (k + 1) * CAP, :] = x_refs[k][...]

    for load in loads(step):
        load.wait()
    gate = mm(rows[...], wg_buf[step])
    up = mm(rows[...], wu_buf[step])
    act, slope = silu_parts(gate)
    act_ref[...] = act
    slope_ref[...] = up * slope
    hidden = (act * up).astype(BF)
    hid_ref[...] = hidden
    part = mm(hidden, wd_buf[step])

    @pl.when(step == 0)
    def _():
        total[...] = part

    @pl.when(step > 0)
    def _():
        total[...] += part

    @pl.when(step == steps - 1)
    def _():
        for k in range(n):
            out_refs[k][...] = total[k * CAP : (k + 1) * CAP, :].astype(BF)


def weight_specs(width, tile):
    by_col = pl.BlockSpec((1, width, tile), lambda j: (0, 0, j))
    by_row = pl.BlockSpec((1, tile, width), lambda j: (0, j, 0))
    return [by_col, by_col, by_row]


def forward(xs, w_gate, w_up, w_down):
    n = len(xs)
    width, ff = w_gate.shape[1:]
    tile = 256
    steps = ff // tile
    rows = n * CAP
    part = pl.BlockSpec((rows, tile), lambda j: (0, j))
    return pl.pallas_call(
        functools.partial(forward_kernel, n, steps, tile),
        grid=(steps,),
        out_shape=[shape_of((rows, ff), F32)] * 2 + [shape_of((rows, ff))] + [shape_of((CAP, width))] * n,
        in_specs=[whole((CAP, width))] * n + [pl.BlockSpec(memory_space=pltpu.HBM)] * 3,
        out_specs=[part, part, part] + [whole((CAP, width))] * n,
        scratch_shapes=[
            pltpu.VMEM((rows, width), BF),
            pltpu.VMEM((rows, width), F32),
            pltpu.VMEM((steps, width, tile), BF),
            pltpu.VMEM((steps, width, tile), BF),
            pltpu.VMEM((steps, tile, width), BF),
            pltpu.SemaphoreType.DMA((3, steps)),
        ],
        compiler_params=params(50),
        cost_estimate=cost(6 * rows * width * ff, 6 * width * ff + 4 * rows * width + 10 * rows * ff),
        name="forward",
    )(*xs, w_gate, w_up, w_down)


def turn_kernel(n, parts, me_ref, *refs):
    x_refs = refs[:n]
    hid_ref, w_ref, keep_ref, send_ref, copy_ref, rows, turned, sem = refs[n:]
    load = pltpu.make_async_copy(w_ref, copy_ref, sem)
    load.start()
    for k in range(n):
        rows[k * CAP : (k + 1) * CAP, :] = x_refs[k][...]
    turned[...] = hid_ref[...].T
    half = parts // 2
    x_size, h_size = rows.shape[1] // parts, turned.shape[0] // parts
    strip = h_size // 6
    for rel in range(parts):
        out_ref, i = (keep_ref, rel) if rel < half else (send_ref, rel - half)
        at = pl.multiple_of(me_ref[rel] * x_size, x_size)
        out_ref[i * x_size : (i + 1) * x_size, :] = rows[:, pl.ds(at, x_size)].T
        for j in range(6):
            at = pl.multiple_of(me_ref[rel] * h_size + j * strip, strip)
            base = half * x_size + ((j % 3) * 2 * half + 2 * i + j // 3) * strip
            out_ref[base : base + strip, :] = turned[pl.ds(at, strip), :]
    load.wait()


def turn(parts, owners, xs, hidden, w_down):
    n = len(xs)
    width = xs[0].shape[1]
    rows, ff = hidden.shape
    high = (width + ff) // 2
    return pl.pallas_call(
        functools.partial(turn_kernel, n, parts),
        grid=(1,),
        out_shape=[shape_of((high, rows))] * 2 + [shape_of(w_down.shape)],
        in_specs=[in_smem()] + [whole((CAP, width))] * n + [whole(hidden.shape), pl.BlockSpec(memory_space=pltpu.HBM)],
        out_specs=[whole((high, rows))] * 2 + [whole(w_down.shape)],
        scratch_shapes=[pltpu.VMEM((rows, width), BF), pltpu.VMEM((ff, rows), BF), pltpu.SemaphoreType.DMA],
        compiler_params=params(),
        cost_estimate=cost(2 * rows * width, 6 * rows * (width + ff)),
        name="turn",
    )(owners, *xs, hidden, w_down)


def outer_kernel(keep_ref, recv_ref, own_ref, other_ref, own_g_ref, other_g_ref, x_send, x_keep, y_send, y_keep):
    step = pl.program_id(0)
    half, high = 4, own_ref.shape[0] // 2
    size = 256
    strip = 16
    for block in range(half):
        at = slice(block * size, (block + 1) * size)
        across, along = block & 1, block >> 1
        gate = mm(keep_ref[at, :], own_ref[:high, :]) + mm(recv_ref[at, :], other_ref[:high, :])
        (x_send if across else x_keep)[along, :size, :] = gate.astype(BF)
        up = mm(keep_ref[at, :], own_ref[high:, :]) + mm(recv_ref[at, :], other_ref[high:, :])
        (y_send if along else y_keep)[across, :size, :] = up.astype(BF)
    at = pl.ds(pl.multiple_of(half * size + step * 2 * half * strip, strip), 2 * half * strip)
    down = mm(keep_ref[at, :], own_g_ref[...]) + mm(recv_ref[at, :], other_g_ref[...])
    down = down.astype(BF)
    tile = x_send.shape[2]
    for block in range(half):
        across, along = block & 1, block >> 1
        for part, (out_ref, i) in enumerate(
            ((x_send if across else x_keep, along), (y_send if along else y_keep, across))
        ):
            base = (2 * block + part) * strip
            for c in range(down.shape[1] // tile):
                out_ref[i, size + c * strip : size + (c + 1) * strip, :] = down[
                    base : base + strip, c * tile : (c + 1) * tile
                ]


def outer(keep, recv, own, other, own_g, other_g, after):
    rows, width = own_g.shape
    ff = own.shape[1]
    tile = 256
    col = pl.BlockSpec((2 * rows, tile), lambda j: (0, j))
    high = 256 + 16 * (width // tile)
    part = pl.BlockSpec((2, high, tile), lambda j: (0, 0, j))
    return call(
        outer_kernel,
        after,
        grid=(ff // tile,),
        out_shape=[shape_of((2, high, ff))] * 4,
        in_specs=[whole(keep.shape)] * 2 + [col] * 2 + [whole(own_g.shape)] * 2,
        args=(keep, recv, own, other, own_g, other_g),
        out_specs=[part] * 4,
        compiler_params=params(),
        cost_estimate=cost(6 * rows * width * ff, 4 * keep.size + 16 * high * ff),
        name="outer",
    )


def hidden_grad_kernel(n, *refs):
    g_refs = refs[:n]
    wd_ref, slope_ref, act_ref, grad_ref, rows = refs[n:]

    @pl.when(pl.program_id(0) == 0)
    def _():
        for k in range(n):
            rows[k * CAP : (k + 1) * CAP, :] = g_refs[k][...]

    grad = mm_cols(rows[...], wd_ref[0])
    grad_ref[: n * CAP, :] = (grad * slope_ref[...]).astype(BF)
    grad_ref[n * CAP :, :] = (grad * act_ref[...]).astype(BF)


def hidden_grad(gs, w_down, slope, act, after):
    n = len(gs)
    ff, width = w_down.shape[1:]
    rows = n * CAP
    tile = 256
    part = pl.BlockSpec((rows, tile), lambda j: (0, j))
    return call(
        functools.partial(hidden_grad_kernel, n),
        after,
        grid=(ff // tile,),
        out_shape=[shape_of((2 * rows, ff)), shape_of((rows, width))],
        in_specs=[whole((CAP, width))] * n + [weight_specs(width, tile)[2], part, part],
        args=(*gs, w_down, slope, act),
        out_specs=[pl.BlockSpec((2 * rows, tile), lambda j: (0, j)), whole((rows, width))],
        compiler_params=params(),
        cost_estimate=cost(2 * rows * width * ff, 2 * width * ff + 4 * rows * width + 12 * rows * ff),
        name="hidden_grad",
    )


def input_grad_kernel(n, steps, tile, grad_ref, wg_ref, wu_ref, *refs):
    out_refs = refs[:n]
    wg_buf, wu_buf, sems = refs[n:]
    step = pl.program_id(0)

    def loads(j):
        at = pl.ds(pl.multiple_of(j * tile, tile), tile)
        return (
            pltpu.make_async_copy(wg_ref.at[0, at, :], wg_buf.at[j], sems.at[0, j]),
            pltpu.make_async_copy(wu_ref.at[0, at, :], wu_buf.at[j], sems.at[1, j]),
        )

    @pl.when(step == 0)
    def _():
        for j in range(steps):
            for load in loads(j):
                load.start()

    for load in loads(step):
        load.wait()
    rows = n * CAP
    total = mm_cols(grad_ref[:rows, :], wg_buf[step]) + mm_cols(grad_ref[rows:, :], wu_buf[step])
    for k in range(n):
        out_refs[k][...] = total[k * CAP : (k + 1) * CAP, :].astype(BF)


def input_grad(n, grad, w_gate, w_up, after):
    rows, ff = n * CAP, grad.shape[1]
    width = w_gate.shape[1]
    tile = 512
    steps = width // tile
    return call(
        functools.partial(input_grad_kernel, n, steps, tile),
        after,
        grid=(steps,),
        out_shape=[shape_of((CAP, width))] * n,
        in_specs=[whole((2 * rows, ff))] + [pl.BlockSpec(memory_space=pltpu.HBM)] * 2,
        args=(grad, w_gate, w_up),
        out_specs=[pl.BlockSpec((CAP, tile), lambda j: (0, j))] * n,
        scratch_shapes=[pltpu.VMEM((steps, tile, ff), BF)] * 2 + [pltpu.SemaphoreType.DMA((2, steps))],
        compiler_params=params(),
        cost_estimate=cost(4 * rows * width * ff, 4 * width * ff + 2 * rows * (width + 2 * ff)),
        name="input_grad",
    )


def hold_kernel(*_):
    pass


def hold(values, after):
    anywhere = pl.BlockSpec(memory_space=pl.ANY)
    return call(
        hold_kernel,
        after,
        [anywhere] * len(values),
        values,
        out_shape=[shape_of(v.shape) for v in values],
        out_specs=[anywhere] * len(values),
        input_output_aliases={i: i for i in range(len(values))},
        cost_estimate=cost(10**11, 0),
        name="hold",
    )


def fold_two_kernel(x_keep, x_recv, y_keep, y_recv, x_next, x_mine, y_next, y_mine):
    for keep, recv, away, mine in ((x_keep, x_recv, x_next, x_mine), (y_keep, y_recv, y_next, y_mine)):
        away[...] = (keep[1].astype(F32) + recv[1].astype(F32)).astype(BF)
        mine[...] = (keep[0].astype(F32) + recv[0].astype(F32)).astype(BF)


def fold_two(x_keep, x_recv, y_keep, y_recv, after):
    _, high, width = x_keep.shape
    return call(
        fold_two_kernel,
        after,
        grid=(1,),
        out_shape=[shape_of((high, width))] * 4,
        in_specs=[whole((2, high, width))] * 4,
        args=(x_keep, x_recv, y_keep, y_recv),
        out_specs=[whole((high, width))] * 4,
        compiler_params=params(),
        cost_estimate=cost(4 * high * width, 24 * high * width),
        name="fold_two",
    )


def fold_last_kernel(x_mine, x_recv, y_mine, y_recv, gate_ref, up_ref, down_ref):
    size, strip = gate_ref.shape[1], 16
    tile = 256
    for i, (mine, recv, out_ref) in enumerate(((x_mine, x_recv, gate_ref), (y_mine, y_recv, up_ref))):
        total = (mine[...].astype(F32) + recv[...].astype(F32)).astype(BF)
        out_ref[0] = total[:size]
        for c in range(down_ref.shape[2] // tile):
            for j in range(3):
                down_ref[0, (3 * i + j) * strip : (3 * i + j + 1) * strip, c * tile : (c + 1) * tile] = total[
                    size + c * strip : size + (c + 1) * strip, j * tile : (j + 1) * tile
                ]


def fold_last(x_mine, x_recv, y_mine, y_recv, shapes, after):
    high, width = x_mine.shape
    return call(
        fold_last_kernel,
        after,
        grid=(1,),
        out_shape=[shape_of(s) for s in shapes],
        in_specs=[whole((high, width))] * 4,
        args=(x_mine, x_recv, y_mine, y_recv),
        out_specs=[whole(s) for s in shapes],
        compiler_params=params(),
        cost_estimate=cost(2 * high * width, 12 * high * width),
        name="fold_last",
    )


CORE, ALONG_X, ALONG_Y = 1, 2, 4


def swap(value, bit, count=8):
    return lax.ppermute(value, "dp", [(i, i ^ bit) for i in range(count)])


def combine_kernel(n, z_ref, ids_ref, prob_ref, grad_ref, *refs):
    out_back_refs, in_back_refs = refs[:n], refs[n : 2 * n]
    out_ref, in_ref, prob_grad_ref, out_rows, in_rows, sums, firsts, seconds = refs[2 * n :]
    tok_count = ids_ref.shape[1]
    step = pl.program_id(0)

    @pl.when(step == 0)
    def _():
        ids = ids_ref[...]
        experts = [jnp.bitwise_xor(z_ref[0], k) for k in range(n)]
        rank = ranks(ids, experts)
        for k in range(n):
            first, second = chosen(ids, experts[k])
            at = places(rank[k : k + 1, :])
            rows = slice(k * CAP, (k + 1) * CAP)
            firsts[rows, :] = jnp.where(jnp.logical_and(at, first), 1.0, 0.0)
            seconds[rows, :] = jnp.where(jnp.logical_and(at, second), 1.0, 0.0)
        sums[...] = jnp.zeros_like(sums)

    for k in range(n):
        out_rows[k * CAP : (k + 1) * CAP, :] = out_back_refs[k][...]
        in_rows[k * CAP : (k + 1) * CAP, :] = in_back_refs[k][...]
    prob = jnp.concatenate([prob_ref[...], jnp.zeros((6, tok_count), F32)], axis=0).T
    grad = grad_ref[...].astype(F32)
    one, two = firsts[...].astype(BF), seconds[...].astype(BF)
    total = 0.0
    part = []
    for choice, at in enumerate((one, two)):
        out = mm_rows(at, out_rows[...])
        total = total + prob[:, choice : choice + 1] * out
        part.append(jnp.sum(grad * out, axis=1, keepdims=True))
    out_ref[...] = total.astype(BF)
    in_ref[...] = mm_rows(one + two, in_rows[...]).astype(BF)
    sums[...] += jnp.concatenate(part + [jnp.zeros((tok_count, 6), F32)], axis=1)

    @pl.when(step == pl.num_programs(0) - 1)
    def _():
        prob_grad_ref[...] = sums[...].T[0:2, :]


def combine(z, ids_t, prob_t, out_grad, back_out, back_in):
    n = len(back_out)
    tok_count, width = out_grad.shape
    tile = 512
    by_tile = pl.BlockSpec((tok_count, tile), lambda j: (0, j))
    rows = n * CAP
    return pl.pallas_call(
        functools.partial(combine_kernel, n),
        grid=(width // tile,),
        out_shape=[shape_of((tok_count, width))] * 2 + [shape_of((2, tok_count), F32)],
        in_specs=[in_smem(), whole(ids_t.shape), whole(prob_t.shape), by_tile]
        + [pl.BlockSpec((CAP, tile), lambda j: (0, j))] * (2 * n),
        out_specs=[by_tile, by_tile, whole((2, tok_count))],
        scratch_shapes=[pltpu.VMEM((rows, tile), BF)] * 2
        + [pltpu.VMEM((tok_count, 8), F32)]
        + [pltpu.VMEM((rows, tok_count), F32)] * 2,
        compiler_params=params(),
        cost_estimate=cost(600 * rows * tok_count * width, 4 * width * (rows + 2 * tok_count)),
        name="combine",
    )(z, ids_t, prob_t, out_grad, *back_out, *back_in)


def exchange(values):
    n = len(values)
    moved = list(values)
    for k in range(n - 1, 0, -1):
        moved[k] = lax.ppermute(values[k], "expert", [(i, i ^ k) for i in range(n)])
    return moved


def local(tokens, expert_ids, gate_probs, w_gate, w_up, w_down, out_grad):
    n = lax.axis_size("expert")
    parts = lax.axis_size("dp")
    z = lax.axis_index("expert").astype(jnp.int32).reshape(1)
    ids_t, prob_t = expert_ids.T, gate_probs.T
    xs = exchange(pick_rows(n, False, z, ids_t, prob_t, tokens))
    gs = exchange(pick_rows(n, True, z, ids_t, prob_t, out_grad))
    made = forward(xs, w_gate, w_up, w_down)
    slope, act, hidden = made[:3]
    back_out = exchange(made[3:])
    if parts == 8:
        me = lax.axis_index("dp").astype(jnp.int32)
        flips = [(r >> 2 & 1) * CORE | (r & 1) * ALONG_X | (r >> 1 & 1) * ALONG_Y for r in range(8)]
        owners = jnp.stack([me ^ f for f in flips])
        keep_t, send_t, w_near = turn(parts, owners, xs, hidden, w_down)
        grad, g_rows = hidden_grad(gs, w_near, slope, act, [])
        x_send, x_keep, y_send, y_keep = outer(
            keep_t, swap(send_t, CORE), grad, swap(grad, CORE), g_rows, swap(g_rows, CORE), []
        )
        din = input_grad(n, grad, w_gate, w_up, [x_send])
        back_in = exchange(din[:1] + hold(din[1:], back_out[1:]))
        x_next, x_mine, y_next, y_mine = fold_two(
            x_keep, swap(x_send, ALONG_X), y_keep, swap(y_send, ALONG_Y), din[:1]
        )
        layer_out, token_grad, prob_grad_t = combine(z, ids_t, prob_t, out_grad, back_out, back_in)
        shapes = [(1, d // parts, w) for d, w in (w_gate.shape[1:], w_up.shape[1:], w_down.shape[1:])]
        sum_gate, sum_up, sum_down = fold_last(
            x_mine, swap(x_next, ALONG_Y), y_mine, swap(y_next, ALONG_X), shapes, [token_grad]
        )
    else:
        grad, d_rows = hidden_grad(gs, w_down, slope, act, [])
        din = input_grad(n, grad, w_gate, w_up, [])
        back_in = exchange(din)
        layer_out, token_grad, prob_grad_t = combine(z, ids_t, prob_t, out_grad, back_out, back_in)
        x_rows, count = jnp.concatenate(xs, 0), n * CAP
        sum_gate, sum_up, sum_down = (
            lax.psum_scatter(mm_rows(a, b).astype(BF), "dp", scatter_dimension=0, tiled=True)[None]
            for a, b in ((x_rows, grad[:count]), (x_rows, grad[count:]), (hidden, d_rows))
        )
    return layer_out, prob_grad_t.T, token_grad, sum_gate, sum_up, sum_down


def solution(mesh):
    rows = P(("dp", "expert"), None)
    weights = P("expert", None, None)
    summed = P("expert", "dp", None)
    return jax.shard_map(
        local,
        mesh=mesh,
        in_specs=(rows, rows, rows, weights, weights, weights, rows),
        out_specs=(rows, rows, rows, summed, summed, summed),
        check_vma=False,
    )
```

```python
import functools
import jax
import jax.numpy as jnp
from jax import lax
from jax.experimental import pallas as pl
from jax.experimental.pallas import tpu as pltpu
from jax.sharding import PartitionSpec as P

CAP = 64
BF = jnp.bfloat16
F32 = jnp.float32
MIB = 1 << 20


def mm(left, right):
    return jnp.dot(left, right, preferred_element_type=F32)


def mm_rows(left, right):
    return lax.dot_general(left, right, (((0,), (0,)), ((), ())), preferred_element_type=F32)


def mm_cols(left, right):
    return lax.dot_general(left, right, (((1,), (1,)), ((), ())), preferred_element_type=F32)


def shape_of(shape, dtype=BF):
    return jax.ShapeDtypeStruct(tuple(shape), dtype)


def whole(shape):
    return pl.BlockSpec(tuple(shape), lambda *_: (0,) * len(shape))


def in_smem():
    return pl.BlockSpec(memory_space=pltpu.SMEM)


def params(limit=16):
    return pltpu.CompilerParams(vmem_limit_bytes=limit * MIB)


def call(kernel, after, in_specs, args, **kwargs):
    count = len(args)

    def body(*refs):
        kernel(*refs[:count], *refs[count + len(after) :])

    specs = list(in_specs) + [pl.BlockSpec(memory_space=pl.ANY)] * len(after)
    return pl.pallas_call(body, in_specs=specs, **kwargs)(*args, *after)


def cost(flops, moved):
    return pl.CostEstimate(flops=int(flops), bytes_accessed=int(moved), transcendentals=0)


def chosen(ids, expert):
    first = ids[0:1, :] == expert
    second = ids[1:2, :] == expert
    return first, second


def ranks(ids, experts):
    tok_count = ids.shape[1]
    masks = [jnp.where(jnp.logical_or(*chosen(ids, e)), 1.0, 0.0) for e in experts]
    mask = jnp.concatenate(masks + [jnp.zeros((-len(masks) % 16, tok_count), F32)], axis=0)
    before = lax.broadcasted_iota(jnp.int32, (tok_count, tok_count), 0)
    after = lax.broadcasted_iota(jnp.int32, (tok_count, tok_count), 1)
    upper = jnp.where(before < after, 1.0, 0.0).astype(BF)
    return mm(mask.astype(BF), upper).astype(jnp.int32)


def places(rank_row):
    tok_count = rank_row.shape[1]
    return lax.broadcasted_iota(jnp.int32, (CAP, tok_count), 0) == rank_row


def pick_kernel(n, scaled, z_ref, ids_ref, prob_ref, rows_ref, *outs):
    ids = ids_ref[...]
    prob = prob_ref[...]
    experts = [jnp.bitwise_xor(z_ref[0], k) for k in range(n)]
    rank = ranks(ids, experts)
    for k in range(n - 1, -1, -1):
        first, second = chosen(ids, experts[k])
        at = places(rank[k : k + 1, :])
        here = jnp.logical_and(at, jnp.logical_or(first, second))
        picked = mm(jnp.where(here, 1.0, 0.0).astype(BF), rows_ref[...])
        if scaled:
            weight = jnp.where(first, prob[0:1, :], prob[1:2, :])
            picked = jnp.sum(jnp.where(here, weight, 0.0), axis=1, keepdims=True) * picked
        outs[k][...] = picked.astype(BF)


def pick_rows(n, scaled, z, ids_t, prob_t, rows):
    tok_count, width = rows.shape
    return pl.pallas_call(
        functools.partial(pick_kernel, n, scaled),
        out_shape=[shape_of((CAP, width))] * n,
        in_specs=[in_smem(), whole(ids_t.shape), whole(prob_t.shape), whole(rows.shape)],
        out_specs=[whole((CAP, width))] * n,
        grid=(1,),
        compiler_params=params(60),
        cost_estimate=cost(2 * n * CAP * tok_count * width, 4 * tok_count * width * 2),
        name="pick_rows",
    )(z, ids_t, prob_t, rows)


def silu_parts(gate):
    sig = jax.nn.sigmoid(gate)
    return gate * sig, sig * (1.0 + gate * (1.0 - sig))


def forward_kernel(n, steps, tile, *refs):
    x_refs = refs[:n]
    weights = refs[n : n + 3]
    slope_ref, act_ref, hid_ref = refs[n + 3 : n + 6]
    out_refs = refs[n + 6 : 2 * n + 6]
    rows, total, wg_buf, wu_buf, wd_buf, sems = refs[2 * n + 6 :]
    step = pl.program_id(0)

    def loads(j):
        at = pl.ds(pl.multiple_of(j * tile, tile), tile)
        wg_ref, wu_ref, wd_ref = weights
        return (
            pltpu.make_async_copy(wg_ref.at[0, :, at], wg_buf.at[j], sems.at[0, j]),
            pltpu.make_async_copy(wu_ref.at[0, :, at], wu_buf.at[j], sems.at[1, j]),
            pltpu.make_async_copy(wd_ref.at[0, at, :], wd_buf.at[j], sems.at[2, j]),
        )

    @pl.when(step == 0)
    def _():
        for j in range(steps):
            for load in loads(j):
                load.start()
        for k in range(n):
            rows[k * CAP : (k + 1) * CAP, :] = x_refs[k][...]

    for load in loads(step):
        load.wait()
    gate = mm(rows[...], wg_buf[step])
    up = mm(rows[...], wu_buf[step])
    act, slope = silu_parts(gate)
    act_ref[...] = act
    slope_ref[...] = up * slope
    hidden = (act * up).astype(BF)
    hid_ref[...] = hidden
    part = mm(hidden, wd_buf[step])

    @pl.when(step == 0)
    def _():
        total[...] = part

    @pl.when(step > 0)
    def _():
        total[...] += part

    @pl.when(step == steps - 1)
    def _():
        for k in range(n):
            out_refs[k][...] = total[k * CAP : (k + 1) * CAP, :].astype(BF)


def weight_specs(width, tile):
    by_col = pl.BlockSpec((1, width, tile), lambda j: (0, 0, j))
    by_row = pl.BlockSpec((1, tile, width), lambda j: (0, j, 0))
    return [by_col, by_col, by_row]


def forward(xs, w_gate, w_up, w_down):
    n = len(xs)
    width, ff = w_gate.shape[1:]
    tile = 256
    steps = ff // tile
    rows = n * CAP
    part = pl.BlockSpec((rows, tile), lambda j: (0, j))
    return pl.pallas_call(
        functools.partial(forward_kernel, n, steps, tile),
        grid=(steps,),
        out_shape=[shape_of((rows, ff), F32)] * 2 + [shape_of((rows, ff))] + [shape_of((CAP, width))] * n,
        in_specs=[whole((CAP, width))] * n + [pl.BlockSpec(memory_space=pltpu.HBM)] * 3,
        out_specs=[part, part, part] + [whole((CAP, width))] * n,
        scratch_shapes=[
            pltpu.VMEM((rows, width), BF),
            pltpu.VMEM((rows, width), F32),
            pltpu.VMEM((steps, width, tile), BF),
            pltpu.VMEM((steps, width, tile), BF),
            pltpu.VMEM((steps, tile, width), BF),
            pltpu.SemaphoreType.DMA((3, steps)),
        ],
        compiler_params=params(50),
        cost_estimate=cost(6 * rows * width * ff, 6 * width * ff + 4 * rows * width + 10 * rows * ff),
        name="forward",
    )(*xs, w_gate, w_up, w_down)


def turn_kernel(n, parts, me_ref, *refs):
    x_refs = refs[:n]
    hid_ref, w_ref, keep_ref, send_ref, copy_ref, rows, turned, sem = refs[n:]
    load = pltpu.make_async_copy(w_ref, copy_ref, sem)
    load.start()
    for k in range(n):
        rows[k * CAP : (k + 1) * CAP, :] = x_refs[k][...]
    turned[...] = hid_ref[...].T
    half = parts // 2
    x_size, h_size = rows.shape[1] // parts, turned.shape[0] // parts
    strip = h_size // 6
    for rel in range(parts):
        out_ref, i = (keep_ref, rel) if rel < half else (send_ref, rel - half)
        at = pl.multiple_of(me_ref[rel] * x_size, x_size)
        out_ref[i * x_size : (i + 1) * x_size, :] = rows[:, pl.ds(at, x_size)].T
        for j in range(6):
            at = pl.multiple_of(me_ref[rel] * h_size + j * strip, strip)
            leaves, spot = (i & 1, i >> 1) if j < 3 else (i >> 1, 2 + (i & 1))
            base = half * x_size + ((j % 3) * 2 * half + leaves * half + spot) * strip
            out_ref[base : base + strip, :] = turned[pl.ds(at, strip), :]
    load.wait()


def turn(parts, owners, xs, hidden, w_down):
    n = len(xs)
    width = xs[0].shape[1]
    rows, ff = hidden.shape
    high = (width + ff) // 2
    return pl.pallas_call(
        functools.partial(turn_kernel, n, parts),
        grid=(1,),
        out_shape=[shape_of((high, rows))] * 2 + [shape_of(w_down.shape)],
        in_specs=[in_smem()] + [whole((CAP, width))] * n + [whole(hidden.shape), pl.BlockSpec(memory_space=pltpu.HBM)],
        out_specs=[whole((high, rows))] * 2 + [whole(w_down.shape)],
        scratch_shapes=[pltpu.VMEM((rows, width), BF), pltpu.VMEM((ff, rows), BF), pltpu.SemaphoreType.DMA],
        compiler_params=params(),
        cost_estimate=cost(2 * rows * width, 6 * rows * (width + ff)),
        name="turn",
    )(owners, *xs, hidden, w_down)


def outer_kernel(group, keep_ref, recv_ref, own_ref, other_ref, own_g_ref, x_ref, y_ref):
    step = pl.program_id(0)
    half, high = 4, own_ref.shape[0] // 2
    size = 256
    strip = 16
    for i in range(2):
        block = 2 * i + group
        at = slice(block * size, (block + 1) * size)
        gate = mm(keep_ref[at, :], own_ref[:high, :]) + mm(recv_ref[at, :], other_ref[:high, :])
        x_ref[i, :size, :] = gate.astype(BF)
        block = 2 * group + i
        at = slice(block * size, (block + 1) * size)
        up = mm(keep_ref[at, :], own_ref[high:, :]) + mm(recv_ref[at, :], other_ref[high:, :])
        y_ref[i, :size, :] = up.astype(BF)
    at = pl.ds(pl.multiple_of(half * size + (2 * step + group) * half * strip, strip), half * strip)
    tile = x_ref.shape[2]
    turned = keep_ref.shape[0]
    for c in range(own_g_ref.shape[1] // tile):
        theirs = recv_ref[turned + c * high : turned + (c + 1) * high, :]
        down = mm(keep_ref[at, :], own_g_ref[:, c * tile : (c + 1) * tile]) + mm(recv_ref[at, :], theirs)
        down = down.astype(BF)
        for spot in range(half):
            out_ref = x_ref if spot < 2 else y_ref
            out_ref[spot % 2, size + c * strip : size + (c + 1) * strip, :] = down[spot * strip : (spot + 1) * strip]


def outer(group, keep, recv, own, other, own_g, after):
    rows, width = own_g.shape
    ff = own.shape[1]
    tile = 256
    col = pl.BlockSpec((2 * rows, tile), lambda j: (0, j))
    high = 256 + 16 * (width // tile)
    part = pl.BlockSpec((2, high, tile), lambda j: (0, 0, j))
    return call(
        functools.partial(outer_kernel, group),
        after,
        grid=(ff // tile,),
        out_shape=[shape_of((2, high, ff))] * 2,
        in_specs=[whole(keep.shape), whole(recv.shape)] + [col] * 2 + [whole(own_g.shape)],
        args=(keep, recv, own, other, own_g),
        out_specs=[part] * 2,
        compiler_params=params(),
        cost_estimate=cost(3 * rows * width * ff, 4 * keep.size + 8 * high * ff),
        name="outer",
    )


def hidden_grad_kernel(n, *refs):
    g_refs = refs[:n]
    wd_ref, slope_ref, act_ref, turned_ref, grad_ref, rows, pack_ref = refs[n:]

    @pl.when(pl.program_id(0) == 0)
    def _():
        for k in range(n):
            rows[k * CAP : (k + 1) * CAP, :] = g_refs[k][...]
        high = turned_ref.shape[0]
        pack_ref[:high, :] = turned_ref[...]
        tile = pack_ref.shape[1]
        for c in range(rows.shape[1] // tile):
            at = high + c * n * CAP
            pack_ref[at : at + n * CAP, :] = rows[:, c * tile : (c + 1) * tile]

    grad = mm_cols(rows[...], wd_ref[0])
    grad_ref[: n * CAP, :] = (grad * slope_ref[...]).astype(BF)
    grad_ref[n * CAP :, :] = (grad * act_ref[...]).astype(BF)


def hidden_grad(gs, w_down, slope, act, turned):
    n = len(gs)
    ff, width = w_down.shape[1:]
    rows = n * CAP
    tile = 256
    part = pl.BlockSpec((rows, tile), lambda j: (0, j))
    tall = (turned.shape[0] + rows * (width // 256), 256)
    return pl.pallas_call(
        functools.partial(hidden_grad_kernel, n),
        grid=(ff // tile,),
        out_shape=[shape_of((2 * rows, ff)), shape_of((rows, width)), shape_of(tall)],
        in_specs=[whole((CAP, width))] * n + [weight_specs(width, tile)[2], part, part, whole(turned.shape)],
        out_specs=[pl.BlockSpec((2 * rows, tile), lambda j: (0, j)), whole((rows, width)), whole(tall)],
        compiler_params=params(),
        cost_estimate=cost(2 * rows * width * ff, 2 * width * ff + 4 * rows * width + 12 * rows * ff),
        name="hidden_grad",
    )(*gs, w_down, slope, act, turned)


def input_grad_kernel(n, steps, tile, grad_ref, wg_ref, wu_ref, *refs):
    out_refs = refs[:n]
    wg_buf, wu_buf, sems = refs[n:]
    step = pl.program_id(0)

    def loads(j):
        at = pl.ds(pl.multiple_of(j * tile, tile), tile)
        return (
            pltpu.make_async_copy(wg_ref.at[0, at, :], wg_buf.at[j], sems.at[0, j]),
            pltpu.make_async_copy(wu_ref.at[0, at, :], wu_buf.at[j], sems.at[1, j]),
        )

    @pl.when(step == 0)
    def _():
        for j in range(steps):
            for load in loads(j):
                load.start()

    for load in loads(step):
        load.wait()
    rows = n * CAP
    total = mm_cols(grad_ref[:rows, :], wg_buf[step]) + mm_cols(grad_ref[rows:, :], wu_buf[step])
    for k in range(n):
        out_refs[k][...] = total[k * CAP : (k + 1) * CAP, :].astype(BF)


def input_grad(n, grad, w_gate, w_up, after):
    rows, ff = n * CAP, grad.shape[1]
    width = w_gate.shape[1]
    tile = 512
    steps = width // tile
    return call(
        functools.partial(input_grad_kernel, n, steps, tile),
        after,
        grid=(steps,),
        out_shape=[shape_of((CAP, width))] * n,
        in_specs=[whole((2 * rows, ff))] + [pl.BlockSpec(memory_space=pltpu.HBM)] * 2,
        args=(grad, w_gate, w_up),
        out_specs=[pl.BlockSpec((CAP, tile), lambda j: (0, j))] * n,
        scratch_shapes=[pltpu.VMEM((steps, tile, ff), BF)] * 2 + [pltpu.SemaphoreType.DMA((2, steps))],
        compiler_params=params(),
        cost_estimate=cost(4 * rows * width * ff, 4 * width * ff + 2 * rows * (width + 2 * ff)),
        name="input_grad",
    )


def hold_kernel(*_):
    pass


def hold(values, after):
    anywhere = pl.BlockSpec(memory_space=pl.ANY)
    return call(
        hold_kernel,
        after,
        [anywhere] * len(values),
        values,
        out_shape=[shape_of(v.shape) for v in values],
        out_specs=[anywhere] * len(values),
        input_output_aliases={i: i for i in range(len(values))},
        cost_estimate=cost(10 * 10**9, 0),
        name="hold",
    )


def fold_two_kernel(x_keep, x_recv, y_keep, y_recv, x_next, x_mine, y_next, y_mine):
    for keep, recv, away, mine in ((x_keep, x_recv, x_next, x_mine), (y_keep, y_recv, y_next, y_mine)):
        away[...] = (keep[1].astype(F32) + recv[1].astype(F32)).astype(BF)
        mine[...] = (keep[0].astype(F32) + recv[0].astype(F32)).astype(BF)


def fold_two(x_keep, x_recv, y_keep, y_recv, after):
    _, high, width = x_keep.shape
    return call(
        fold_two_kernel,
        after,
        grid=(1,),
        out_shape=[shape_of((high, width))] * 4,
        in_specs=[whole((2, high, width))] * 4,
        args=(x_keep, x_recv, y_keep, y_recv),
        out_specs=[whole((high, width))] * 4,
        compiler_params=params(),
        cost_estimate=cost(4 * high * width, 24 * high * width),
        name="fold_two",
    )


def fold_last_kernel(x_mine, x_recv, y_mine, y_recv, gate_ref, up_ref, down_ref):
    size, strip = gate_ref.shape[1], 16
    tile = 256
    for i, (mine, recv, out_ref) in enumerate(((x_mine, x_recv, gate_ref), (y_mine, y_recv, up_ref))):
        total = (mine[...].astype(F32) + recv[...].astype(F32)).astype(BF)
        out_ref[0] = total[:size]
        for c in range(down_ref.shape[2] // tile):
            for j in range(3):
                down_ref[0, (3 * i + j) * strip : (3 * i + j + 1) * strip, c * tile : (c + 1) * tile] = total[
                    size + c * strip : size + (c + 1) * strip, j * tile : (j + 1) * tile
                ]


def fold_last(x_mine, x_recv, y_mine, y_recv, shapes, after):
    high, width = x_mine.shape
    return call(
        fold_last_kernel,
        after,
        grid=(1,),
        out_shape=[shape_of(s) for s in shapes],
        in_specs=[whole((high, width))] * 4,
        args=(x_mine, x_recv, y_mine, y_recv),
        out_specs=[whole(s) for s in shapes],
        compiler_params=params(),
        cost_estimate=cost(2 * high * width, 12 * high * width),
        name="fold_last",
    )


CORE, ALONG_X, ALONG_Y = 1, 2, 4


def swap(value, bit, count=8):
    return lax.ppermute(value, "dp", [(i, i ^ bit) for i in range(count)])


def combine_out_kernel(n, z_ref, ids_ref, prob_ref, grad_ref, *refs):
    back_refs = refs[:n]
    out_ref, prob_grad_ref, rows, sums, firsts, seconds = refs[n:]
    tok_count = ids_ref.shape[1]
    step = pl.program_id(0)

    @pl.when(step == 0)
    def _():
        ids = ids_ref[...]
        experts = [jnp.bitwise_xor(z_ref[0], k) for k in range(n)]
        rank = ranks(ids, experts)
        for k in range(n):
            first, second = chosen(ids, experts[k])
            at = places(rank[k : k + 1, :])
            here = slice(k * CAP, (k + 1) * CAP)
            firsts[here, :] = jnp.where(jnp.logical_and(at, first), 1.0, 0.0)
            seconds[here, :] = jnp.where(jnp.logical_and(at, second), 1.0, 0.0)
        sums[...] = jnp.zeros_like(sums)

    for k in range(n):
        rows[k * CAP : (k + 1) * CAP, :] = back_refs[k][...]
    prob = jnp.concatenate([prob_ref[...], jnp.zeros((6, tok_count), F32)], axis=0).T
    grad = grad_ref[...].astype(F32)
    total = 0.0
    part = []
    for choice, at in enumerate((firsts, seconds)):
        out = mm_rows(at[...].astype(BF), rows[...])
        total = total + prob[:, choice : choice + 1] * out
        part.append(jnp.sum(grad * out, axis=1, keepdims=True))
    out_ref[...] = total.astype(BF)
    sums[...] += jnp.concatenate(part + [jnp.zeros((tok_count, 6), F32)], axis=1)

    @pl.when(step == pl.num_programs(0) - 1)
    def _():
        prob_grad_ref[...] = sums[...].T[0:2, :]


def combine_out(z, ids_t, prob_t, out_grad, backs):
    n = len(backs)
    tok_count, width = out_grad.shape
    tile = 512
    by_tile = pl.BlockSpec((tok_count, tile), lambda j: (0, j))
    rows = n * CAP
    return pl.pallas_call(
        functools.partial(combine_out_kernel, n),
        grid=(width // tile,),
        out_shape=[shape_of((tok_count, width)), shape_of((2, tok_count), F32)],
        in_specs=[in_smem(), whole(ids_t.shape), whole(prob_t.shape), by_tile]
        + [pl.BlockSpec((CAP, tile), lambda j: (0, j))] * n,
        out_specs=[by_tile, whole((2, tok_count))],
        scratch_shapes=[pltpu.VMEM((rows, tile), BF), pltpu.VMEM((tok_count, 8), F32)]
        + [pltpu.VMEM((rows, tok_count), F32)] * 2,
        compiler_params=params(),
        cost_estimate=cost(4 * rows * tok_count * width, 2 * width * (rows + 2 * tok_count)),
        name="combine_out",
    )(z, ids_t, prob_t, out_grad, *backs)


def combine_in_kernel(n, z_ref, ids_ref, *refs):
    back_refs = refs[:n]
    out_ref, rows, picks = refs[n:]

    @pl.when(pl.program_id(0) == 0)
    def _():
        ids = ids_ref[...]
        experts = [jnp.bitwise_xor(z_ref[0], k) for k in range(n)]
        rank = ranks(ids, experts)
        for k in range(n):
            here = jnp.logical_and(places(rank[k : k + 1, :]), jnp.logical_or(*chosen(ids, experts[k])))
            picks[k * CAP : (k + 1) * CAP, :] = jnp.where(here, 1.0, 0.0)

    for k in range(n):
        rows[k * CAP : (k + 1) * CAP, :] = back_refs[k][...]
    out_ref[...] = mm_rows(picks[...].astype(BF), rows[...]).astype(BF)


def combine_in(z, ids_t, backs, hint):
    n = len(backs)
    width = backs[0].shape[1]
    tok_count = ids_t.shape[1]
    tile = 1024
    rows = n * CAP
    return pl.pallas_call(
        functools.partial(combine_in_kernel, n),
        grid=(width // tile,),
        out_shape=shape_of((tok_count, width)),
        in_specs=[in_smem(), whole(ids_t.shape)] + [pl.BlockSpec((CAP, tile), lambda j: (0, j))] * n,
        out_specs=pl.BlockSpec((tok_count, tile), lambda j: (0, j)),
        scratch_shapes=[pltpu.VMEM((rows, tile), BF), pltpu.VMEM((rows, tok_count), F32)],
        compiler_params=params(),
        cost_estimate=cost(hint, 2 * width * (rows + tok_count)),
        name="combine_in",
    )(z, ids_t, *backs)


def exchange(values):
    n = len(values)
    moved = list(values)
    for k in range(n - 1, 0, -1):
        moved[k] = lax.ppermute(values[k], "expert", [(i, i ^ k) for i in range(n)])
    return moved


def local(tokens, expert_ids, gate_probs, w_gate, w_up, w_down, out_grad):
    n = lax.axis_size("expert")
    parts = lax.axis_size("dp")
    z = lax.axis_index("expert").astype(jnp.int32).reshape(1)
    ids_t, prob_t = expert_ids.T, gate_probs.T
    xs = exchange(pick_rows(n, False, z, ids_t, prob_t, tokens))
    gs = exchange(pick_rows(n, True, z, ids_t, prob_t, out_grad))
    made = forward(xs, w_gate, w_up, w_down)
    slope, act, hidden = made[:3]
    back_out = exchange(made[3:])
    layer_out, prob_grad_t = combine_out(z, ids_t, prob_t, out_grad, back_out)
    if parts == 8:
        me = lax.axis_index("dp").astype(jnp.int32)
        flips = [(r >> 2 & 1) * CORE | (r & 1) * ALONG_X | (r >> 1 & 1) * ALONG_Y for r in range(8)]
        owners = jnp.stack([me ^ f for f in flips])
        keep_t, send_t, w_near = turn(parts, owners, xs, hidden, w_down)
        grad, g_rows, pack = hidden_grad(gs, w_near, slope, act, send_t)
        other, recv = swap(grad, CORE), swap(pack, CORE)
        x_send, y_send = outer(1, keep_t, recv, grad, other, g_rows, [])
        din = input_grad(n, grad, w_gate, w_up, [x_send])
        x_keep, y_keep = outer(0, keep_t, recv, grad, other, g_rows, din[:1])
        back_in = exchange(din[:1] + hold(din[1:], [*back_out[1:], x_keep]))
        x_next, x_mine, y_next, y_mine = fold_two(
            x_keep, swap(x_send, ALONG_X), y_keep, swap(y_send, ALONG_Y), [*din[:1], layer_out]
        )
        token_grad = combine_in(z, ids_t, back_in, 10 * 10**9)
        shapes = [(1, d // parts, w) for d, w in (w_gate.shape[1:], w_up.shape[1:], w_down.shape[1:])]
        sum_gate, sum_up, sum_down = fold_last(
            x_mine, swap(x_next, ALONG_Y), y_mine, swap(y_next, ALONG_X), shapes, [token_grad]
        )
    else:
        grad, d_rows, _ = hidden_grad(gs, w_down, slope, act, hidden[:16, :256])
        din = input_grad(n, grad, w_gate, w_up, [])
        back_in = exchange(din)
        token_grad = combine_in(z, ids_t, back_in, 10**8)
        x_rows, count = jnp.concatenate(xs, 0), n * CAP
        sum_gate, sum_up, sum_down = (
            lax.psum_scatter(mm_rows(a, b).astype(BF), "dp", scatter_dimension=0, tiled=True)[None]
            for a, b in ((x_rows, grad[:count]), (x_rows, grad[count:]), (hidden, d_rows))
        )
    return layer_out, prob_grad_t.T, token_grad, sum_gate, sum_up, sum_down


def solution(mesh):
    rows = P(("dp", "expert"), None)
    weights = P("expert", None, None)
    summed = P("expert", "dp", None)
    return jax.shard_map(
        local,
        mesh=mesh,
        in_specs=(rows, rows, rows, weights, weights, weights, rows),
        out_specs=(rows, rows, rows, summed, summed, summed),
        check_vma=False,
    )
```

```python
import functools
import jax
import jax.numpy as jnp
from jax import lax
from jax.experimental import pallas as pl
from jax.experimental.pallas import tpu as pltpu
from jax.sharding import PartitionSpec as P

CAP = 64
BF = jnp.bfloat16
F32 = jnp.float32
MIB = 1 << 20


def mm(left, right):
    return jnp.dot(left, right, preferred_element_type=F32)


def mm_rows(left, right):
    return lax.dot_general(left, right, (((0,), (0,)), ((), ())), preferred_element_type=F32)


def mm_cols(left, right):
    return lax.dot_general(left, right, (((1,), (1,)), ((), ())), preferred_element_type=F32)


def shape_of(shape, dtype=BF):
    return jax.ShapeDtypeStruct(tuple(shape), dtype)


def whole(shape):
    return pl.BlockSpec(tuple(shape), lambda *_: (0,) * len(shape))


def in_smem():
    return pl.BlockSpec(memory_space=pltpu.SMEM)


def params(limit=16):
    return pltpu.CompilerParams(vmem_limit_bytes=limit * MIB)


def call(kernel, after, in_specs, args, **kwargs):
    count = len(args)

    def body(*refs):
        kernel(*refs[:count], *refs[count + len(after) :])

    specs = list(in_specs) + [pl.BlockSpec(memory_space=pl.ANY)] * len(after)
    return pl.pallas_call(body, in_specs=specs, **kwargs)(*args, *after)


TOKEN = (8, 128)


def mark(ref):
    ref[...] = jnp.zeros(TOKEN, F32)


def cost(flops, moved):
    return pl.CostEstimate(flops=int(flops), bytes_accessed=int(moved), transcendentals=0)


def chosen(ids, expert):
    first = ids[0:1, :] == expert
    second = ids[1:2, :] == expert
    return first, second


def ranks(ids, experts):
    tok_count = ids.shape[1]
    masks = [jnp.where(jnp.logical_or(*chosen(ids, e)), 1.0, 0.0) for e in experts]
    mask = jnp.concatenate(masks + [jnp.zeros((-len(masks) % 16, tok_count), F32)], axis=0)
    before = lax.broadcasted_iota(jnp.int32, (tok_count, tok_count), 0)
    after = lax.broadcasted_iota(jnp.int32, (tok_count, tok_count), 1)
    upper = jnp.where(before < after, 1.0, 0.0).astype(BF)
    return mm(mask.astype(BF), upper).astype(jnp.int32)


def places(rank_row):
    tok_count = rank_row.shape[1]
    return lax.broadcasted_iota(jnp.int32, (CAP, tok_count), 0) == rank_row


def pick_kernel(n, scaled, z_ref, ids_ref, prob_ref, rows_ref, *outs):
    ids = ids_ref[...]
    prob = prob_ref[...]
    experts = [jnp.bitwise_xor(z_ref[0], k) for k in range(n)]
    rank = ranks(ids, experts)
    for k in range(n - 1, -1, -1):
        first, second = chosen(ids, experts[k])
        at = places(rank[k : k + 1, :])
        here = jnp.logical_and(at, jnp.logical_or(first, second))
        picked = mm(jnp.where(here, 1.0, 0.0).astype(BF), rows_ref[...])
        if scaled:
            weight = jnp.where(first, prob[0:1, :], prob[1:2, :])
            picked = jnp.sum(jnp.where(here, weight, 0.0), axis=1, keepdims=True) * picked
        outs[k][...] = picked.astype(BF)


def pick_rows(n, scaled, z, ids_t, prob_t, rows):
    tok_count, width = rows.shape
    return pl.pallas_call(
        functools.partial(pick_kernel, n, scaled),
        out_shape=[shape_of((CAP, width))] * n,
        in_specs=[in_smem(), whole(ids_t.shape), whole(prob_t.shape), whole(rows.shape)],
        out_specs=[whole((CAP, width))] * n,
        grid=(1,),
        compiler_params=params(60),
        cost_estimate=cost(2 * n * CAP * tok_count * width, 4 * tok_count * width * 2),
        name="pick_rows",
    )(z, ids_t, prob_t, rows)


def silu_parts(gate):
    sig = jax.nn.sigmoid(gate)
    return gate * sig, sig * (1.0 + gate * (1.0 - sig))


def forward_kernel(n, steps, tile, *refs):
    x_refs = refs[:n]
    weights = refs[n : n + 3]
    slope_ref, act_ref, hid_ref = refs[n + 3 : n + 6]
    out_refs = refs[n + 6 : 2 * n + 6]
    rows, total, wg_buf, wu_buf, wd_buf, sems = refs[2 * n + 6 :]
    step = pl.program_id(0)

    def loads(j):
        at = pl.ds(pl.multiple_of(j * tile, tile), tile)
        wg_ref, wu_ref, wd_ref = weights
        return (
            pltpu.make_async_copy(wg_ref.at[0, :, at], wg_buf.at[j], sems.at[0, j]),
            pltpu.make_async_copy(wu_ref.at[0, :, at], wu_buf.at[j], sems.at[1, j]),
            pltpu.make_async_copy(wd_ref.at[0, at, :], wd_buf.at[j], sems.at[2, j]),
        )

    @pl.when(step == 0)
    def _():
        for j in range(steps):
            for load in loads(j):
                load.start()
        for k in range(n):
            rows[k * CAP : (k + 1) * CAP, :] = x_refs[k][...]

    for load in loads(step):
        load.wait()
    gate = mm(rows[...], wg_buf[step])
    up = mm(rows[...], wu_buf[step])
    act, slope = silu_parts(gate)
    act_ref[...] = act
    slope_ref[...] = up * slope
    hidden = (act * up).astype(BF)
    hid_ref[...] = hidden
    part = mm(hidden, wd_buf[step])

    @pl.when(step == 0)
    def _():
        total[...] = part

    @pl.when(step > 0)
    def _():
        total[...] += part

    @pl.when(step == steps - 1)
    def _():
        for k in range(n):
            out_refs[k][...] = total[k * CAP : (k + 1) * CAP, :].astype(BF)


def weight_specs(width, tile):
    by_col = pl.BlockSpec((1, width, tile), lambda j: (0, 0, j))
    by_row = pl.BlockSpec((1, tile, width), lambda j: (0, j, 0))
    return [by_col, by_col, by_row]


def forward(xs, w_gate, w_up, w_down):
    n = len(xs)
    width, ff = w_gate.shape[1:]
    tile = 256
    steps = ff // tile
    rows = n * CAP
    part = pl.BlockSpec((rows, tile), lambda j: (0, j))
    return pl.pallas_call(
        functools.partial(forward_kernel, n, steps, tile),
        grid=(steps,),
        out_shape=[shape_of((rows, ff), F32)] * 2 + [shape_of((rows, ff))] + [shape_of((CAP, width))] * n,
        in_specs=[whole((CAP, width))] * n + [pl.BlockSpec(memory_space=pltpu.HBM)] * 3,
        out_specs=[part, part, part] + [whole((CAP, width))] * n,
        scratch_shapes=[
            pltpu.VMEM((rows, width), BF),
            pltpu.VMEM((rows, width), F32),
            pltpu.VMEM((steps, width, tile), BF),
            pltpu.VMEM((steps, width, tile), BF),
            pltpu.VMEM((steps, tile, width), BF),
            pltpu.SemaphoreType.DMA((3, steps)),
        ],
        compiler_params=params(50),
        cost_estimate=cost(6 * rows * width * ff, 6 * width * ff + 4 * rows * width + 10 * rows * ff),
        name="forward",
    )(*xs, w_gate, w_up, w_down)


def turn_kernel(n, parts, me_ref, *refs):
    x_refs = refs[:n]
    hid_ref, w_ref, keep_ref, send_ref, copy_ref, rows, turned, sem = refs[n:]
    load = pltpu.make_async_copy(w_ref, copy_ref, sem)
    load.start()
    for k in range(n):
        rows[k * CAP : (k + 1) * CAP, :] = x_refs[k][...]
    turned[...] = hid_ref[...].T
    half = parts // 2
    x_size, h_size = rows.shape[1] // parts, turned.shape[0] // parts
    strip = h_size // 6
    for rel in range(parts):
        out_ref, i = (keep_ref, rel) if rel < half else (send_ref, rel - half)
        at = pl.multiple_of(me_ref[rel] * x_size, x_size)
        out_ref[i * x_size : (i + 1) * x_size, :] = rows[:, pl.ds(at, x_size)].T
        for j in range(6):
            at = pl.multiple_of(me_ref[rel] * h_size + j * strip, strip)
            leaves, spot = (i & 1, i >> 1) if j < 3 else (i >> 1, 2 + (i & 1))
            base = half * x_size + ((j % 3) * 2 * half + leaves * half + spot) * strip
            out_ref[base : base + strip, :] = turned[pl.ds(at, strip), :]
    load.wait()


def turn(parts, owners, xs, hidden, w_down):
    n = len(xs)
    width = xs[0].shape[1]
    rows, ff = hidden.shape
    high = (width + ff) // 2
    return pl.pallas_call(
        functools.partial(turn_kernel, n, parts),
        grid=(1,),
        out_shape=[shape_of((high, rows))] * 2 + [shape_of(w_down.shape)],
        in_specs=[in_smem()] + [whole((CAP, width))] * n + [whole(hidden.shape), pl.BlockSpec(memory_space=pltpu.HBM)],
        out_specs=[whole((high, rows))] * 2 + [whole(w_down.shape)],
        scratch_shapes=[pltpu.VMEM((rows, width), BF), pltpu.VMEM((ff, rows), BF), pltpu.SemaphoreType.DMA],
        compiler_params=params(),
        cost_estimate=cost(2 * rows * width, 6 * rows * (width + ff)),
        name="turn",
    )(owners, *xs, hidden, w_down)


def outer_kernel(group, keep_ref, recv_ref, own_ref, other_ref, own_g_ref, x_ref, y_ref, token_ref):
    mark(token_ref)
    step = pl.program_id(0)
    half, high = 4, own_ref.shape[0] // 2
    size = 256
    strip = 16
    for i in range(2):
        block = 2 * i + group
        at = slice(block * size, (block + 1) * size)
        gate = mm(keep_ref[at, :], own_ref[:high, :]) + mm(recv_ref[at, :], other_ref[:high, :])
        x_ref[i, :size, :] = gate.astype(BF)
        block = 2 * group + i
        at = slice(block * size, (block + 1) * size)
        up = mm(keep_ref[at, :], own_ref[high:, :]) + mm(recv_ref[at, :], other_ref[high:, :])
        y_ref[i, :size, :] = up.astype(BF)
    at = pl.ds(pl.multiple_of(half * size + (2 * step + group) * half * strip, strip), half * strip)
    tile = x_ref.shape[2]
    turned = keep_ref.shape[0]
    for c in range(own_g_ref.shape[1] // tile):
        theirs = recv_ref[turned + c * high : turned + (c + 1) * high, :]
        down = mm(keep_ref[at, :], own_g_ref[:, c * tile : (c + 1) * tile]) + mm(recv_ref[at, :], theirs)
        down = down.astype(BF)
        for spot in range(half):
            out_ref = x_ref if spot < 2 else y_ref
            out_ref[spot % 2, size + c * strip : size + (c + 1) * strip, :] = down[spot * strip : (spot + 1) * strip]


def outer(group, keep, recv, own, other, own_g, after):
    rows, width = own_g.shape
    ff = own.shape[1]
    tile = 256
    col = pl.BlockSpec((2 * rows, tile), lambda j: (0, j))
    high = 256 + 16 * (width // tile)
    part = pl.BlockSpec((2, high, tile), lambda j: (0, 0, j))
    return call(
        functools.partial(outer_kernel, group),
        after,
        grid=(ff // tile,),
        out_shape=[shape_of((2, high, ff))] * 2 + [shape_of(TOKEN, F32)],
        in_specs=[whole(keep.shape), whole(recv.shape)] + [col] * 2 + [whole(own_g.shape)],
        args=(keep, recv, own, other, own_g),
        out_specs=[part] * 2 + [whole(TOKEN)],
        compiler_params=params(),
        cost_estimate=cost(3 * rows * width * ff, 4 * keep.size + 8 * high * ff),
        name="outer",
    )


def hidden_grad_kernel(n, *refs):
    g_refs = refs[:n]
    wd_ref, slope_ref, act_ref, turned_ref, grad_ref, rows, pack_ref = refs[n:]

    @pl.when(pl.program_id(0) == 0)
    def _():
        for k in range(n):
            rows[k * CAP : (k + 1) * CAP, :] = g_refs[k][...]
        high = turned_ref.shape[0]
        pack_ref[:high, :] = turned_ref[...]
        tile = pack_ref.shape[1]
        for c in range(rows.shape[1] // tile):
            at = high + c * n * CAP
            pack_ref[at : at + n * CAP, :] = rows[:, c * tile : (c + 1) * tile]

    grad = mm_cols(rows[...], wd_ref[0])
    grad_ref[: n * CAP, :] = (grad * slope_ref[...]).astype(BF)
    grad_ref[n * CAP :, :] = (grad * act_ref[...]).astype(BF)


def hidden_grad(gs, w_down, slope, act, turned):
    n = len(gs)
    ff, width = w_down.shape[1:]
    rows = n * CAP
    tile = 256
    part = pl.BlockSpec((rows, tile), lambda j: (0, j))
    tall = (turned.shape[0] + rows * (width // 256), 256)
    return pl.pallas_call(
        functools.partial(hidden_grad_kernel, n),
        grid=(ff // tile,),
        out_shape=[shape_of((2 * rows, ff)), shape_of((rows, width)), shape_of(tall)],
        in_specs=[whole((CAP, width))] * n + [weight_specs(width, tile)[2], part, part, whole(turned.shape)],
        out_specs=[pl.BlockSpec((2 * rows, tile), lambda j: (0, j)), whole((rows, width)), whole(tall)],
        compiler_params=params(),
        cost_estimate=cost(2 * rows * width * ff, 2 * width * ff + 4 * rows * width + 12 * rows * ff),
        name="hidden_grad",
    )(*gs, w_down, slope, act, turned)


def input_grad_kernel(n, steps, tile, grad_ref, wg_ref, wu_ref, *refs):
    out_refs = refs[:n]
    token_ref, wg_buf, wu_buf, sems = refs[n:]
    mark(token_ref)
    step = pl.program_id(0)

    def loads(j):
        at = pl.ds(pl.multiple_of(j * tile, tile), tile)
        return (
            pltpu.make_async_copy(wg_ref.at[0, at, :], wg_buf.at[j], sems.at[0, j]),
            pltpu.make_async_copy(wu_ref.at[0, at, :], wu_buf.at[j], sems.at[1, j]),
        )

    @pl.when(step == 0)
    def _():
        for j in range(steps):
            for load in loads(j):
                load.start()

    for load in loads(step):
        load.wait()
    rows = n * CAP
    total = mm_cols(grad_ref[:rows, :], wg_buf[step]) + mm_cols(grad_ref[rows:, :], wu_buf[step])
    for k in range(n):
        out_refs[k][...] = total[k * CAP : (k + 1) * CAP, :].astype(BF)


def input_grad(n, grad, w_gate, w_up, after):
    rows, ff = n * CAP, grad.shape[1]
    width = w_gate.shape[1]
    tile = 512
    steps = width // tile
    return call(
        functools.partial(input_grad_kernel, n, steps, tile),
        after,
        grid=(steps,),
        out_shape=[shape_of((CAP, width))] * n + [shape_of(TOKEN, F32)],
        in_specs=[whole((2 * rows, ff))] + [pl.BlockSpec(memory_space=pltpu.HBM)] * 2,
        args=(grad, w_gate, w_up),
        out_specs=[pl.BlockSpec((CAP, tile), lambda j: (0, j))] * n + [whole(TOKEN)],
        scratch_shapes=[pltpu.VMEM((steps, tile, ff), BF)] * 2 + [pltpu.SemaphoreType.DMA((2, steps))],
        compiler_params=params(),
        cost_estimate=cost(4 * rows * width * ff, 4 * width * ff + 2 * rows * (width + 2 * ff)),
        name="input_grad",
    )


def hold_kernel(*_):
    pass


def hold(values, after):
    anywhere = pl.BlockSpec(memory_space=pl.ANY)
    return call(
        hold_kernel,
        after,
        [anywhere] * len(values),
        values,
        out_shape=[shape_of(v.shape) for v in values],
        out_specs=[anywhere] * len(values),
        input_output_aliases={i: i for i in range(len(values))},
        cost_estimate=cost(10 * 10**9, 0),
        name="hold",
    )


def fold_two_kernel(keep, recv, away, mine, token_ref):
    mark(token_ref)
    away[...] = (keep[1].astype(F32) + recv[1].astype(F32)).astype(BF)
    mine[...] = (keep[0].astype(F32) + recv[0].astype(F32)).astype(BF)


def fold_two(keep, recv, after):
    _, high, width = keep.shape
    return call(
        fold_two_kernel,
        after,
        grid=(1,),
        out_shape=[shape_of((high, width))] * 2 + [shape_of(TOKEN, F32)],
        in_specs=[whole((2, high, width))] * 2,
        args=(keep, recv),
        out_specs=[whole((high, width))] * 2 + [whole(TOKEN)],
        compiler_params=params(),
        cost_estimate=cost(2 * high * width, 12 * high * width),
        name="fold_two",
    )


def fold_last_kernel(x_mine, x_recv, y_mine, y_recv, gate_ref, up_ref, down_ref):
    size, strip = gate_ref.shape[1], 16
    tile = 256
    for i, (mine, recv, out_ref) in enumerate(((x_mine, x_recv, gate_ref), (y_mine, y_recv, up_ref))):
        total = (mine[...].astype(F32) + recv[...].astype(F32)).astype(BF)
        out_ref[0] = total[:size]
        for c in range(down_ref.shape[2] // tile):
            for j in range(3):
                down_ref[0, (3 * i + j) * strip : (3 * i + j + 1) * strip, c * tile : (c + 1) * tile] = total[
                    size + c * strip : size + (c + 1) * strip, j * tile : (j + 1) * tile
                ]


def fold_last(x_mine, x_recv, y_mine, y_recv, shapes, after):
    high, width = x_mine.shape
    return call(
        fold_last_kernel,
        after,
        grid=(1,),
        out_shape=[shape_of(s) for s in shapes],
        in_specs=[whole((high, width))] * 4,
        args=(x_mine, x_recv, y_mine, y_recv),
        out_specs=[whole(s) for s in shapes],
        compiler_params=params(),
        cost_estimate=cost(2 * high * width, 12 * high * width),
        name="fold_last",
    )


CORE, ALONG_X, ALONG_Y = 1, 2, 4


def swap(value, bit, count=8):
    return lax.ppermute(value, "dp", [(i, i ^ bit) for i in range(count)])


def combine_out_kernel(n, z_ref, ids_ref, prob_ref, grad_ref, *refs):
    back_refs = refs[:n]
    out_ref, prob_grad_ref, token_ref, rows, sums, firsts, seconds = refs[n:]
    mark(token_ref)
    tok_count = ids_ref.shape[1]
    step = pl.program_id(0)

    @pl.when(step == 0)
    def _():
        ids = ids_ref[...]
        experts = [jnp.bitwise_xor(z_ref[0], k) for k in range(n)]
        rank = ranks(ids, experts)
        for k in range(n):
            first, second = chosen(ids, experts[k])
            at = places(rank[k : k + 1, :])
            here = slice(k * CAP, (k + 1) * CAP)
            firsts[here, :] = jnp.where(jnp.logical_and(at, first), 1.0, 0.0)
            seconds[here, :] = jnp.where(jnp.logical_and(at, second), 1.0, 0.0)
        sums[...] = jnp.zeros_like(sums)

    for k in range(n):
        rows[k * CAP : (k + 1) * CAP, :] = back_refs[k][...]
    prob = jnp.concatenate([prob_ref[...], jnp.zeros((6, tok_count), F32)], axis=0).T
    grad = grad_ref[...].astype(F32)
    total = 0.0
    part = []
    for choice, at in enumerate((firsts, seconds)):
        out = mm_rows(at[...].astype(BF), rows[...])
        total = total + prob[:, choice : choice + 1] * out
        part.append(jnp.sum(grad * out, axis=1, keepdims=True))
    out_ref[...] = total.astype(BF)
    sums[...] += jnp.concatenate(part + [jnp.zeros((tok_count, 6), F32)], axis=1)

    @pl.when(step == pl.num_programs(0) - 1)
    def _():
        prob_grad_ref[...] = sums[...].T[0:2, :]


def combine_out(z, ids_t, prob_t, out_grad, backs):
    n = len(backs)
    tok_count, width = out_grad.shape
    tile = 512
    by_tile = pl.BlockSpec((tok_count, tile), lambda j: (0, j))
    rows = n * CAP
    return pl.pallas_call(
        functools.partial(combine_out_kernel, n),
        grid=(width // tile,),
        out_shape=[shape_of((tok_count, width)), shape_of((2, tok_count), F32), shape_of(TOKEN, F32)],
        in_specs=[in_smem(), whole(ids_t.shape), whole(prob_t.shape), by_tile]
        + [pl.BlockSpec((CAP, tile), lambda j: (0, j))] * n,
        out_specs=[by_tile, whole((2, tok_count)), whole(TOKEN)],
        scratch_shapes=[pltpu.VMEM((rows, tile), BF), pltpu.VMEM((tok_count, 8), F32)]
        + [pltpu.VMEM((rows, tok_count), F32)] * 2,
        compiler_params=params(),
        cost_estimate=cost(4 * rows * tok_count * width, 2 * width * (rows + 2 * tok_count)),
        name="combine_out",
    )(z, ids_t, prob_t, out_grad, *backs)


def combine_in_kernel(n, z_ref, ids_ref, *refs):
    back_refs = refs[:n]
    out_ref, token_ref, rows, picks = refs[n:]
    mark(token_ref)

    @pl.when(pl.program_id(0) == 0)
    def _():
        ids = ids_ref[...]
        experts = [jnp.bitwise_xor(z_ref[0], k) for k in range(n)]
        rank = ranks(ids, experts)
        for k in range(n):
            here = jnp.logical_and(places(rank[k : k + 1, :]), jnp.logical_or(*chosen(ids, experts[k])))
            picks[k * CAP : (k + 1) * CAP, :] = jnp.where(here, 1.0, 0.0)

    for k in range(n):
        rows[k * CAP : (k + 1) * CAP, :] = back_refs[k][...]
    out_ref[...] = mm_rows(picks[...].astype(BF), rows[...]).astype(BF)


def combine_in(z, ids_t, backs, hint):
    n = len(backs)
    width = backs[0].shape[1]
    tok_count = ids_t.shape[1]
    tile = 1024
    rows = n * CAP
    return pl.pallas_call(
        functools.partial(combine_in_kernel, n),
        grid=(width // tile,),
        out_shape=[shape_of((tok_count, width)), shape_of(TOKEN, F32)],
        in_specs=[in_smem(), whole(ids_t.shape)] + [pl.BlockSpec((CAP, tile), lambda j: (0, j))] * n,
        out_specs=[pl.BlockSpec((tok_count, tile), lambda j: (0, j)), whole(TOKEN)],
        scratch_shapes=[pltpu.VMEM((rows, tile), BF), pltpu.VMEM((rows, tok_count), F32)],
        compiler_params=params(),
        cost_estimate=cost(hint, 2 * width * (rows + tok_count)),
        name="combine_in",
    )(z, ids_t, *backs)


def exchange(values):
    n = len(values)
    moved = list(values)
    for k in range(n - 1, 0, -1):
        moved[k] = lax.ppermute(values[k], "expert", [(i, i ^ k) for i in range(n)])
    return moved


def local(tokens, expert_ids, gate_probs, w_gate, w_up, w_down, out_grad):
    n = lax.axis_size("expert")
    parts = lax.axis_size("dp")
    z = lax.axis_index("expert").astype(jnp.int32).reshape(1)
    ids_t, prob_t = expert_ids.T, gate_probs.T
    xs = exchange(pick_rows(n, False, z, ids_t, prob_t, tokens))
    gs = exchange(pick_rows(n, True, z, ids_t, prob_t, out_grad))
    made = forward(xs, w_gate, w_up, w_down)
    slope, act, hidden = made[:3]
    back_out = exchange(made[3:])
    layer_out, prob_grad_t, shown = combine_out(z, ids_t, prob_t, out_grad, back_out)
    if parts == 8:
        me = lax.axis_index("dp").astype(jnp.int32)
        flips = [(r >> 2 & 1) * CORE | (r & 1) * ALONG_X | (r >> 1 & 1) * ALONG_Y for r in range(8)]
        owners = jnp.stack([me ^ f for f in flips])
        keep_t, send_t, w_near = turn(parts, owners, xs, hidden, w_down)
        grad, g_rows, pack = hidden_grad(gs, w_near, slope, act, send_t)
        other, recv = swap(grad, CORE), swap(pack, CORE)
        x_send, y_send, token = outer(1, keep_t, recv, grad, other, g_rows, [])
        *din, token = input_grad(n, grad, w_gate, w_up, [token])
        x_keep, y_keep, token = outer(0, keep_t, recv, grad, other, g_rows, [token])
        back_in = exchange([din[0], *hold(din[1:], [*back_out[1:], token])])
        x_next, x_mine, token = fold_two(x_keep, swap(x_send, ALONG_X), [shown])
        y_next, y_mine, _ = fold_two(y_keep, swap(y_send, ALONG_Y), [token])
        token_grad, token = combine_in(z, ids_t, back_in, 10 * 10**9)
        shapes = [(1, d // parts, w) for d, w in (w_gate.shape[1:], w_up.shape[1:], w_down.shape[1:])]
        sum_gate, sum_up, sum_down = fold_last(
            x_mine, swap(x_next, ALONG_Y), y_mine, swap(y_next, ALONG_X), shapes, [token]
        )
    else:
        grad, d_rows, _ = hidden_grad(gs, w_down, slope, act, hidden[:16, :256])
        *din, _ = input_grad(n, grad, w_gate, w_up, [])
        back_in = exchange(din)
        token_grad, _ = combine_in(z, ids_t, back_in, 10**8)
        x_rows, count = jnp.concatenate(xs, 0), n * CAP
        sum_gate, sum_up, sum_down = (
            lax.psum_scatter(mm_rows(a, b).astype(BF), "dp", scatter_dimension=0, tiled=True)[None]
            for a, b in ((x_rows, grad[:count]), (x_rows, grad[count:]), (hidden, d_rows))
        )
    return layer_out, prob_grad_t.T, token_grad, sum_gate, sum_up, sum_down


def solution(mesh):
    rows = P(("dp", "expert"), None)
    weights = P("expert", None, None)
    summed = P("expert", "dp", None)
    return jax.shard_map(
        local,
        mesh=mesh,
        in_specs=(rows, rows, rows, weights, weights, weights, rows),
        out_specs=(rows, rows, rows, summed, summed, summed),
        check_vma=False,
    )
```

```python
import functools
import jax
import jax.numpy as jnp
from jax import lax
from jax.experimental import pallas as pl
from jax.experimental.pallas import tpu as pltpu
from jax.sharding import PartitionSpec as P

CAP = 64
BF = jnp.bfloat16
F32 = jnp.float32
MIB = 1 << 20


def mm(left, right):
    return jnp.dot(left, right, preferred_element_type=F32)


def mm_rows(left, right):
    return lax.dot_general(left, right, (((0,), (0,)), ((), ())), preferred_element_type=F32)


def mm_cols(left, right):
    return lax.dot_general(left, right, (((1,), (1,)), ((), ())), preferred_element_type=F32)


def shape_of(shape, dtype=BF):
    return jax.ShapeDtypeStruct(tuple(shape), dtype)


def whole(shape):
    return pl.BlockSpec(tuple(shape), lambda *_: (0,) * len(shape))


def in_smem():
    return pl.BlockSpec(memory_space=pltpu.SMEM)


def params(limit=16):
    return pltpu.CompilerParams(vmem_limit_bytes=limit * MIB)


def call(kernel, after, in_specs, args, **kwargs):
    count = len(args)

    def body(*refs):
        kernel(*refs[:count], *refs[count + len(after) :])

    specs = list(in_specs) + [pl.BlockSpec(memory_space=pl.ANY)] * len(after)
    return pl.pallas_call(body, in_specs=specs, **kwargs)(*args, *after)


TOKEN = (8, 128)


def mark(ref):
    ref[...] = jnp.zeros(TOKEN, F32)


def cost(flops, moved):
    return pl.CostEstimate(flops=int(flops), bytes_accessed=int(moved), transcendentals=0)


def partners(n):
    return [0] + list(range(n - 1, 0, -1))


def chosen(ids, expert):
    first = ids[0:1, :] == expert
    second = ids[1:2, :] == expert
    return first, second


def ranks(ids, experts):
    tok_count = ids.shape[1]
    masks = [jnp.where(jnp.logical_or(*chosen(ids, e)), 1.0, 0.0) for e in experts]
    mask = jnp.concatenate(masks + [jnp.zeros((-len(masks) % 16, tok_count), F32)], axis=0)
    before = lax.broadcasted_iota(jnp.int32, (tok_count, tok_count), 0)
    after = lax.broadcasted_iota(jnp.int32, (tok_count, tok_count), 1)
    upper = jnp.where(before < after, 1.0, 0.0).astype(BF)
    return mm(mask.astype(BF), upper).astype(jnp.int32)


def places(rank_row):
    tok_count = rank_row.shape[1]
    return lax.broadcasted_iota(jnp.int32, (CAP, tok_count), 0) == rank_row


def pick_kernel(n, scaled, z_ref, ids_ref, prob_ref, rows_ref, *outs):
    ids = ids_ref[...]
    prob = prob_ref[...]
    experts = [jnp.bitwise_xor(z_ref[0], k) for k in partners(n)]
    rank = ranks(ids, experts)
    for k in range(n - 1, -1, -1):
        first, second = chosen(ids, experts[k])
        at = places(rank[k : k + 1, :])
        here = jnp.logical_and(at, jnp.logical_or(first, second))
        picked = mm(jnp.where(here, 1.0, 0.0).astype(BF), rows_ref[...])
        if scaled:
            weight = jnp.where(first, prob[0:1, :], prob[1:2, :])
            picked = jnp.sum(jnp.where(here, weight, 0.0), axis=1, keepdims=True) * picked
        outs[k][...] = picked.astype(BF)


def pick_rows(n, scaled, z, ids_t, prob_t, rows):
    tok_count, width = rows.shape
    return pl.pallas_call(
        functools.partial(pick_kernel, n, scaled),
        out_shape=[shape_of((CAP, width))] * n,
        in_specs=[in_smem(), whole(ids_t.shape), whole(prob_t.shape), whole(rows.shape)],
        out_specs=[whole((CAP, width))] * n,
        grid=(1,),
        compiler_params=params(60),
        cost_estimate=cost(2 * n * CAP * tok_count * width, 4 * tok_count * width * 2),
        name="pick_rows",
    )(z, ids_t, prob_t, rows)


def silu_parts(gate):
    sig = jax.nn.sigmoid(gate)
    return gate * sig, sig * (1.0 + gate * (1.0 - sig))


def forward_kernel(n, steps, tile, *refs):
    x_refs = refs[:n]
    weights = refs[n : n + 3]
    slope_ref, act_ref, hid_ref = refs[n + 3 : n + 6]
    out_refs = refs[n + 6 : 2 * n + 6]
    rows, total, wg_buf, wu_buf, wd_buf, sems = refs[2 * n + 6 :]
    step = pl.program_id(0)

    def loads(j):
        at = pl.ds(pl.multiple_of(j * tile, tile), tile)
        wg_ref, wu_ref, wd_ref = weights
        return (
            pltpu.make_async_copy(wg_ref.at[0, :, at], wg_buf.at[j], sems.at[0, j]),
            pltpu.make_async_copy(wu_ref.at[0, :, at], wu_buf.at[j], sems.at[1, j]),
            pltpu.make_async_copy(wd_ref.at[0, at, :], wd_buf.at[j], sems.at[2, j]),
        )

    @pl.when(step == 0)
    def _():
        for j in range(steps):
            for load in loads(j):
                load.start()
        for k in range(n):
            rows[k * CAP : (k + 1) * CAP, :] = x_refs[k][...]

    for load in loads(step):
        load.wait()
    gate = mm(rows[...], wg_buf[step])
    up = mm(rows[...], wu_buf[step])
    act, slope = silu_parts(gate)
    act_ref[...] = act
    slope_ref[...] = up * slope
    hidden = (act * up).astype(BF)
    hid_ref[...] = hidden
    part = mm(hidden, wd_buf[step])

    @pl.when(step == 0)
    def _():
        total[...] = part

    @pl.when(step > 0)
    def _():
        total[...] += part

    @pl.when(step == steps - 1)
    def _():
        for k in range(n):
            out_refs[k][...] = total[k * CAP : (k + 1) * CAP, :].astype(BF)


def weight_specs(width, tile):
    by_col = pl.BlockSpec((1, width, tile), lambda j: (0, 0, j))
    by_row = pl.BlockSpec((1, tile, width), lambda j: (0, j, 0))
    return [by_col, by_col, by_row]


def forward(xs, w_gate, w_up, w_down):
    n = len(xs)
    width, ff = w_gate.shape[1:]
    tile = 256
    steps = ff // tile
    rows = n * CAP
    part = pl.BlockSpec((rows, tile), lambda j: (0, j))
    return pl.pallas_call(
        functools.partial(forward_kernel, n, steps, tile),
        grid=(steps,),
        out_shape=[shape_of((rows, ff), F32)] * 2 + [shape_of((rows, ff))] + [shape_of((CAP, width))] * n,
        in_specs=[whole((CAP, width))] * n + [pl.BlockSpec(memory_space=pltpu.HBM)] * 3,
        out_specs=[part, part, part] + [whole((CAP, width))] * n,
        scratch_shapes=[
            pltpu.VMEM((rows, width), BF),
            pltpu.VMEM((rows, width), F32),
            pltpu.VMEM((steps, width, tile), BF),
            pltpu.VMEM((steps, width, tile), BF),
            pltpu.VMEM((steps, tile, width), BF),
            pltpu.SemaphoreType.DMA((3, steps)),
        ],
        compiler_params=params(50),
        cost_estimate=cost(6 * rows * width * ff, 6 * width * ff + 4 * rows * width + 10 * rows * ff),
        name="forward",
    )(*xs, w_gate, w_up, w_down)


def turn_kernel(n, parts, me_ref, *refs):
    x_refs = refs[:n]
    hid_ref, w_ref, keep_ref, send_ref, copy_ref, rows, turned, sem = refs[n:]
    load = pltpu.make_async_copy(w_ref, copy_ref, sem)
    load.start()
    for k in range(n):
        rows[k * CAP : (k + 1) * CAP, :] = x_refs[k][...]
    turned[...] = hid_ref[...].T
    half = parts // 2
    x_size, h_size = rows.shape[1] // parts, turned.shape[0] // parts
    strip = h_size // 6
    for rel in range(parts):
        out_ref, i = (keep_ref, rel) if rel < half else (send_ref, rel - half)
        at = pl.multiple_of(me_ref[rel] * x_size, x_size)
        out_ref[i * x_size : (i + 1) * x_size, :] = rows[:, pl.ds(at, x_size)].T
        for j in range(6):
            at = pl.multiple_of(me_ref[rel] * h_size + j * strip, strip)
            leaves, spot = (i & 1, i >> 1) if j < 3 else (i >> 1, 2 + (i & 1))
            base = half * x_size + ((j % 3) * 2 * half + leaves * half + spot) * strip
            out_ref[base : base + strip, :] = turned[pl.ds(at, strip), :]
    load.wait()


def turn(parts, owners, xs, hidden, w_down):
    n = len(xs)
    width = xs[0].shape[1]
    rows, ff = hidden.shape
    high = (width + ff) // 2
    return pl.pallas_call(
        functools.partial(turn_kernel, n, parts),
        grid=(1,),
        out_shape=[shape_of((high, rows))] * 2 + [shape_of(w_down.shape)],
        in_specs=[in_smem()] + [whole((CAP, width))] * n + [whole(hidden.shape), pl.BlockSpec(memory_space=pltpu.HBM)],
        out_specs=[whole((high, rows))] * 2 + [whole(w_down.shape)],
        scratch_shapes=[pltpu.VMEM((rows, width), BF), pltpu.VMEM((ff, rows), BF), pltpu.SemaphoreType.DMA],
        compiler_params=params(),
        cost_estimate=cost(2 * rows * width, 6 * rows * (width + ff)),
        name="turn",
    )(owners, *xs, hidden, w_down)


def outer_kernel(group, keep_ref, recv_ref, own_ref, other_ref, own_g_ref, x_ref, y_ref, token_ref):
    mark(token_ref)
    step = pl.program_id(0)
    half, high = 4, own_ref.shape[0] // 2
    size = 256
    strip = 16
    for i in range(2):
        block = 2 * i + group
        at = slice(block * size, (block + 1) * size)
        gate = mm(keep_ref[at, :], own_ref[:high, :]) + mm(recv_ref[at, :], other_ref[:high, :])
        x_ref[i, :size, :] = gate.astype(BF)
        block = 2 * group + i
        at = slice(block * size, (block + 1) * size)
        up = mm(keep_ref[at, :], own_ref[high:, :]) + mm(recv_ref[at, :], other_ref[high:, :])
        y_ref[i, :size, :] = up.astype(BF)
    at = pl.ds(pl.multiple_of(half * size + (2 * step + group) * half * strip, strip), half * strip)
    tile = x_ref.shape[2]
    turned = keep_ref.shape[0]
    for c in range(own_g_ref.shape[1] // tile):
        theirs = recv_ref[turned + c * high : turned + (c + 1) * high, :]
        down = mm(keep_ref[at, :], own_g_ref[:, c * tile : (c + 1) * tile]) + mm(recv_ref[at, :], theirs)
        down = down.astype(BF)
        for spot in range(half):
            out_ref = x_ref if spot < 2 else y_ref
            out_ref[spot % 2, size + c * strip : size + (c + 1) * strip, :] = down[spot * strip : (spot + 1) * strip]


def outer(group, keep, recv, own, other, own_g, after):
    rows, width = own_g.shape
    ff = own.shape[1]
    tile = 256
    col = pl.BlockSpec((2 * rows, tile), lambda j: (0, j))
    high = 256 + 16 * (width // tile)
    part = pl.BlockSpec((2, high, tile), lambda j: (0, 0, j))
    return call(
        functools.partial(outer_kernel, group),
        after,
        grid=(ff // tile,),
        out_shape=[shape_of((2, high, ff))] * 2 + [shape_of(TOKEN, F32)],
        in_specs=[whole(keep.shape), whole(recv.shape)] + [col] * 2 + [whole(own_g.shape)],
        args=(keep, recv, own, other, own_g),
        out_specs=[part] * 2 + [whole(TOKEN)],
        compiler_params=params(),
        cost_estimate=cost(3 * rows * width * ff, 4 * keep.size + 8 * high * ff),
        name="outer",
    )


def hidden_grad_kernel(n, *refs):
    g_refs = refs[:n]
    wd_ref, slope_ref, act_ref, turned_ref, grad_ref, rows, pack_ref = refs[n:]

    @pl.when(pl.program_id(0) == 0)
    def _():
        for k in range(n):
            rows[k * CAP : (k + 1) * CAP, :] = g_refs[-k][...]
        high = turned_ref.shape[0]
        pack_ref[:high, :] = turned_ref[...]
        tile = pack_ref.shape[1]
        for c in range(rows.shape[1] // tile):
            at = high + c * n * CAP
            pack_ref[at : at + n * CAP, :] = rows[:, c * tile : (c + 1) * tile]

    grad = mm_cols(rows[...], wd_ref[0])
    grad_ref[: n * CAP, :] = (grad * slope_ref[...]).astype(BF)
    grad_ref[n * CAP :, :] = (grad * act_ref[...]).astype(BF)


def hidden_grad(gs, w_down, slope, act, turned):
    n = len(gs)
    ff, width = w_down.shape[1:]
    rows = n * CAP
    tile = 256
    part = pl.BlockSpec((rows, tile), lambda j: (0, j))
    tall = (turned.shape[0] + rows * (width // 256), 256)
    return pl.pallas_call(
        functools.partial(hidden_grad_kernel, n),
        grid=(ff // tile,),
        out_shape=[shape_of((2 * rows, ff)), shape_of((rows, width)), shape_of(tall)],
        in_specs=[whole((CAP, width))] * n + [weight_specs(width, tile)[2], part, part, whole(turned.shape)],
        out_specs=[pl.BlockSpec((2 * rows, tile), lambda j: (0, j)), whole((rows, width)), whole(tall)],
        compiler_params=params(),
        cost_estimate=cost(2 * rows * width * ff, 2 * width * ff + 4 * rows * width + 12 * rows * ff),
        name="hidden_grad",
    )(gs[0], *gs[:0:-1], w_down, slope, act, turned)


def input_grad_kernel(n, steps, tile, grad_ref, wg_ref, wu_ref, *refs):
    out_refs = refs[:n]
    token_ref, wg_buf, wu_buf, sems = refs[n:]
    mark(token_ref)
    step = pl.program_id(0)

    def loads(j):
        at = pl.ds(pl.multiple_of(j * tile, tile), tile)
        return (
            pltpu.make_async_copy(wg_ref.at[0, at, :], wg_buf.at[j], sems.at[0, j]),
            pltpu.make_async_copy(wu_ref.at[0, at, :], wu_buf.at[j], sems.at[1, j]),
        )

    @pl.when(step == 0)
    def _():
        for j in range(steps):
            for load in loads(j):
                load.start()

    for load in loads(step):
        load.wait()
    rows = n * CAP
    total = mm_cols(grad_ref[:rows, :], wg_buf[step]) + mm_cols(grad_ref[rows:, :], wu_buf[step])
    for k in range(n):
        out_refs[k][...] = total[k * CAP : (k + 1) * CAP, :].astype(BF)


def input_grad(n, grad, w_gate, w_up, after):
    rows, ff = n * CAP, grad.shape[1]
    width = w_gate.shape[1]
    tile = 512
    steps = width // tile
    return call(
        functools.partial(input_grad_kernel, n, steps, tile),
        after,
        grid=(steps,),
        out_shape=[shape_of((CAP, width))] * n + [shape_of(TOKEN, F32)],
        in_specs=[whole((2 * rows, ff))] + [pl.BlockSpec(memory_space=pltpu.HBM)] * 2,
        args=(grad, w_gate, w_up),
        out_specs=[pl.BlockSpec((CAP, tile), lambda j: (0, j))] * n + [whole(TOKEN)],
        scratch_shapes=[pltpu.VMEM((steps, tile, ff), BF)] * 2 + [pltpu.SemaphoreType.DMA((2, steps))],
        compiler_params=params(),
        cost_estimate=cost(4 * rows * width * ff, 4 * width * ff + 2 * rows * (width + 2 * ff)),
        name="input_grad",
    )


def hold_kernel(*_):
    pass


def hold(values, after):
    anywhere = pl.BlockSpec(memory_space=pl.ANY)
    return call(
        hold_kernel,
        after,
        [anywhere] * len(values),
        values,
        out_shape=[shape_of(v.shape) for v in values],
        out_specs=[anywhere] * len(values),
        input_output_aliases={i: i for i in range(len(values))},
        cost_estimate=cost(10 * 10**9, 0),
        name="hold",
    )


def fold_two_kernel(keep, recv, away, mine, token_ref):
    mark(token_ref)
    away[...] = (keep[1].astype(F32) + recv[1].astype(F32)).astype(BF)
    mine[...] = (keep[0].astype(F32) + recv[0].astype(F32)).astype(BF)


def fold_two(keep, recv, after):
    _, high, width = keep.shape
    return call(
        fold_two_kernel,
        after,
        grid=(1,),
        out_shape=[shape_of((high, width))] * 2 + [shape_of(TOKEN, F32)],
        in_specs=[whole((2, high, width))] * 2,
        args=(keep, recv),
        out_specs=[whole((high, width))] * 2 + [whole(TOKEN)],
        compiler_params=params(),
        cost_estimate=cost(2 * high * width, 12 * high * width),
        name="fold_two",
    )


def fold_last_kernel(x_mine, x_recv, y_mine, y_recv, gate_ref, up_ref, down_ref):
    size, strip = gate_ref.shape[1], 16
    tile = 256
    for i, (mine, recv, out_ref) in enumerate(((x_mine, x_recv, gate_ref), (y_mine, y_recv, up_ref))):
        total = (mine[...].astype(F32) + recv[...].astype(F32)).astype(BF)
        out_ref[0] = total[:size]
        for c in range(down_ref.shape[2] // tile):
            for j in range(3):
                down_ref[0, (3 * i + j) * strip : (3 * i + j + 1) * strip, c * tile : (c + 1) * tile] = total[
                    size + c * strip : size + (c + 1) * strip, j * tile : (j + 1) * tile
                ]


def fold_last(x_mine, x_recv, y_mine, y_recv, shapes, after):
    high, width = x_mine.shape
    return call(
        fold_last_kernel,
        after,
        grid=(1,),
        out_shape=[shape_of(s) for s in shapes],
        in_specs=[whole((high, width))] * 4,
        args=(x_mine, x_recv, y_mine, y_recv),
        out_specs=[whole(s) for s in shapes],
        compiler_params=params(),
        cost_estimate=cost(2 * high * width, 12 * high * width),
        name="fold_last",
    )


CORE, ALONG_X, ALONG_Y = 1, 2, 4


def swap(value, bit, count=8):
    return lax.ppermute(value, "dp", [(i, i ^ bit) for i in range(count)])


def combine_out_kernel(n, z_ref, ids_ref, prob_ref, grad_ref, *refs):
    back_refs = refs[:n]
    out_ref, prob_grad_ref, token_ref, rows, sums, firsts, seconds = refs[n:]
    mark(token_ref)
    tok_count = ids_ref.shape[1]
    step = pl.program_id(0)

    @pl.when(step == 0)
    def _():
        ids = ids_ref[...]
        experts = [jnp.bitwise_xor(z_ref[0], k) for k in partners(n)]
        rank = ranks(ids, experts)
        for k in range(n):
            first, second = chosen(ids, experts[k])
            at = places(rank[k : k + 1, :])
            here = slice(k * CAP, (k + 1) * CAP)
            firsts[here, :] = jnp.where(jnp.logical_and(at, first), 1.0, 0.0)
            seconds[here, :] = jnp.where(jnp.logical_and(at, second), 1.0, 0.0)
        sums[...] = jnp.zeros_like(sums)

    for k in range(n):
        rows[k * CAP : (k + 1) * CAP, :] = back_refs[k][...]
    prob = jnp.concatenate([prob_ref[...], jnp.zeros((6, tok_count), F32)], axis=0).T
    grad = grad_ref[...].astype(F32)
    total = 0.0
    part = []
    for choice, at in enumerate((firsts, seconds)):
        out = mm_rows(at[...].astype(BF), rows[...])
        total = total + prob[:, choice : choice + 1] * out
        part.append(jnp.sum(grad * out, axis=1, keepdims=True))
    out_ref[...] = total.astype(BF)
    sums[...] += jnp.concatenate(part + [jnp.zeros((tok_count, 6), F32)], axis=1)

    @pl.when(step == pl.num_programs(0) - 1)
    def _():
        prob_grad_ref[...] = sums[...].T[0:2, :]


def combine_out(z, ids_t, prob_t, out_grad, backs):
    n = len(backs)
    tok_count, width = out_grad.shape
    tile = 512
    by_tile = pl.BlockSpec((tok_count, tile), lambda j: (0, j))
    rows = n * CAP
    return pl.pallas_call(
        functools.partial(combine_out_kernel, n),
        grid=(width // tile,),
        out_shape=[shape_of((tok_count, width)), shape_of((2, tok_count), F32), shape_of(TOKEN, F32)],
        in_specs=[in_smem(), whole(ids_t.shape), whole(prob_t.shape), by_tile]
        + [pl.BlockSpec((CAP, tile), lambda j: (0, j))] * n,
        out_specs=[by_tile, whole((2, tok_count)), whole(TOKEN)],
        scratch_shapes=[pltpu.VMEM((rows, tile), BF), pltpu.VMEM((tok_count, 8), F32)]
        + [pltpu.VMEM((rows, tok_count), F32)] * 2,
        compiler_params=params(),
        cost_estimate=cost(4 * rows * tok_count * width, 2 * width * (rows + 2 * tok_count)),
        name="combine_out",
    )(z, ids_t, prob_t, out_grad, *backs)


def combine_in_kernel(n, z_ref, ids_ref, *refs):
    back_refs = refs[:n]
    out_ref, token_ref, rows, picks = refs[n:]
    mark(token_ref)

    @pl.when(pl.program_id(0) == 0)
    def _():
        ids = ids_ref[...]
        experts = [jnp.bitwise_xor(z_ref[0], k) for k in partners(n)]
        rank = ranks(ids, experts)
        for k in range(n):
            here = jnp.logical_and(places(rank[k : k + 1, :]), jnp.logical_or(*chosen(ids, experts[k])))
            picks[k * CAP : (k + 1) * CAP, :] = jnp.where(here, 1.0, 0.0)

    for k in range(n):
        rows[k * CAP : (k + 1) * CAP, :] = back_refs[k][...]
    out_ref[...] = mm_rows(picks[...].astype(BF), rows[...]).astype(BF)


def combine_in(z, ids_t, backs, hint):
    n = len(backs)
    width = backs[0].shape[1]
    tok_count = ids_t.shape[1]
    tile = 1024
    rows = n * CAP
    return pl.pallas_call(
        functools.partial(combine_in_kernel, n),
        grid=(width // tile,),
        out_shape=[shape_of((tok_count, width)), shape_of(TOKEN, F32)],
        in_specs=[in_smem(), whole(ids_t.shape)] + [pl.BlockSpec((CAP, tile), lambda j: (0, j))] * n,
        out_specs=[pl.BlockSpec((tok_count, tile), lambda j: (0, j)), whole(TOKEN)],
        scratch_shapes=[pltpu.VMEM((rows, tile), BF), pltpu.VMEM((rows, tok_count), F32)],
        compiler_params=params(),
        cost_estimate=cost(hint, 2 * width * (rows + tok_count)),
        name="combine_in",
    )(z, ids_t, *backs)


def exchange(values):
    n = len(values)
    moved = list(values)
    for i, k in enumerate(partners(n)):
        if k:
            moved[i] = lax.ppermute(values[i], "expert", [(d, d ^ k) for d in range(n)])
    return moved


def local(tokens, expert_ids, gate_probs, w_gate, w_up, w_down, out_grad):
    n = lax.axis_size("expert")
    parts = lax.axis_size("dp")
    z = lax.axis_index("expert").astype(jnp.int32).reshape(1)
    ids_t, prob_t = expert_ids.T, gate_probs.T
    xs = exchange(pick_rows(n, False, z, ids_t, prob_t, tokens))
    gs = exchange(pick_rows(n, True, z, ids_t, prob_t, out_grad))
    made = forward(xs, w_gate, w_up, w_down)
    slope, act, hidden = made[:3]
    back_out = exchange(made[3:])
    layer_out, prob_grad_t, shown = combine_out(z, ids_t, prob_t, out_grad, back_out)
    if parts == 8:
        me = lax.axis_index("dp").astype(jnp.int32)
        flips = [(r >> 2 & 1) * CORE | (r & 1) * ALONG_X | (r >> 1 & 1) * ALONG_Y for r in range(8)]
        owners = jnp.stack([me ^ f for f in flips])
        keep_t, send_t, w_near = turn(parts, owners, xs, hidden, w_down)
        grad, g_rows, pack = hidden_grad(gs, w_near, slope, act, send_t)
        other, recv = swap(grad, CORE), swap(pack, CORE)
        x_send, y_send, token = outer(1, keep_t, recv, grad, other, g_rows, [])
        *din, token = input_grad(n, grad, w_gate, w_up, [token])
        x_keep, y_keep, token = outer(0, keep_t, recv, grad, other, g_rows, [token])
        back_in = exchange([din[0], *hold(din[1:], [*back_out[1:], token])])
        x_next, x_mine, token = fold_two(x_keep, swap(x_send, ALONG_X), [shown])
        y_next, y_mine, _ = fold_two(y_keep, swap(y_send, ALONG_Y), [token])
        token_grad, token = combine_in(z, ids_t, back_in, 10 * 10**9)
        shapes = [(1, d // parts, w) for d, w in (w_gate.shape[1:], w_up.shape[1:], w_down.shape[1:])]
        sum_gate, sum_up, sum_down = fold_last(
            x_mine, swap(x_next, ALONG_Y), y_mine, swap(y_next, ALONG_X), shapes, [token]
        )
    else:
        grad, d_rows, _ = hidden_grad(gs, w_down, slope, act, hidden[:16, :256])
        *din, _ = input_grad(n, grad, w_gate, w_up, [])
        back_in = exchange(din)
        token_grad, _ = combine_in(z, ids_t, back_in, 10**8)
        x_rows, count = jnp.concatenate(xs, 0), n * CAP
        sum_gate, sum_up, sum_down = (
            lax.psum_scatter(mm_rows(a, b).astype(BF), "dp", scatter_dimension=0, tiled=True)[None]
            for a, b in ((x_rows, grad[:count]), (x_rows, grad[count:]), (hidden, d_rows))
        )
    return layer_out, prob_grad_t.T, token_grad, sum_gate, sum_up, sum_down


def solution(mesh):
    rows = P(("dp", "expert"), None)
    weights = P("expert", None, None)
    summed = P("expert", "dp", None)
    return jax.shard_map(
        local,
        mesh=mesh,
        in_specs=(rows, rows, rows, weights, weights, weights, rows),
        out_specs=(rows, rows, rows, summed, summed, summed),
        check_vma=False,
    )
```

```python
import functools
import jax
import jax.numpy as jnp
from jax import lax
from jax.experimental import pallas as pl
from jax.experimental.pallas import tpu as pltpu
from jax.sharding import PartitionSpec as P

CAP = 64
BF = jnp.bfloat16
F32 = jnp.float32
MIB = 1 << 20


def mm(left, right):
    return jnp.dot(left, right, preferred_element_type=F32)


def mm_rows(left, right):
    return lax.dot_general(left, right, (((0,), (0,)), ((), ())), preferred_element_type=F32)


def mm_cols(left, right):
    return lax.dot_general(left, right, (((1,), (1,)), ((), ())), preferred_element_type=F32)


def shape_of(shape, dtype=BF):
    return jax.ShapeDtypeStruct(tuple(shape), dtype)


def whole(shape):
    return pl.BlockSpec(tuple(shape), lambda *_: (0,) * len(shape))


def in_smem():
    return pl.BlockSpec(memory_space=pltpu.SMEM)


def params(limit=16):
    return pltpu.CompilerParams(vmem_limit_bytes=limit * MIB)


def call(kernel, after, in_specs, args, **kwargs):
    count = len(args)

    def body(*refs):
        kernel(*refs[:count], *refs[count + len(after) :])

    specs = list(in_specs) + [pl.BlockSpec(memory_space=pl.ANY)] * len(after)
    return pl.pallas_call(body, in_specs=specs, **kwargs)(*args, *after)


TOKEN = (8, 128)


def mark(ref):
    ref[...] = jnp.zeros(TOKEN, F32)


def cost(flops, moved):
    return pl.CostEstimate(flops=int(flops), bytes_accessed=int(moved), transcendentals=0)


def partners(n):
    return [0] + list(range(n - 1, 0, -1))


def chosen(ids, expert):
    first = ids[0:1, :] == expert
    second = ids[1:2, :] == expert
    return first, second


def ranks(ids, experts):
    tok_count = ids.shape[1]
    masks = [jnp.where(jnp.logical_or(*chosen(ids, e)), 1.0, 0.0) for e in experts]
    mask = jnp.concatenate(masks + [jnp.zeros((-len(masks) % 16, tok_count), F32)], axis=0)
    before = lax.broadcasted_iota(jnp.int32, (tok_count, tok_count), 0)
    after = lax.broadcasted_iota(jnp.int32, (tok_count, tok_count), 1)
    upper = jnp.where(before < after, 1.0, 0.0).astype(BF)
    return mm(mask.astype(BF), upper).astype(jnp.int32)


def places(rank_row):
    tok_count = rank_row.shape[1]
    return lax.broadcasted_iota(jnp.int32, (CAP, tok_count), 0) == rank_row


def pick_kernel(n, scaled, z_ref, ids_ref, prob_ref, rows_ref, *outs):
    ids = ids_ref[...]
    prob = prob_ref[...]
    experts = [jnp.bitwise_xor(z_ref[0], k) for k in partners(n)]
    rank = ranks(ids, experts)
    for k in range(n - 1, -1, -1):
        first, second = chosen(ids, experts[k])
        at = places(rank[k : k + 1, :])
        here = jnp.logical_and(at, jnp.logical_or(first, second))
        picked = mm(jnp.where(here, 1.0, 0.0).astype(BF), rows_ref[...])
        if scaled:
            weight = jnp.where(first, prob[0:1, :], prob[1:2, :])
            picked = jnp.sum(jnp.where(here, weight, 0.0), axis=1, keepdims=True) * picked
        outs[k][...] = picked.astype(BF)


def pick_rows(n, scaled, z, ids_t, prob_t, rows):
    tok_count, width = rows.shape
    return pl.pallas_call(
        functools.partial(pick_kernel, n, scaled),
        out_shape=[shape_of((CAP, width))] * n,
        in_specs=[in_smem(), whole(ids_t.shape), whole(prob_t.shape), whole(rows.shape)],
        out_specs=[whole((CAP, width))] * n,
        grid=(1,),
        compiler_params=params(60),
        cost_estimate=cost(2 * n * CAP * tok_count * width, 4 * tok_count * width * 2),
        name="pick_rows",
    )(z, ids_t, prob_t, rows)


def silu_parts(gate):
    sig = jax.nn.sigmoid(gate)
    return gate * sig, sig * (1.0 + gate * (1.0 - sig))


def forward_kernel(n, steps, tile, *refs):
    x_refs = refs[:n]
    weights = refs[n : n + 3]
    slope_ref, act_ref, hid_ref = refs[n + 3 : n + 6]
    out_refs = refs[n + 6 : 2 * n + 6]
    rows, total, wg_buf, wu_buf, wd_buf, sems = refs[2 * n + 6 :]
    step = pl.program_id(0)

    def loads(j):
        at = pl.ds(pl.multiple_of(j * tile, tile), tile)
        wg_ref, wu_ref, wd_ref = weights
        return (
            pltpu.make_async_copy(wg_ref.at[0, :, at], wg_buf.at[j], sems.at[0, j]),
            pltpu.make_async_copy(wu_ref.at[0, :, at], wu_buf.at[j], sems.at[1, j]),
            pltpu.make_async_copy(wd_ref.at[0, at, :], wd_buf.at[j], sems.at[2, j]),
        )

    @pl.when(step == 0)
    def _():
        for j in range(steps):
            for load in loads(j):
                load.start()
        for k in range(n):
            rows[k * CAP : (k + 1) * CAP, :] = x_refs[k][...]

    for load in loads(step):
        load.wait()
    gate = mm(rows[...], wg_buf[step])
    up = mm(rows[...], wu_buf[step])
    act, slope = silu_parts(gate)
    act_ref[...] = act
    slope_ref[...] = up * slope
    hidden = (act * up).astype(BF)
    hid_ref[...] = hidden
    part = mm(hidden, wd_buf[step])

    @pl.when(step == 0)
    def _():
        total[...] = part

    @pl.when(step > 0)
    def _():
        total[...] += part

    @pl.when(step == steps - 1)
    def _():
        for k in range(n):
            out_refs[k][...] = total[k * CAP : (k + 1) * CAP, :].astype(BF)


def weight_specs(width, tile):
    by_col = pl.BlockSpec((1, width, tile), lambda j: (0, 0, j))
    by_row = pl.BlockSpec((1, tile, width), lambda j: (0, j, 0))
    return [by_col, by_col, by_row]


def forward(xs, w_gate, w_up, w_down):
    n = len(xs)
    width, ff = w_gate.shape[1:]
    tile = 256
    steps = ff // tile
    rows = n * CAP
    part = pl.BlockSpec((rows, tile), lambda j: (0, j))
    return pl.pallas_call(
        functools.partial(forward_kernel, n, steps, tile),
        grid=(steps,),
        out_shape=[shape_of((rows, ff), F32)] * 2 + [shape_of((rows, ff))] + [shape_of((CAP, width))] * n,
        in_specs=[whole((CAP, width))] * n + [pl.BlockSpec(memory_space=pltpu.HBM)] * 3,
        out_specs=[part, part, part] + [whole((CAP, width))] * n,
        scratch_shapes=[
            pltpu.VMEM((rows, width), BF),
            pltpu.VMEM((rows, width), F32),
            pltpu.VMEM((steps, width, tile), BF),
            pltpu.VMEM((steps, width, tile), BF),
            pltpu.VMEM((steps, tile, width), BF),
            pltpu.SemaphoreType.DMA((3, steps)),
        ],
        compiler_params=params(50),
        cost_estimate=cost(6 * rows * width * ff, 6 * width * ff + 4 * rows * width + 10 * rows * ff),
        name="forward",
    )(*xs, w_gate, w_up, w_down)


def turn_kernel(n, parts, me_ref, *refs):
    x_refs = refs[:n]
    hid_ref, w_ref, keep_ref, send_ref, copy_ref, rows, turned, sem = refs[n:]
    load = pltpu.make_async_copy(w_ref, copy_ref, sem)
    load.start()
    for k in range(n):
        rows[k * CAP : (k + 1) * CAP, :] = x_refs[k][...]
    turned[...] = hid_ref[...].T
    half = parts // 2
    x_size, h_size = rows.shape[1] // parts, turned.shape[0] // parts
    strip = h_size // 6
    for rel in range(parts):
        out_ref, i = (keep_ref, rel) if rel < half else (send_ref, rel - half)
        at = pl.multiple_of(me_ref[rel] * x_size, x_size)
        out_ref[i * x_size : (i + 1) * x_size, :] = rows[:, pl.ds(at, x_size)].T
        for j in range(6):
            at = pl.multiple_of(me_ref[rel] * h_size + j * strip, strip)
            leaves, spot = (i & 1, i >> 1) if j < 3 else (i >> 1, 2 + (i & 1))
            base = half * x_size + ((j % 3) * 2 * half + leaves * half + spot) * strip
            out_ref[base : base + strip, :] = turned[pl.ds(at, strip), :]
    load.wait()


def turn(parts, owners, xs, hidden, w_down):
    n = len(xs)
    width = xs[0].shape[1]
    rows, ff = hidden.shape
    high = (width + ff) // 2
    return pl.pallas_call(
        functools.partial(turn_kernel, n, parts),
        grid=(1,),
        out_shape=[shape_of((high, rows))] * 2 + [shape_of(w_down.shape)],
        in_specs=[in_smem()] + [whole((CAP, width))] * n + [whole(hidden.shape), pl.BlockSpec(memory_space=pltpu.HBM)],
        out_specs=[whole((high, rows))] * 2 + [whole(w_down.shape)],
        scratch_shapes=[pltpu.VMEM((rows, width), BF), pltpu.VMEM((ff, rows), BF), pltpu.SemaphoreType.DMA],
        compiler_params=params(),
        cost_estimate=cost(2 * rows * width, 6 * rows * (width + ff)),
        name="turn",
    )(owners, *xs, hidden, w_down)


def outer_kernel(group, keep_ref, recv_ref, own_ref, other_ref, own_g_ref, x_ref, y_ref, token_ref):
    mark(token_ref)
    step = pl.program_id(0)
    half, high = 4, own_ref.shape[0] // 2
    size = 256
    strip = 16
    for i in range(2):
        block = 2 * i + group
        at = slice(block * size, (block + 1) * size)
        gate = mm(keep_ref[at, :], own_ref[:high, :]) + mm(recv_ref[at, :], other_ref[:high, :])
        x_ref[i, :size, :] = gate.astype(BF)
        block = 2 * group + i
        at = slice(block * size, (block + 1) * size)
        up = mm(keep_ref[at, :], own_ref[high:, :]) + mm(recv_ref[at, :], other_ref[high:, :])
        y_ref[i, :size, :] = up.astype(BF)
    at = pl.ds(pl.multiple_of(half * size + (2 * step + group) * half * strip, strip), half * strip)
    tile = x_ref.shape[2]
    turned = keep_ref.shape[0]
    for c in range(own_g_ref.shape[1] // tile):
        theirs = recv_ref[turned + c * high : turned + (c + 1) * high, :]
        down = mm(keep_ref[at, :], own_g_ref[:, c * tile : (c + 1) * tile]) + mm(recv_ref[at, :], theirs)
        down = down.astype(BF)
        for spot in range(half):
            out_ref = x_ref if spot < 2 else y_ref
            out_ref[spot % 2, size + c * strip : size + (c + 1) * strip, :] = down[spot * strip : (spot + 1) * strip]


def outer(group, keep, recv, own, other, own_g, after):
    rows, width = own_g.shape
    ff = own.shape[1]
    tile = 256
    col = pl.BlockSpec((2 * rows, tile), lambda j: (0, j))
    high = 256 + 16 * (width // tile)
    part = pl.BlockSpec((2, high, tile), lambda j: (0, 0, j))
    return call(
        functools.partial(outer_kernel, group),
        after,
        grid=(ff // tile,),
        out_shape=[shape_of((2, high, ff))] * 2 + [shape_of(TOKEN, F32)],
        in_specs=[whole(keep.shape), whole(recv.shape)] + [col] * 2 + [whole(own_g.shape)],
        args=(keep, recv, own, other, own_g),
        out_specs=[part] * 2 + [whole(TOKEN)],
        compiler_params=params(),
        cost_estimate=cost(3 * rows * width * ff, 4 * keep.size + 8 * high * ff),
        name="outer",
    )


def hidden_grad_kernel(n, *refs):
    g_refs = refs[:n]
    wd_ref, slope_ref, act_ref, turned_ref, grad_ref, rows, pack_ref = refs[n:]

    @pl.when(pl.program_id(0) == 0)
    def _():
        for k in range(n):
            rows[k * CAP : (k + 1) * CAP, :] = g_refs[-k][...]
        high = turned_ref.shape[0]
        pack_ref[:high, :] = turned_ref[...]
        tile = pack_ref.shape[1]
        for c in range(rows.shape[1] // tile):
            at = high + c * n * CAP
            pack_ref[at : at + n * CAP, :] = rows[:, c * tile : (c + 1) * tile]

    grad = mm_cols(rows[...], wd_ref[0])
    grad_ref[: n * CAP, :] = (grad * slope_ref[...]).astype(BF)
    grad_ref[n * CAP :, :] = (grad * act_ref[...]).astype(BF)


def hidden_grad(gs, w_down, slope, act, turned):
    n = len(gs)
    ff, width = w_down.shape[1:]
    rows = n * CAP
    tile = 256
    part = pl.BlockSpec((rows, tile), lambda j: (0, j))
    tall = (turned.shape[0] + rows * (width // 256), 256)
    return pl.pallas_call(
        functools.partial(hidden_grad_kernel, n),
        grid=(ff // tile,),
        out_shape=[shape_of((2 * rows, ff)), shape_of((rows, width)), shape_of(tall)],
        in_specs=[whole((CAP, width))] * n + [weight_specs(width, tile)[2], part, part, whole(turned.shape)],
        out_specs=[pl.BlockSpec((2 * rows, tile), lambda j: (0, j)), whole((rows, width)), whole(tall)],
        compiler_params=params(),
        cost_estimate=cost(2 * rows * width * ff, 2 * width * ff + 4 * rows * width + 12 * rows * ff),
        name="hidden_grad",
    )(gs[0], *gs[:0:-1], w_down, slope, act, turned)


def input_grad_kernel(n, steps, tile, grad_ref, wg_ref, wu_ref, *refs):
    out_refs = refs[:n]
    token_ref, wg_buf, wu_buf, sems = refs[n:]
    mark(token_ref)
    step = pl.program_id(0)

    def loads(j):
        at = pl.ds(pl.multiple_of(j * tile, tile), tile)
        return (
            pltpu.make_async_copy(wg_ref.at[0, at, :], wg_buf.at[j], sems.at[0, j]),
            pltpu.make_async_copy(wu_ref.at[0, at, :], wu_buf.at[j], sems.at[1, j]),
        )

    @pl.when(step == 0)
    def _():
        for j in range(steps):
            for load in loads(j):
                load.start()

    for load in loads(step):
        load.wait()
    rows = n * CAP
    total = mm_cols(grad_ref[:rows, :], wg_buf[step]) + mm_cols(grad_ref[rows:, :], wu_buf[step])
    for k in range(n):
        out_refs[k][...] = total[k * CAP : (k + 1) * CAP, :].astype(BF)


def input_grad(n, grad, w_gate, w_up, after):
    rows, ff = n * CAP, grad.shape[1]
    width = w_gate.shape[1]
    tile = 512
    steps = width // tile
    return call(
        functools.partial(input_grad_kernel, n, steps, tile),
        after,
        grid=(steps,),
        out_shape=[shape_of((CAP, width))] * n + [shape_of(TOKEN, F32)],
        in_specs=[whole((2 * rows, ff))] + [pl.BlockSpec(memory_space=pltpu.HBM)] * 2,
        args=(grad, w_gate, w_up),
        out_specs=[pl.BlockSpec((CAP, tile), lambda j: (0, j))] * n + [whole(TOKEN)],
        scratch_shapes=[pltpu.VMEM((steps, tile, ff), BF)] * 2 + [pltpu.SemaphoreType.DMA((2, steps))],
        compiler_params=params(),
        cost_estimate=cost(4 * rows * width * ff, 4 * width * ff + 2 * rows * (width + 2 * ff)),
        name="input_grad",
    )


def hold_kernel(*_):
    pass


def hold(values, after):
    anywhere = pl.BlockSpec(memory_space=pl.ANY)
    return call(
        hold_kernel,
        after,
        [anywhere] * len(values),
        values,
        out_shape=[shape_of(v.shape) for v in values],
        out_specs=[anywhere] * len(values),
        input_output_aliases={i: i for i in range(len(values))},
        cost_estimate=cost(10 * 10**9, 0),
        name="hold",
    )


def fold_two_kernel(keep, recv, away, mine, token_ref):
    mark(token_ref)
    away[...] = (keep[1].astype(F32) + recv[1].astype(F32)).astype(BF)
    mine[...] = (keep[0].astype(F32) + recv[0].astype(F32)).astype(BF)


def fold_two(keep, recv, after):
    _, high, width = keep.shape
    return call(
        fold_two_kernel,
        after,
        grid=(1,),
        out_shape=[shape_of((high, width))] * 2 + [shape_of(TOKEN, F32)],
        in_specs=[whole((2, high, width))] * 2,
        args=(keep, recv),
        out_specs=[whole((high, width))] * 2 + [whole(TOKEN)],
        compiler_params=params(),
        cost_estimate=cost(2 * high * width, 12 * high * width),
        name="fold_two",
    )


def fold_last_kernel(x_mine, x_recv, y_mine, y_recv, gate_ref, up_ref, down_ref):
    size, strip = gate_ref.shape[1], 16
    tile = 256
    for i, (mine, recv, out_ref) in enumerate(((x_mine, x_recv, gate_ref), (y_mine, y_recv, up_ref))):
        total = (mine[...].astype(F32) + recv[...].astype(F32)).astype(BF)
        out_ref[0] = total[:size]
        for c in range(down_ref.shape[2] // tile):
            for j in range(3):
                down_ref[0, (3 * i + j) * strip : (3 * i + j + 1) * strip, c * tile : (c + 1) * tile] = total[
                    size + c * strip : size + (c + 1) * strip, j * tile : (j + 1) * tile
                ]


def fold_last(x_mine, x_recv, y_mine, y_recv, shapes, after):
    high, width = x_mine.shape
    return call(
        fold_last_kernel,
        after,
        grid=(1,),
        out_shape=[shape_of(s) for s in shapes],
        in_specs=[whole((high, width))] * 4,
        args=(x_mine, x_recv, y_mine, y_recv),
        out_specs=[whole(s) for s in shapes],
        compiler_params=params(),
        cost_estimate=cost(2 * high * width, 12 * high * width),
        name="fold_last",
    )


CORE, ALONG_X, ALONG_Y = 1, 2, 4


def swap(value, bit, count=8):
    return lax.ppermute(value, "dp", [(i, i ^ bit) for i in range(count)])


def combine_out_kernel(n, z_ref, ids_ref, prob_ref, grad_ref, *refs):
    back_refs = refs[:n]
    out_ref, prob_grad_ref, token_ref, rows, sums, firsts, seconds = refs[n:]
    mark(token_ref)
    tok_count = ids_ref.shape[1]
    step = pl.program_id(0)

    @pl.when(step == 0)
    def _():
        ids = ids_ref[...]
        experts = [jnp.bitwise_xor(z_ref[0], k) for k in partners(n)]
        rank = ranks(ids, experts)
        for k in range(n):
            first, second = chosen(ids, experts[k])
            at = places(rank[k : k + 1, :])
            here = slice(k * CAP, (k + 1) * CAP)
            firsts[here, :] = jnp.where(jnp.logical_and(at, first), 1.0, 0.0)
            seconds[here, :] = jnp.where(jnp.logical_and(at, second), 1.0, 0.0)
        sums[...] = jnp.zeros_like(sums)

    for k in range(n):
        rows[k * CAP : (k + 1) * CAP, :] = back_refs[k][...]
    prob = jnp.concatenate([prob_ref[...], jnp.zeros((6, tok_count), F32)], axis=0).T
    grad = grad_ref[...].astype(F32)
    total = 0.0
    part = []
    for choice, at in enumerate((firsts, seconds)):
        out = mm_rows(at[...].astype(BF), rows[...])
        total = total + prob[:, choice : choice + 1] * out
        part.append(jnp.sum(grad * out, axis=1, keepdims=True))
    out_ref[...] = total.astype(BF)
    sums[...] += jnp.concatenate(part + [jnp.zeros((tok_count, 6), F32)], axis=1)

    @pl.when(step == pl.num_programs(0) - 1)
    def _():
        prob_grad_ref[...] = sums[...].T[0:2, :]


def combine_out(z, ids_t, prob_t, out_grad, backs):
    n = len(backs)
    tok_count, width = out_grad.shape
    tile = 512
    by_tile = pl.BlockSpec((tok_count, tile), lambda j: (0, j))
    rows = n * CAP
    return pl.pallas_call(
        functools.partial(combine_out_kernel, n),
        grid=(width // tile,),
        out_shape=[shape_of((tok_count, width)), shape_of((2, tok_count), F32), shape_of(TOKEN, F32)],
        in_specs=[in_smem(), whole(ids_t.shape), whole(prob_t.shape), by_tile]
        + [pl.BlockSpec((CAP, tile), lambda j: (0, j))] * n,
        out_specs=[by_tile, whole((2, tok_count)), whole(TOKEN)],
        scratch_shapes=[pltpu.VMEM((rows, tile), BF), pltpu.VMEM((tok_count, 8), F32)]
        + [pltpu.VMEM((rows, tok_count), F32)] * 2,
        compiler_params=params(),
        cost_estimate=cost(4 * rows * tok_count * width, 2 * width * (rows + 2 * tok_count)),
        name="combine_out",
    )(z, ids_t, prob_t, out_grad, *backs)


def combine_in_kernel(n, z_ref, ids_ref, *refs):
    back_refs = refs[:n]
    out_ref, token_ref, rows, picks = refs[n:]
    mark(token_ref)

    @pl.when(pl.program_id(0) == 0)
    def _():
        ids = ids_ref[...]
        experts = [jnp.bitwise_xor(z_ref[0], k) for k in partners(n)]
        rank = ranks(ids, experts)
        for k in range(n):
            here = jnp.logical_and(places(rank[k : k + 1, :]), jnp.logical_or(*chosen(ids, experts[k])))
            picks[k * CAP : (k + 1) * CAP, :] = jnp.where(here, 1.0, 0.0)

    for k in range(n):
        rows[k * CAP : (k + 1) * CAP, :] = back_refs[k][...]
    out_ref[...] = mm_rows(picks[...].astype(BF), rows[...]).astype(BF)


def combine_in(z, ids_t, backs, hint):
    n = len(backs)
    width = backs[0].shape[1]
    tok_count = ids_t.shape[1]
    tile = 1024
    rows = n * CAP
    return pl.pallas_call(
        functools.partial(combine_in_kernel, n),
        grid=(width // tile,),
        out_shape=[shape_of((tok_count, width)), shape_of(TOKEN, F32)],
        in_specs=[in_smem(), whole(ids_t.shape)] + [pl.BlockSpec((CAP, tile), lambda j: (0, j))] * n,
        out_specs=[pl.BlockSpec((tok_count, tile), lambda j: (0, j)), whole(TOKEN)],
        scratch_shapes=[pltpu.VMEM((rows, tile), BF), pltpu.VMEM((rows, tok_count), F32)],
        compiler_params=params(),
        cost_estimate=cost(hint, 2 * width * (rows + tok_count)),
        name="combine_in",
    )(z, ids_t, *backs)


def exchange(values):
    n = len(values)
    moved = list(values)
    for i, k in enumerate(partners(n)):
        if k:
            moved[i] = lax.ppermute(values[i], "expert", [(d, d ^ k) for d in range(n)])
    return moved


def local(tokens, expert_ids, gate_probs, w_gate, w_up, w_down, out_grad):
    n = lax.axis_size("expert")
    parts = lax.axis_size("dp")
    z = lax.axis_index("expert").astype(jnp.int32).reshape(1)
    ids_t, prob_t = expert_ids.T, gate_probs.T
    xs = exchange(pick_rows(n, False, z, ids_t, prob_t, tokens))
    gs = exchange(pick_rows(n, True, z, ids_t, prob_t, out_grad))
    made = forward(xs, w_gate, w_up, w_down)
    slope, act, hidden = made[:3]
    back_out = exchange(made[3:])
    layer_out, prob_grad_t, shown = combine_out(z, ids_t, prob_t, out_grad, back_out)
    if parts == 8:
        me = lax.axis_index("dp").astype(jnp.int32)
        flips = [(r >> 2 & 1) * CORE | (r & 1) * ALONG_X | (r >> 1 & 1) * ALONG_Y for r in range(8)]
        owners = jnp.stack([me ^ f for f in flips])
        keep_t, send_t, w_near = turn(parts, owners, xs, hidden, w_down)
        grad, g_rows, pack = hidden_grad(gs, w_near, slope, act, send_t)
        other, recv = swap(grad, CORE), swap(pack, CORE)
        x_send, y_send, token = outer(1, keep_t, recv, grad, other, g_rows, [])
        *din, token = input_grad(n, grad, w_gate, w_up, [token])
        x_keep, y_keep, token = outer(0, keep_t, recv, grad, other, g_rows, [token])
        back_in = exchange([din[0], *hold(din[1:], [*back_out[1:], token])])
        x_next, x_mine, _ = fold_two(x_keep, swap(x_send, ALONG_X), [shown])
        y_next, y_mine, _ = fold_two(y_keep, swap(y_send, ALONG_Y), [shown])
        token_grad, token = combine_in(z, ids_t, back_in, 10 * 10**9)
        shapes = [(1, d // parts, w) for d, w in (w_gate.shape[1:], w_up.shape[1:], w_down.shape[1:])]
        sum_gate, sum_up, sum_down = fold_last(
            x_mine, swap(x_next, ALONG_Y), y_mine, swap(y_next, ALONG_X), shapes, [token]
        )
    else:
        grad, d_rows, _ = hidden_grad(gs, w_down, slope, act, hidden[:16, :256])
        *din, _ = input_grad(n, grad, w_gate, w_up, [])
        back_in = exchange(din)
        token_grad, _ = combine_in(z, ids_t, back_in, 10**8)
        x_rows, count = jnp.concatenate(xs, 0), n * CAP
        sum_gate, sum_up, sum_down = (
            lax.psum_scatter(mm_rows(a, b).astype(BF), "dp", scatter_dimension=0, tiled=True)[None]
            for a, b in ((x_rows, grad[:count]), (x_rows, grad[count:]), (hidden, d_rows))
        )
    return layer_out, prob_grad_t.T, token_grad, sum_gate, sum_up, sum_down


def solution(mesh):
    rows = P(("dp", "expert"), None)
    weights = P("expert", None, None)
    summed = P("expert", "dp", None)
    return jax.shard_map(
        local,
        mesh=mesh,
        in_specs=(rows, rows, rows, weights, weights, weights, rows),
        out_specs=(rows, rows, rows, summed, summed, summed),
        check_vma=False,
    )
```
